32 devices in a mesh: grp: 2 (over x), lon: 16 (over z, y, core).
Axes of the slice: x: 2, y: 2, z: 4, core: 2. Of those that a mesh axis runs over, the one named last changes fastest.
Arguments:
- tracer_pert: float32 [4, 50, 32, 1024], P('grp', None, 'lon'), parts along dimension 0, may hold values from -60 to 60
- surface_pert: float32 [4, 32, 1024], P('grp', 'lon'), parts along dimension 0, may hold values from -60 to 60
- zonal_flow: float32 [50, 32, 1024], P(None, 'lon'), may hold values from -3.2 to 3.2
- merid_flow: float32 [50, 32, 1024], P(None, 'lon'), may hold values from -3.2 to 3.2
- bottom_level: int32 [32, 1024], P('lon'), may hold values from 0 to 50
Outputs:
- tracer_vec: float32 [4, 50, 32, 1024], P('grp', None, 'lon'), parts along dimension 0
- surface_vec: float32 [4, 32, 1024], P('grp', 'lon'), parts along dimension 0
- growth: float32 [6], P('grp'), parts along dimension 0
The draws below stay inside these ranges and needn't reach their ends.
There are 2 independent parts, one for each index of `grp`. The reference program is written for one: setup_inputs(seed, part) draws one part's arguments, and reference() takes and returns one part's arrays. A program takes and returns all parts, laid end to end along the dimension named above; an argument that names none is the same for every part. Nothing has to cross between parts.
Inputs may be any that keep to these rules, and one draw needn't show every extreme that they name: `bottom_level`: 0 marks a land column, 50 a column wet to the bottom level.
All inputs are finite; a program needn't handle non-finite values.
Results may differ from the reference program's by a relative error of at most 0.0001.
Values sent between devices are 32-bit elements; how exact they have to be, the bound alone decides.
No kernel may reach another device: no remote copies, remote signals or barrier semaphores. Data moves between devices by JAX's collectives and lax.ppermute only.
A program may use at most 64 MiB of HBM per device.

```python
import jax
import jax.numpy as jnp
from jax import lax

NV = 2
NZ = 50
NY = 1024
NSUB = 2
ITERS = 3
NX = 32


def shaped_field(key, shape):
    key_base, key_rough, key_rows = jax.random.split(key, 3)
    base = jnp.clip(jax.random.normal(key_base, shape, jnp.float32), -4.0, 4.0)
    mixed = jnp.concatenate([base[:1], 0.6 * base[:1] + 0.8 * base[1:]], axis=0)
    envelope = 0.5 + 1.5 * jnp.arange(NX, dtype=jnp.float32) / NX
    rough = jnp.exp(jax.random.uniform(key_rough, shape, jnp.float32, -0.5, 0.5))
    row_scale = jnp.exp(jax.random.uniform(key_rows, (NY,), jnp.float32, -1.15, 1.15))
    return mixed * envelope[:, None] * rough * row_scale


def draw_tracer_pert(key, part):
    return shaped_field(jax.random.fold_in(key, 11), (NV, NZ, NX, NY))


def draw_surface_pert(key, part):
    return shaped_field(jax.random.fold_in(key, 23), (NV, NX, NY))


def touch_ends(drawn, key, least, largest):
    longest = drawn.shape.index(max(drawn.shape))
    spots = []
    for shift in (0, 1):
        where = [jax.random.randint(jax.random.fold_in(key, axis), (), 0, length) for axis, length in enumerate(drawn.shape)]
        where[longest] = (where[longest] + shift) % drawn.shape[longest]
        spots.append(tuple(where))
    return drawn.at[spots[0]].set(least).at[spots[1]].set(largest)


def level_of(rng, dims, shards, low, high):
    factor_of = 1.0
    for position, shards_of in shards:
        steps = jax.random.uniform(jax.random.fold_in(jax.random.fold_in(rng, 6), position), (shards_of,), jnp.float32, low / len(shards), high / len(shards))
        factor_of = factor_of * jnp.repeat(jnp.exp(steps), dims[position] // shards_of).reshape((-1,) + (1,) * (len(dims) - 1 - position))
    return factor_of


def scatter_about(own_key, shape, deviation, bound, cuts=(), held_as=jnp.bfloat16):
    array = deviation * jax.random.normal(own_key, shape, jnp.float32)
    if cuts:
        array = array * level_of(own_key, shape, cuts, -0.22, 0.18)
    return jnp.clip(array, -bound, bound).astype(held_as)


def setup_inputs(seed: int = 0, part: int = 0) -> dict:
    seeds = jax.random.split(jax.random.key(seed), 6)
    part_splits = jax.random.split(jax.random.fold_in(seeds[5], part), 6)
    return {
        "tracer_pert": draw_tracer_pert(jax.random.fold_in(jax.random.fold_in(seeds[5], part), 71), part),
        "surface_pert": draw_surface_pert(jax.random.fold_in(jax.random.fold_in(seeds[5], part), 71), part),
        "zonal_flow": scatter_about(seeds[2], (NZ, NX, NY), 0.8, 3.2, ((1, 16),), jnp.float32),
        "merid_flow": scatter_about(seeds[3], (NZ, NX, NY), 0.8, 3.2, ((1, 16),), jnp.float32),
        "bottom_level": touch_ends(jax.random.randint(seeds[4], (NX, NY), 0, NZ + 1), jax.random.fold_in(seeds[4], 1), 0, NZ).astype(jnp.int32),
    }


DIFFUSIVITY = 0.5
TIME_STEP = 0.2
SURFACE_COUPLING = 0.5
STERIC_GAIN = 2.0
EPSILON = 1e-06

def tracer_update(tracer, zonal_flow, merid_flow, wet_cells):
    east_vals = jnp.roll(tracer, -1, axis=2)
    face_x = wet_cells * jnp.roll(wet_cells, -1, axis=1)
    flow_x = 0.5 * (zonal_flow + jnp.roll(zonal_flow, -1, axis=1))
    flux_x = face_x * (0.5 * flow_x * (tracer + east_vals) - DIFFUSIVITY * (east_vals - tracer))
    div_x = flux_x - jnp.roll(flux_x, 1, axis=2)
    face_y = wet_cells[..., :-1] * wet_cells[..., 1:]
    flow_y = 0.5 * (merid_flow[..., :-1] + merid_flow[..., 1:])
    flux_y = face_y * (0.5 * flow_y * (tracer[..., :-1] + tracer[..., 1:]) - DIFFUSIVITY * (tracer[..., 1:] - tracer[..., :-1]))
    padded = jnp.pad(flux_y, ((0, 0), (0, 0), (0, 0), (1, 1)))
    div_y = padded[..., 1:] - padded[..., :-1]
    return tracer - TIME_STEP * (div_x + div_y)

def surface_operator(surface, face_x, face_y):
    grad_x = face_x * (jnp.roll(surface, -1, axis=1) - surface)
    lap_x = grad_x - jnp.roll(grad_x, 1, axis=1)
    grad_y = face_y * (surface[..., 1:] - surface[..., :-1])
    padded = jnp.pad(grad_y, ((0, 0), (0, 0), (1, 1)))
    lap_y = padded[..., 1:] - padded[..., :-1]
    return surface - SURFACE_COUPLING * (lap_x + lap_y)

def reference(tracer_pert, surface_pert, zonal_flow, merid_flow, bottom_level):
    levels = jnp.arange(NZ, dtype=jnp.int32)[:, None, None]
    wet_cells = (levels < bottom_level[None]).astype(jnp.float32)
    depths = bottom_level.astype(jnp.float32)
    tracer = wet_cells[None] * tracer_pert
    for substep in range(NSUB):
        tracer = tracer_update(tracer, zonal_flow, merid_flow, wet_cells)
    height = surface_pert * (depths > 0).astype(jnp.float32)[None]
    forcing = height + STERIC_GAIN * lax.optimization_barrier(jnp.sum(tracer, axis=1)) / NZ
    face_x = jnp.minimum(depths, jnp.roll(depths, -1, axis=0))
    face_y = jnp.minimum(depths[:, :-1], depths[:, 1:])
    solution = height
    residual = forcing - surface_operator(height, face_x, face_y)
    direction = residual
    norm_now = lax.optimization_barrier(jnp.sum(residual * residual, axis=(1, 2)))
    for iteration in range(ITERS):
        image_vec = surface_operator(direction, face_x, face_y)
        step_size = norm_now / lax.optimization_barrier(jnp.sum(direction * image_vec, axis=(1, 2)))
        solution = solution + step_size[:, None, None] * direction
        residual = residual - step_size[:, None, None] * image_vec
        if iteration + 1 < ITERS:
            norm_next = lax.optimization_barrier(jnp.sum(residual * residual, axis=(1, 2)))
            direction = residual + (norm_next / norm_now)[:, None, None] * direction
            norm_now = norm_next
    cell_count = (NZ + 1) * NX * NY

    def inner_product(tracer_a, surface_a, tracer_b, surface_b):
        return (jnp.sum(tracer_a * tracer_b) + jnp.sum(surface_a * surface_b)) / cell_count
    first_tracer, second_tracer = (tracer[0], tracer[1])
    first_surface, second_surface = (solution[0], solution[1])
    scale_one = jnp.sqrt(inner_product(first_tracer, first_surface, first_tracer, first_surface) + EPSILON)
    unit_tracer = first_tracer / scale_one
    unit_surface = first_surface / scale_one
    cross = inner_product(second_tracer, second_surface, unit_tracer, unit_surface)
    rest_tracer = second_tracer - cross * unit_tracer
    rest_surface = second_surface - cross * unit_surface
    scale_two = jnp.sqrt(inner_product(rest_tracer, rest_surface, rest_tracer, rest_surface) + EPSILON)
    tracer_vec = jnp.stack([unit_tracer, rest_tracer / scale_two])
    surface_vec = jnp.stack([unit_surface, rest_surface / scale_two])
    growth = jnp.stack([scale_one, cross, scale_two])
    return (tracer_vec, surface_vec, growth)
```

```python
import functools

import jax
import jax.numpy as jnp
from jax import lax
from jax.experimental import pallas as pl
from jax.experimental.pallas import tpu as pltpu
from jax.sharding import PartitionSpec as P

ITERS = 3


DIFFUSIVITY = 0.5
TIME_STEP = 0.2
SURFACE_COUPLING = 0.5
STERIC_GAIN = 2.0
EPSILON = 1e-06

LANES = 128
VECTORS = 2
SLOPE = 0.25 * TIME_STEP
SPREAD = TIME_STEP * DIFFUSIVITY


def next_row(tile):
    turned = pltpu.roll(tile, LANES - 1, 1)
    carried = pltpu.roll(turned, tile.shape[0] - 1, 0)
    lane = lax.broadcasted_iota(jnp.int32, tile.shape, 1)
    return jnp.where(lane == LANES - 1, carried, turned)


def prior_row(tile):
    turned = pltpu.roll(tile, 1, 1)
    carried = pltpu.roll(turned, 1, 0)
    lane = lax.broadcasted_iota(jnp.int32, tile.shape, 1)
    return jnp.where(lane == 0, carried, turned)


def wall_depth(depth):
    subs, lane = (lax.broadcasted_iota(jnp.int32, depth.shape, axis) for axis in (0, 1))
    last = (subs == depth.shape[0] - 1) & (lane == LANES - 1)
    return jnp.where(last, jnp.zeros_like(depth), jnp.minimum(depth, next_row(depth)))


def face_pair(level, face_depth, flow_sum):
    slope = SLOPE * flow_sum
    open_face = level < face_depth
    return (
        jnp.where(open_face, slope + SPREAD, 0.0),
        jnp.where(open_face, slope - SPREAD, 0.0),
    )


def outflow(pair, near, far):
    return pair[0] * near + pair[1] * far


def divergence_y(pair, tile):
    flux = outflow(pair, tile, next_row(tile))
    return flux - prior_row(flux)


def orientation():
    outer = lax.rem(lax.axis_index("lon"), 2)
    return outer, 1 - outer, (2 * outer - 1).astype(jnp.float32)


def first_kernel(levels, sub, tracer, zonal, merid, bottom, cross, mate):
    outer, inner, sign = orientation()

    def column(ref, where, *lead):
        return ref[(*lead, pl.ds(where, sub, stride=2), slice(None))]

    depth = [column(bottom, where).astype(jnp.float32) for where in (outer, inner)]
    between = jnp.minimum(*depth)
    along = [wall_depth(d) for d in depth]
    for buffer, d in zip((cross, mate), depth):
        buffer[(VECTORS * 2 + 1) * levels] = d

    def body(k, carry):
        level = k.astype(jnp.float32)
        flow = [column(zonal, where, k) for where in (outer, inner)]
        turn = [column(merid, where, k) for where in (outer, inner)]
        middle = face_pair(level, between, -sign * (flow[0] + flow[1]))
        sides = [face_pair(level, along[c], turn[c] + next_row(turn[c])) for c in range(2)]
        for v in range(VECTORS):
            cells = [column(tracer, where, v, k) for where in (outer, inner)]
            flux = outflow(middle, *cells)
            for c, buffer in enumerate((cross, mate)):
                kept = jnp.where(level < depth[c], cells[c], 0.0)
                gone = flux if c == 0 else -flux
                buffer[v * levels + k] = cells[c]
                buffer[(VECTORS + 1 + v) * levels + k] = (
                    kept - gone - divergence_y(sides[c], cells[c])
                )
        for c, buffer in enumerate((cross, mate)):
            buffer[VECTORS * levels + k] = flow[c]
        return carry

    lax.fori_loop(0, levels, body, 0, unroll=2)


def second_kernel(levels, sub, cross, mate, cross_far, mate_far, merid, tracer, message):
    outer, inner, sign = orientation()
    depth_row = (VECTORS * 2 + 1) * levels
    near, far = (cross, mate), (cross_far, mate_far)
    depth = [ref[depth_row] for ref in near]
    beside = [jnp.minimum(d, ref[depth_row]) for d, ref in zip(depth, far)]
    between = jnp.minimum(*depth)
    along = [wall_depth(d) for d in depth]
    zero = jnp.zeros_like(between)

    def body(k, carry):
        level = k.astype(jnp.float32)
        flow = [ref[VECTORS * levels + k] for ref in near]
        flow_far = [ref[VECTORS * levels + k] for ref in far]
        turn = [merid[k, pl.ds(where, sub, stride=2), :] for where in (outer, inner)]
        middle = face_pair(level, between, -sign * (flow[0] + flow[1]))
        edges = [
            face_pair(level, beside[c], (sign, -sign)[c] * (flow[c] + flow_far[c]))
            for c in range(2)
        ]
        sides = [face_pair(level, along[c], turn[c] + next_row(turn[c])) for c in range(2)]
        totals, grams = list(carry[:4]), list(carry[4:])
        done = []
        for v in range(VECTORS):
            first, last = v * levels + k, (VECTORS + 1 + v) * levels + k
            own, other = [], []
            for c in range(2):
                flux = outflow(edges[c], near[c][first], far[c][first])
                own.append(near[c][last] - flux)
                other.append(far[c][last] + flux)
            crossing = outflow(middle, *own)
            fresh = []
            for c, where in enumerate((outer, inner)):
                gone = crossing if c == 0 else -crossing
                value = (
                    own[c]
                    - outflow(edges[c], own[c], other[c])
                    - gone
                    - divergence_y(sides[c], own[c])
                )
                tracer[v, k, pl.ds(where, sub, stride=2), :] = value
                totals[v * 2 + c] = totals[v * 2 + c] + value
                fresh.append(value)
            done.append(fresh)
        for c in range(2):
            a, b = done[0][c], done[1][c]
            grams = [grams[0] + a * a, grams[1] + a * b, grams[2] + b * b]
        return (*totals, *grams)

    sums = lax.fori_loop(0, levels, body, (zero,) * 7, unroll=2)
    gain = STERIC_GAIN / levels
    subs = lax.broadcasted_iota(jnp.int32, zero.shape, 0)
    packed = zero
    for i, gram in enumerate(sums[4:]):
        packed = jnp.where(subs == i, jnp.sum(gram, axis=0, keepdims=True), packed)

    def copy(d, carry):
        for v in range(VECTORS):
            for c, where in enumerate((outer, inner)):
                message[d, v * 2 + where] = gain * sums[v * 2 + c]
        message[d, VECTORS * 2] = packed
        return carry

    lax.fori_loop(0, message.shape[0], copy, 0)


def total(tile):
    return jnp.sum(jnp.sum(tile, axis=0, keepdims=True), axis=1, keepdims=True)


def third_kernel(
    levels, sub, gathered, rim, tracer, tracer_out, surface_out, growth, pole, residual, answer, image, face_x, face_y
):
    count = gathered.shape[0]
    width = 2 * count
    me = lax.axis_index("lon")
    zero = jnp.zeros((sub, LANES), jnp.float32)
    group = 2

    def over(body, init, step=1):
        return lax.fori_loop(0, count, body, init, unroll=min(count, 4))

    def depth_of(d, c):
        return rim[d, VECTORS, pl.ds(c, sub, stride=2), :]

    def prepare(d, carry):
        here = [depth_of(d, c) for c in range(group)]
        after = depth_of(lax.rem(d + 1, count), 0)
        spans = [jnp.minimum(here[0], here[1]), jnp.minimum(here[1], after)]
        for c in range(group):
            face_x[2 * d + c + 1] = SURFACE_COUPLING * spans[c]
            face_y[2 * d + c] = SURFACE_COUPLING * wall_depth(here[c])
            for v in range(VECTORS):
                height = jnp.where(here[c] > 0, rim[d, v, pl.ds(c, sub, stride=2), :], 0.0)
                answer[v, 2 * d + c] = height
                pole[v, 2 * d + c + 1] = height
        return carry

    def close(v):
        pole[v, 0] = pole[v, width]
        pole[v, width + 1] = pole[v, 1]

    def spread(d, v):
        x = 2 * d
        cells = [pole[v, x + j] for j in range(group + 2)]
        flux = [face_x[x + j] * (cells[j + 1] - cells[j]) for j in range(group + 1)]
        found = []
        for j in range(group):
            centre = cells[j + 1]
            rise = face_y[x + j] * (next_row(centre) - centre)
            found.append((centre, (flux[j + 1] - flux[j]) + (rise - prior_row(rise))))
        return found

    over(prepare, 0)
    face_x[0] = face_x[width]
    for v in range(VECTORS):
        close(v)

    def start(d, carry):
        sums = list(carry)
        for v in range(VECTORS):
            for c, (_, lap) in enumerate(spread(d, v)):
                value = gathered[d, v * 2 + c] + lap
                residual[v, 2 * d + c] = value
                sums[v] = sums[v] + value * value
        return tuple(sums)

    norm = [total(t) for t in over(start, (zero,) * VECTORS)]

    def restart(d, carry):
        for v in range(VECTORS):
            for c in range(group):
                pole[v, 2 * d + c + 1] = residual[v, 2 * d + c]
        return carry

    over(restart, 0)
    for v in range(VECTORS):
        close(v)

    def apply(d, carry):
        sums = list(carry)
        for v in range(VECTORS):
            for c, (centre, lap) in enumerate(spread(d, v)):
                value = centre - lap
                image[v, 2 * d + c] = value
                sums[v] = sums[v] + centre * value
        return tuple(sums)

    for iteration in range(ITERS):
        energy = [total(t) for t in over(apply, (zero,) * VECTORS)]
        size = [n / e for n, e in zip(norm, energy)]
        if iteration + 1 < ITERS:

            def advance(d, carry, size=size):
                sums = list(carry)
                for v in range(VECTORS):
                    for c in range(group):
                        x = 2 * d + c
                        answer[v, x] = answer[v, x] + size[v] * pole[v, x + 1]
                        value = residual[v, x] - size[v] * image[v, x]
                        residual[v, x] = value
                        sums[v] = sums[v] + value * value
                return tuple(sums)

            fresh = [total(t) for t in over(advance, (zero,) * VECTORS)]
            ratio = [f / n for f, n in zip(fresh, norm)]

            def turn(d, carry, ratio=ratio):
                for v in range(VECTORS):
                    for c in range(group):
                        x = 2 * d + c
                        pole[v, x + 1] = residual[v, x] + ratio[v] * pole[v, x + 1]
                return carry

            over(turn, 0)
            for v in range(VECTORS):
                close(v)
            norm = fresh

    def finish(d, carry):
        grams = list(carry)
        for c in range(group):
            x = 2 * d + c
            a, b = (answer[v, x] + size[v] * pole[v, x + 1] for v in range(VECTORS))
            answer[0, x], answer[1, x] = a, b
            grams = [grams[0] + a * a, grams[1] + a * b, grams[2] + b * b]
        return (*grams, carry[3] + gathered[d, VECTORS * 2])

    *grams, packed = over(finish, (zero,) * 4)
    cells = (levels + 1) * width * sub * LANES
    one, mix, two = (
        (total(g) + jnp.sum(packed[i : i + 1], axis=1, keepdims=True)) / cells
        for i, g in enumerate(grams)
    )
    scale_one = jnp.sqrt(one + EPSILON)
    cross = mix / scale_one
    rest = two - 2.0 * cross * cross + cross * cross * one / (one + EPSILON)
    scale_two = jnp.sqrt(rest + EPSILON)
    over_one, over_two = 1.0 / scale_one, 1.0 / scale_two
    for i, value in enumerate((scale_one, cross, scale_two)):
        growth[i] = value[0, 0]

    for c in range(group):
        x = 2 * me + c
        unit = answer[0, x] * over_one
        surface_out[0, pl.ds(c, sub, stride=2), :] = unit
        surface_out[1, pl.ds(c, sub, stride=2), :] = (answer[1, x] - cross * unit) * over_two

    def scale(k, carry):
        unit = tracer[0, k] * over_one
        tracer_out[0, k] = unit
        tracer_out[1, k] = (tracer[1, k] - cross * unit) * over_two
        return carry

    lax.fori_loop(0, levels, scale, 0, unroll=5)


def tiled(array):
    *lead, columns, rows = array.shape
    split = array.reshape(*lead, columns, rows // LANES, LANES)
    return jnp.swapaxes(split, -3, -2).reshape(*lead, rows // LANES * columns, LANES)


def untiled(array, columns):
    *lead, high, lanes = array.shape
    split = array.reshape(*lead, high // columns, columns, lanes)
    return jnp.swapaxes(split, -3, -2).reshape(*lead, columns, high // columns * lanes)


def on_device(tracer_pert, surface_pert, zonal_flow, merid_flow, bottom_level):
    vectors, levels, columns, rows = tracer_pert.shape
    count = lax.axis_size("lon")
    sub = rows // LANES
    assert vectors == VECTORS and columns == 2 and count % 2 == 0 and rows % LANES == 0
    f32 = jnp.float32
    vmem = pl.BlockSpec(memory_space=pltpu.VMEM)
    params = pltpu.CompilerParams(vmem_limit_bytes=24 * 2**20)

    rim = lax.all_gather(
        jnp.concatenate([surface_pert, bottom_level[None].astype(f32)]), "lon"
    )
    merid = tiled(merid_flow)
    planes = (VECTORS * 2 + 1) * levels + 1
    edge = jax.ShapeDtypeStruct((planes, sub, LANES), f32)
    cross, mate = pl.pallas_call(
        functools.partial(first_kernel, levels, sub),
        out_shape=(edge, edge),
        in_specs=[vmem] * 4,
        out_specs=(vmem, vmem),
        compiler_params=params,
        name="partial_step",
    )(tiled(tracer_pert), tiled(zonal_flow), merid, tiled(bottom_level))
    cross_far = lax.ppermute(
        cross, "lon", [(i, (i + 1) % count if i % 2 else (i - 1) % count) for i in range(count)]
    )
    mate_far = lax.ppermute(mate, "lon", [(i, i + 1 - 2 * (i % 2)) for i in range(count)])
    blocks = VECTORS * 2 + 1
    tracer, message = pl.pallas_call(
        functools.partial(second_kernel, levels, sub),
        out_shape=(
            jax.ShapeDtypeStruct((vectors, levels, sub * 2, LANES), f32),
            jax.ShapeDtypeStruct((count, blocks, sub, LANES), f32),
        ),
        in_specs=[vmem] * 5,
        out_specs=(vmem, vmem),
        compiler_params=params,
        name="both_steps",
    )(cross, mate, cross_far, mate_far, merid)
    gathered = lax.all_to_all(message, "lon", 0, 0)
    width = 2 * count
    field = lambda extra: pltpu.VMEM((vectors, width + extra, sub, LANES), f32)
    tracer_vec, surface_vec, growth = pl.pallas_call(
        functools.partial(third_kernel, levels, sub),
        out_shape=(
            jax.ShapeDtypeStruct((vectors, levels, sub * 2, LANES), f32),
            jax.ShapeDtypeStruct((vectors, sub * 2, LANES), f32),
            jax.ShapeDtypeStruct((3,), f32),
        ),
        in_specs=[vmem] * 3,
        out_specs=(vmem, vmem, pl.BlockSpec(memory_space=pltpu.SMEM)),
        scratch_shapes=[
            field(2),
            field(0),
            field(0),
            field(0),
            pltpu.VMEM((width + 1, sub, LANES), f32),
            pltpu.VMEM((width, sub, LANES), f32),
        ],
        compiler_params=pltpu.CompilerParams(vmem_limit_bytes=32 * 2**20),
        name="surface_and_scale",
    )(gathered, tiled(rim), tracer)
    return (untiled(tracer_vec, 2), untiled(surface_vec, 2), growth)


def solution(mesh):
    placed = (
        P("grp", None, "lon", None),
        P("grp", "lon", None),
        P(None, "lon", None),
        P(None, "lon", None),
        P("lon", None),
    )
    return jax.shard_map(
        on_device,
        mesh=mesh,
        in_specs=placed,
        out_specs=(P("grp", None, "lon", None), P("grp", "lon", None), P("grp")),
        check_vma=False,
    )
```

```python
import functools

import jax
import jax.numpy as jnp
from jax import lax
from jax.experimental import pallas as pl
from jax.experimental.pallas import tpu as pltpu
from jax.sharding import PartitionSpec as P

ITERS = 3


DIFFUSIVITY = 0.5
TIME_STEP = 0.2
SURFACE_COUPLING = 0.5
STERIC_GAIN = 2.0
EPSILON = 1e-06

LANES = 128
VECTORS = 2
SLOPE = 0.25 * TIME_STEP
SPREAD = TIME_STEP * DIFFUSIVITY
HEIGHTS = VECTORS * 2
DEPTHS = HEIGHTS + VECTORS * 2
GRAMS = DEPTHS + 2
BLOCKS = GRAMS + 1


def next_row(tile):
    turned = pltpu.roll(tile, LANES - 1, 1)
    carried = pltpu.roll(turned, tile.shape[0] - 1, 0)
    lane = lax.broadcasted_iota(jnp.int32, tile.shape, 1)
    return jnp.where(lane == LANES - 1, carried, turned)


def prior_row(tile):
    turned = pltpu.roll(tile, 1, 1)
    carried = pltpu.roll(turned, 1, 0)
    lane = lax.broadcasted_iota(jnp.int32, tile.shape, 1)
    return jnp.where(lane == 0, carried, turned)


def wall_depth(depth):
    subs, lane = (lax.broadcasted_iota(jnp.int32, depth.shape, axis) for axis in (0, 1))
    last = (subs == depth.shape[0] - 1) & (lane == LANES - 1)
    return jnp.where(last, jnp.zeros_like(depth), jnp.minimum(depth, next_row(depth)))


def face_pair(level, face_depth, flow_sum):
    slope = SLOPE * flow_sum
    open_face = level < face_depth
    return (
        jnp.where(open_face, slope + SPREAD, 0.0),
        jnp.where(open_face, slope - SPREAD, 0.0),
    )


def outflow(pair, near, far):
    return pair[0] * near + pair[1] * far


def side_pairs(level, depths, flow):
    return (
        face_pair(level, depths[0], flow + next_row(flow)),
        face_pair(level, depths[1], -(flow + prior_row(flow))),
    )


def divergence_y(pairs, tile):
    return outflow(pairs[0], tile, next_row(tile)) + outflow(pairs[1], tile, prior_row(tile))


def side_depths(depth):
    north = wall_depth(depth)
    return north, prior_row(north)


def orientation():
    outer = lax.rem(lax.axis_index("lon"), 2)
    return outer, 1 - outer, (2 * outer - 1).astype(jnp.float32)


def first_kernel(levels, sub, tracer, zonal, merid, bottom, cross, mate):
    outer, inner, sign = orientation()

    def column(ref, where, *lead):
        return ref[(*lead, pl.ds(where, sub, stride=2), slice(None))]

    depth = [column(bottom, where).astype(jnp.float32) for where in (outer, inner)]
    between = jnp.minimum(*depth)
    along = [side_depths(d) for d in depth]
    for buffer, d in zip((cross, mate), depth):
        buffer[(VECTORS * 2 + 1) * levels] = d

    def body(k, carry):
        level = k.astype(jnp.float32)
        flow = [column(zonal, where, k) for where in (outer, inner)]
        turn = [column(merid, where, k) for where in (outer, inner)]
        middle = face_pair(level, between, -sign * (flow[0] + flow[1]))
        sides = [side_pairs(level, along[c], turn[c]) for c in range(2)]
        for v in range(VECTORS):
            cells = [column(tracer, where, v, k) for where in (outer, inner)]
            flux = outflow(middle, *cells)
            for c, buffer in enumerate((cross, mate)):
                kept = jnp.where(level < depth[c], cells[c], 0.0)
                gone = flux if c == 0 else -flux
                buffer[v * levels + k] = cells[c]
                buffer[(VECTORS + 1 + v) * levels + k] = (
                    kept - gone - divergence_y(sides[c], cells[c])
                )
        for c, buffer in enumerate((cross, mate)):
            buffer[VECTORS * levels + k] = flow[c]
        return carry

    lax.fori_loop(0, levels, body, 0, unroll=10)


def second_kernel(
    levels, sub, cross, mate, cross_far, mate_far, merid, surface, bottom, tracer, message
):
    outer, inner, sign = orientation()
    depth_row = (VECTORS * 2 + 1) * levels
    near, far = (cross, mate), (cross_far, mate_far)
    depth = [ref[depth_row] for ref in near]
    beside = [jnp.minimum(d, ref[depth_row]) for d, ref in zip(depth, far)]
    between = jnp.minimum(*depth)
    along = [side_depths(d) for d in depth]
    zero = jnp.zeros_like(between)

    def body(k, carry):
        level = k.astype(jnp.float32)
        flow = [ref[VECTORS * levels + k] for ref in near]
        flow_far = [ref[VECTORS * levels + k] for ref in far]
        turn = [merid[k, pl.ds(where, sub, stride=2), :] for where in (outer, inner)]
        middle = face_pair(level, between, -sign * (flow[0] + flow[1]))
        edges = [
            face_pair(level, beside[c], (sign, -sign)[c] * (flow[c] + flow_far[c]))
            for c in range(2)
        ]
        sides = [side_pairs(level, along[c], turn[c]) for c in range(2)]
        totals, grams = list(carry[:4]), list(carry[4:])
        done = []
        for v in range(VECTORS):
            first, last = v * levels + k, (VECTORS + 1 + v) * levels + k
            own, other = [], []
            for c in range(2):
                flux = outflow(edges[c], near[c][first], far[c][first])
                own.append(near[c][last] - flux)
                other.append(far[c][last] + flux)
            crossing = outflow(middle, *own)
            fresh = []
            for c, where in enumerate((outer, inner)):
                gone = crossing if c == 0 else -crossing
                value = (
                    own[c]
                    - outflow(edges[c], own[c], other[c])
                    - gone
                    - divergence_y(sides[c], own[c])
                )
                tracer[v, k, pl.ds(where, sub, stride=2), :] = value
                totals[v * 2 + c] = totals[v * 2 + c] + value
                fresh.append(value)
            done.append(fresh)
        for c in range(2):
            a, b = done[0][c], done[1][c]
            grams = [grams[0] + a * a, grams[1] + a * b, grams[2] + b * b]
        return (*totals, *grams)

    sums = lax.fori_loop(0, levels, body, (zero,) * 7, unroll=10)
    gain = STERIC_GAIN / levels
    subs = lax.broadcasted_iota(jnp.int32, zero.shape, 0)
    packed = zero
    for i, gram in enumerate(sums[4:]):
        packed = jnp.where(subs == i, jnp.sum(gram, axis=0, keepdims=True), packed)

    def copy(d, carry):
        for v in range(VECTORS):
            for c, where in enumerate((outer, inner)):
                message[d, v * 2 + where] = gain * sums[v * 2 + c]
            for c in range(2):
                message[d, HEIGHTS + v * 2 + c] = surface[v, pl.ds(c, sub, stride=2), :]
        for c in range(2):
            message[d, DEPTHS + c] = bottom[pl.ds(c, sub, stride=2), :].astype(jnp.float32)
        message[d, GRAMS] = packed
        return carry

    lax.fori_loop(0, message.shape[0], copy, 0)


def total(tile):
    return jnp.sum(jnp.sum(tile, axis=0, keepdims=True), axis=1, keepdims=True)


def third_kernel(
    levels, sub, gathered, tracer, tracer_out, surface_out, growth, pole, residual, answer, image, face_x, face_y
):
    count = gathered.shape[0]
    width = 2 * count
    me = lax.axis_index("lon")
    zero = jnp.zeros((sub, LANES), jnp.float32)
    group = 2

    def over(body, init, step=1):
        return lax.fori_loop(0, count, body, init, unroll=min(count, 4))

    def depth_of(d, c):
        return gathered[d, DEPTHS + c]

    def prepare(d, carry):
        here = [depth_of(d, c) for c in range(group)]
        after = depth_of(lax.rem(d + 1, count), 0)
        spans = [jnp.minimum(here[0], here[1]), jnp.minimum(here[1], after)]
        for c in range(group):
            face_x[2 * d + c + 1] = SURFACE_COUPLING * spans[c]
            face_y[2 * d + c] = SURFACE_COUPLING * wall_depth(here[c])
            for v in range(VECTORS):
                height = jnp.where(here[c] > 0, gathered[d, HEIGHTS + v * 2 + c], 0.0)
                answer[v, 2 * d + c] = height
                pole[v, 2 * d + c + 1] = height
        return carry

    def close(v):
        pole[v, 0] = pole[v, width]
        pole[v, width + 1] = pole[v, 1]

    def spread(d, v):
        x = 2 * d
        cells = [pole[v, x + j] for j in range(group + 2)]
        flux = [face_x[x + j] * (cells[j + 1] - cells[j]) for j in range(group + 1)]
        found = []
        for j in range(group):
            centre = cells[j + 1]
            rise = face_y[x + j] * (next_row(centre) - centre)
            found.append((centre, (flux[j + 1] - flux[j]) + (rise - prior_row(rise))))
        return found

    over(prepare, 0)
    face_x[0] = face_x[width]
    for v in range(VECTORS):
        close(v)

    def start(d, carry):
        sums = list(carry)
        for v in range(VECTORS):
            for c, (_, lap) in enumerate(spread(d, v)):
                value = gathered[d, v * 2 + c] + lap
                residual[v, 2 * d + c] = value
                sums[v] = sums[v] + value * value
        return tuple(sums)

    norm = [total(t) for t in over(start, (zero,) * VECTORS)]

    def restart(d, carry):
        for v in range(VECTORS):
            for c in range(group):
                pole[v, 2 * d + c + 1] = residual[v, 2 * d + c]
        return carry

    over(restart, 0)
    for v in range(VECTORS):
        close(v)

    def apply(d, carry):
        sums = list(carry)
        for v in range(VECTORS):
            for c, (centre, lap) in enumerate(spread(d, v)):
                value = centre - lap
                image[v, 2 * d + c] = value
                sums[v] = sums[v] + centre * value
        return tuple(sums)

    for iteration in range(ITERS):
        energy = [total(t) for t in over(apply, (zero,) * VECTORS)]
        size = [n / e for n, e in zip(norm, energy)]
        if iteration + 1 < ITERS:

            def advance(d, carry, size=size):
                sums = list(carry)
                for v in range(VECTORS):
                    for c in range(group):
                        x = 2 * d + c
                        answer[v, x] = answer[v, x] + size[v] * pole[v, x + 1]
                        value = residual[v, x] - size[v] * image[v, x]
                        residual[v, x] = value
                        sums[v] = sums[v] + value * value
                return tuple(sums)

            fresh = [total(t) for t in over(advance, (zero,) * VECTORS)]
            ratio = [f / n for f, n in zip(fresh, norm)]

            def turn(d, carry, ratio=ratio):
                for v in range(VECTORS):
                    for c in range(group):
                        x = 2 * d + c
                        pole[v, x + 1] = residual[v, x] + ratio[v] * pole[v, x + 1]
                return carry

            over(turn, 0)
            for v in range(VECTORS):
                close(v)
            norm = fresh

    def finish(d, carry):
        grams = list(carry)
        for c in range(group):
            x = 2 * d + c
            a, b = (answer[v, x] + size[v] * pole[v, x + 1] for v in range(VECTORS))
            answer[0, x], answer[1, x] = a, b
            grams = [grams[0] + a * a, grams[1] + a * b, grams[2] + b * b]
        return (*grams, carry[3] + gathered[d, GRAMS])

    *grams, packed = over(finish, (zero,) * 4)
    cells = (levels + 1) * width * sub * LANES
    one, mix, two = (
        (total(g) + jnp.sum(packed[i : i + 1], axis=1, keepdims=True)) / cells
        for i, g in enumerate(grams)
    )
    scale_one = jnp.sqrt(one + EPSILON)
    cross = mix / scale_one
    rest = two - 2.0 * cross * cross + cross * cross * one / (one + EPSILON)
    scale_two = jnp.sqrt(rest + EPSILON)
    over_one, over_two = 1.0 / scale_one, 1.0 / scale_two
    for i, value in enumerate((scale_one, cross, scale_two)):
        growth[i] = value[0, 0]

    for c in range(group):
        x = 2 * me + c
        unit = answer[0, x] * over_one
        surface_out[0, pl.ds(c, sub, stride=2), :] = unit
        surface_out[1, pl.ds(c, sub, stride=2), :] = (answer[1, x] - cross * unit) * over_two

    def scale(k, carry):
        unit = tracer[0, k] * over_one
        tracer_out[0, k] = unit
        tracer_out[1, k] = (tracer[1, k] - cross * unit) * over_two
        return carry

    lax.fori_loop(0, levels, scale, 0, unroll=5)


def tiled(array):
    *lead, columns, rows = array.shape
    split = array.reshape(*lead, columns, rows // LANES, LANES)
    return jnp.swapaxes(split, -3, -2).reshape(*lead, rows // LANES * columns, LANES)


def untiled(array, columns):
    *lead, high, lanes = array.shape
    split = array.reshape(*lead, high // columns, columns, lanes)
    return jnp.swapaxes(split, -3, -2).reshape(*lead, columns, high // columns * lanes)


def on_device(tracer_pert, surface_pert, zonal_flow, merid_flow, bottom_level):
    vectors, levels, columns, rows = tracer_pert.shape
    count = lax.axis_size("lon")
    sub = rows // LANES
    assert vectors == VECTORS and columns == 2 and count % 2 == 0 and rows % LANES == 0
    f32 = jnp.float32
    vmem = pl.BlockSpec(memory_space=pltpu.VMEM)
    params = pltpu.CompilerParams(vmem_limit_bytes=24 * 2**20)

    merid = tiled(merid_flow)
    planes = (VECTORS * 2 + 1) * levels + 1
    edge = jax.ShapeDtypeStruct((planes, sub, LANES), f32)
    cross, mate = pl.pallas_call(
        functools.partial(first_kernel, levels, sub),
        out_shape=(edge, edge),
        in_specs=[vmem] * 4,
        out_specs=(vmem, vmem),
        compiler_params=params,
        name="partial_step",
    )(tiled(tracer_pert), tiled(zonal_flow), merid, tiled(bottom_level))
    cross_far = lax.ppermute(
        cross, "lon", [(i, (i + 1) % count if i % 2 else (i - 1) % count) for i in range(count)]
    )
    mate_far = lax.ppermute(mate, "lon", [(i, i + 1 - 2 * (i % 2)) for i in range(count)])
    tracer, message = pl.pallas_call(
        functools.partial(second_kernel, levels, sub),
        out_shape=(
            jax.ShapeDtypeStruct((vectors, levels, sub * 2, LANES), f32),
            jax.ShapeDtypeStruct((count, BLOCKS, sub, LANES), f32),
        ),
        in_specs=[vmem] * 7,
        out_specs=(vmem, vmem),
        compiler_params=params,
        name="both_steps",
    )(cross, mate, cross_far, mate_far, merid, tiled(surface_pert), tiled(bottom_level))
    gathered = lax.all_to_all(message, "lon", 0, 0)
    width = 2 * count
    field = lambda extra: pltpu.VMEM((vectors, width + extra, sub, LANES), f32)
    tracer_vec, surface_vec, growth = pl.pallas_call(
        functools.partial(third_kernel, levels, sub),
        out_shape=(
            jax.ShapeDtypeStruct((vectors, levels, sub * 2, LANES), f32),
            jax.ShapeDtypeStruct((vectors, sub * 2, LANES), f32),
            jax.ShapeDtypeStruct((3,), f32),
        ),
        in_specs=[vmem] * 2,
        out_specs=(vmem, vmem, pl.BlockSpec(memory_space=pltpu.SMEM)),
        scratch_shapes=[
            field(2),
            field(0),
            field(0),
            field(0),
            pltpu.VMEM((width + 1, sub, LANES), f32),
            pltpu.VMEM((width, sub, LANES), f32),
        ],
        compiler_params=pltpu.CompilerParams(vmem_limit_bytes=32 * 2**20),
        name="surface_and_scale",
    )(gathered, tracer)
    return (untiled(tracer_vec, 2), untiled(surface_vec, 2), growth)


def solution(mesh):
    placed = (
        P("grp", None, "lon", None),
        P("grp", "lon", None),
        P(None, "lon", None),
        P(None, "lon", None),
        P("lon", None),
    )
    return jax.shard_map(
        on_device,
        mesh=mesh,
        in_specs=placed,
        out_specs=(P("grp", None, "lon", None), P("grp", "lon", None), P("grp")),
        check_vma=False,
    )
```

```python
import functools

import jax
import jax.numpy as jnp
from jax import lax
from jax.experimental import pallas as pl
from jax.experimental.pallas import tpu as pltpu
from jax.sharding import PartitionSpec as P

ITERS = 3


DIFFUSIVITY = 0.5
TIME_STEP = 0.2
SURFACE_COUPLING = 0.5
STERIC_GAIN = 2.0
EPSILON = 1e-06

LANES = 128
VECTORS = 2
SLOPE = 0.25 * TIME_STEP
SPREAD = TIME_STEP * DIFFUSIVITY
GRAMS = VECTORS * 2
BLOCKS = GRAMS + 1
DEPTHS = VECTORS * 2
RIM = DEPTHS + 2


def next_row(tile):
    turned = pltpu.roll(tile, LANES - 1, 1)
    carried = pltpu.roll(turned, tile.shape[0] - 1, 0)
    lane = lax.broadcasted_iota(jnp.int32, tile.shape, 1)
    return jnp.where(lane == LANES - 1, carried, turned)


def prior_row(tile):
    turned = pltpu.roll(tile, 1, 1)
    carried = pltpu.roll(turned, 1, 0)
    lane = lax.broadcasted_iota(jnp.int32, tile.shape, 1)
    return jnp.where(lane == 0, carried, turned)


def wall_depth(depth):
    subs, lane = (lax.broadcasted_iota(jnp.int32, depth.shape, axis) for axis in (0, 1))
    last = (subs == depth.shape[0] - 1) & (lane == LANES - 1)
    return jnp.where(last, jnp.zeros_like(depth), jnp.minimum(depth, next_row(depth)))


def face_pair(level, face_depth, flow_sum):
    slope = SLOPE * flow_sum
    open_face = level < face_depth
    return (
        jnp.where(open_face, slope + SPREAD, 0.0),
        jnp.where(open_face, slope - SPREAD, 0.0),
    )


def outflow(pair, near, far):
    return pair[0] * near + pair[1] * far


def side_pairs(level, depths, flow):
    return (
        face_pair(level, depths[0], flow + next_row(flow)),
        face_pair(level, depths[1], -(flow + prior_row(flow))),
    )


def divergence_y(pairs, tile):
    return outflow(pairs[0], tile, next_row(tile)) + outflow(pairs[1], tile, prior_row(tile))


def side_depths(depth):
    north = wall_depth(depth)
    return north, prior_row(north)


def orientation():
    outer = lax.rem(lax.axis_index("lon"), 2)
    return outer, 1 - outer, (2 * outer - 1).astype(jnp.float32)


def steps(count, most):
    return max(u for u in range(1, most + 1) if count % u == 0)


def share(levels):
    size = lax.axis_size("grp")
    assert size == 2
    part = (levels + 1) // 2
    return lax.axis_index("grp") * (levels - part), part


def first_kernel(
    levels, sub, tracer_hbm, zonal_hbm, merid_hbm, surface_hbm, bottom_hbm,
    cross_hbm, flow_hbm, mate_hbm, rim_hbm,
    tracer, zonal, merid, surface, bottom, cross, flow_part, mate, rim, sems_in, sems_out,
):
    outer, inner, sign = orientation()
    part_start, part = share(levels)
    chunk = steps(levels, 10)
    parts = levels // chunk

    def moves(pairs, sems):
        copies = [
            pltpu.make_async_copy(source, target, sems.at[i])
            for i, (source, target) in enumerate(pairs)
        ]
        for copy in copies:
            copy.start()
        return copies

    def rows(n):
        return pl.ds(n * chunk, chunk)

    small = moves([(bottom_hbm, bottom), (surface_hbm, surface)], sems_in.at[parts])
    arrivals = [
        moves(
            [
                (tracer_hbm.at[:, rows(n)], tracer.at[:, rows(n)]),
                (zonal_hbm.at[rows(n)], zonal.at[rows(n)]),
                (merid_hbm.at[rows(n)], merid.at[rows(n)]),
            ],
            sems_in.at[n],
        )
        for n in range(parts)
    ]

    def column(ref, where, *lead):
        return ref[(*lead, pl.ds(where, sub, stride=2), slice(None))]

    for copy in small:
        copy.wait()
    for c in range(2):
        for v in range(VECTORS):
            rim[v * 2 + c] = column(surface, c, v)
        rim[DEPTHS + c] = column(bottom, c).astype(jnp.float32)
    depth = [column(bottom, where).astype(jnp.float32) for where in (outer, inner)]
    between = jnp.minimum(*depth)
    along = [side_depths(d) for d in depth]
    departures = moves([(rim, rim_hbm)], sems_out.at[parts])

    def body(k, carry):
        level = k.astype(jnp.float32)
        flow = [column(zonal, where, k) for where in (outer, inner)]
        turn = [column(merid, where, k) for where in (outer, inner)]
        middle = face_pair(level, between, -sign * (flow[0] + flow[1]))
        sides = [side_pairs(level, along[c], turn[c]) for c in range(2)]
        for v in range(VECTORS):
            cells = [column(tracer, where, v, k) for where in (outer, inner)]
            flux = outflow(middle, *cells)
            kept = [
                jnp.where(level < depth[c], cells[c], 0.0) - divergence_y(sides[c], cells[c])
                for c in range(2)
            ]
            cross[v, k] = cells[0]
            cross[VECTORS + v, k] = kept[0] - flux
            mate[v, k] = cells[1]
            mate[VECTORS + v, k] = kept[1] + flux
        mate[VECTORS * 2, k] = flow[1]
        return carry

    for n in range(parts):
        for copy in arrivals[n]:
            copy.wait()
        lax.fori_loop(n * chunk, (n + 1) * chunk, body, 0, unroll=chunk)
        departures += moves(
            [
                (cross.at[:, rows(n)], cross_hbm.at[:, rows(n)]),
                (mate.at[:, rows(n)], mate_hbm.at[:, rows(n)]),
            ],
            sems_out.at[n],
        )

    def pack(i, carry):
        flow_part[i] = column(zonal, outer, part_start + i)
        return carry

    lax.fori_loop(0, part, pack, 0, unroll=steps(part, 10))
    departures += moves([(flow_part, flow_hbm)], sems_out.at[parts + 1])
    for copy in departures:
        copy.wait()


def surface_kernel(
    count, quad, far, far_mate, depth, face_x, face_y, face_z, height, lap, pole
):
    me = lax.axis_index("lon")
    core = lax.rem(me, 2)
    width = 2 * count

    def place(owner, block):
        for c in range(2):
            depth[2 * owner + c] = block(DEPTHS + c)
            for v in range(VECTORS):
                wet = block(DEPTHS + c) > 0
                height[v, 2 * owner + c] = jnp.where(wet, block(v * 2 + c), 0.0)

    for slot in range(quad.shape[0]):
        place(me ^ slot, lambda row, slot=slot: quad[slot, row])
    groups = count // quad.shape[0]
    for ref, flip in ((far, 0), (far_mate, 1)):
        for j in range(far.shape[0]):
            mask = 2 * j + 1 + (core ^ flip)
            for slot in range(quad.shape[0]):

                @pl.when(mask < groups)
                def _(ref=ref, flip=flip, j=j, mask=mask, slot=slot):
                    owner = me ^ flip ^ (mask * quad.shape[0]) ^ slot
                    place(owner, lambda row: ref[j, slot, row])

    def prepare(x, carry):
        here, after = depth[x], depth[lax.rem(x + 1, width)]
        face_x[x + 1] = SURFACE_COUPLING * jnp.minimum(here, after)
        north, south = side_depths(here)
        face_y[x] = SURFACE_COUPLING * north
        face_z[x] = SURFACE_COUPLING * south
        for v in range(VECTORS):
            pole[v, x + 1] = height[v, x]
        return carry

    lax.fori_loop(0, width, prepare, 0, unroll=steps(width, 8))
    face_x[0] = face_x[width]
    wrap(pole, width)

    def bend(x, carry):
        for v in range(VECTORS):
            lap[v, x] = spread(pole, face_x, face_y, face_z, v, x)
        return carry

    lax.fori_loop(0, width, bend, 0, unroll=steps(width, 8))


def wrap(pole, width):
    for v in range(VECTORS):
        pole[v, 0] = pole[v, width]
        pole[v, width + 1] = pole[v, 1]


def spread(pole, face_x, face_y, face_z, v, x):
    west, centre, east = (pole[v, x + j] for j in range(3))
    return (face_x[x + 1] * (east - centre) - face_x[x] * (centre - west)) + (
        face_y[x] * (next_row(centre) - centre) - face_z[x] * (centre - prior_row(centre))
    )


def second_kernel(
    levels, sub, cross, mate, cross_far, mate_far, flow_half, flow_other, zonal, merid, depths,
    tracer, message, flow_far,
):
    outer, inner, sign = orientation()
    part_start, part = share(levels)
    me, width = lax.axis_index("lon"), depths.shape[0]

    def unpack(i, carry):
        flow_far[part_start + i] = flow_half[i]
        flow_far[levels - part - part_start + i] = flow_other[i]
        return carry

    lax.fori_loop(0, part, unpack, 0, unroll=steps(part, 10))
    depth = [depths[2 * me + where] for where in (outer, inner)]
    beside = [
        jnp.minimum(depth[0], depths[lax.rem(2 * me + 3 * outer - 1 + width, width)]),
        jnp.minimum(depth[1], depths[2 * me + 3 * inner - 1]),
    ]
    between = jnp.minimum(*depth)
    along = [side_depths(d) for d in depth]
    zero = jnp.zeros_like(between)
    near, far = (cross, mate), (cross_far, mate_far)

    def body(k, carry):
        level = k.astype(jnp.float32)
        flow = [zonal[k, pl.ds(outer, sub, stride=2), :], mate[VECTORS * 2, k]]
        beyond = [flow_far[k], mate_far[VECTORS * 2, k]]
        turn = [merid[k, pl.ds(where, sub, stride=2), :] for where in (outer, inner)]
        middle = face_pair(level, between, -sign * (flow[0] + flow[1]))
        edges = [
            face_pair(level, beside[c], (sign, -sign)[c] * (flow[c] + beyond[c])) for c in range(2)
        ]
        sides = [side_pairs(level, along[c], turn[c]) for c in range(2)]
        totals, grams = list(carry[:4]), list(carry[4:])
        done = []
        for v in range(VECTORS):
            own, other = [], []
            for c in range(2):
                flux = outflow(edges[c], near[c][v, k], far[c][v, k])
                own.append(near[c][VECTORS + v, k] - flux)
                other.append(far[c][VECTORS + v, k] + flux)
            crossing = outflow(middle, *own)
            fresh = []
            for c, where in enumerate((outer, inner)):
                gone = crossing if c == 0 else -crossing
                value = (
                    own[c]
                    - outflow(edges[c], own[c], other[c])
                    - gone
                    - divergence_y(sides[c], own[c])
                )
                tracer[v, k, pl.ds(where, sub, stride=2), :] = value
                totals[v * 2 + c] = totals[v * 2 + c] + value
                fresh.append(value)
            done.append(fresh)
        for c in range(2):
            a, b = done[0][c], done[1][c]
            grams = [grams[0] + a * a, grams[1] + a * b, grams[2] + b * b]
        return (*totals, *grams)

    sums = lax.fori_loop(0, levels, body, (zero,) * 7, unroll=steps(levels, 10))
    gain = STERIC_GAIN / levels
    subs = lax.broadcasted_iota(jnp.int32, zero.shape, 0)
    packed = zero
    for i, gram in enumerate(sums[4:]):
        packed = jnp.where(subs == i, jnp.sum(gram, axis=0, keepdims=True), packed)

    def copy(d, carry):
        for v in range(VECTORS):
            for c, where in enumerate((outer, inner)):
                message[d, v * 2 + where] = gain * sums[v * 2 + c]
        message[d, GRAMS] = packed
        return carry

    count = message.shape[0]
    lax.fori_loop(0, count, copy, 0, unroll=steps(count, 16))


def total(tile):
    return jnp.sum(jnp.sum(tile, axis=0, keepdims=True), axis=1, keepdims=True)


def third_kernel(
    levels, sub, gathered, face_x, face_y, face_z, height, lap, tracer,
    tracer_out, surface_out, growth, pole, residual, answer, image,
):
    count = gathered.shape[0]
    width = 2 * count
    me = lax.axis_index("lon")
    zero = jnp.zeros((sub, LANES), jnp.float32)
    none = (zero,) * VECTORS

    def over(body, init):
        return lax.fori_loop(0, count, body, init, unroll=steps(count, 16))

    def each(d):
        return [(v, c, 2 * d + c) for v in range(VECTORS) for c in range(2)]

    def start(d, carry):
        sums = list(carry)
        for v, c, x in each(d):
            value = gathered[d, v * 2 + c] + lap[v, x]
            residual[v, x] = value
            pole[v, x + 1] = value
            sums[v] = sums[v] + value * value
        return tuple(sums)

    norm = [total(t) for t in over(start, none)]
    wrap(pole, width)

    def apply(d, carry):
        sums = list(carry)
        for v, _, x in each(d):
            centre = pole[v, x + 1]
            value = centre - spread(pole, face_x, face_y, face_z, v, x)
            image[v, x] = value
            sums[v] = sums[v] + centre * value
        return tuple(sums)

    for iteration in range(ITERS):
        energy = [total(t) for t in over(apply, none)]
        size = [n / e for n, e in zip(norm, energy)]
        held = height if iteration == 0 else answer
        if iteration + 1 < ITERS:

            def advance(d, carry, size=size, held=held):
                sums = list(carry)
                for v, _, x in each(d):
                    answer[v, x] = held[v, x] + size[v] * pole[v, x + 1]
                    value = residual[v, x] - size[v] * image[v, x]
                    residual[v, x] = value
                    sums[v] = sums[v] + value * value
                return tuple(sums)

            fresh = [total(t) for t in over(advance, none)]
            ratio = [f / n for f, n in zip(fresh, norm)]

            def turn(d, carry, ratio=ratio):
                for v, _, x in each(d):
                    pole[v, x + 1] = residual[v, x] + ratio[v] * pole[v, x + 1]
                return carry

            over(turn, 0)
            wrap(pole, width)
            norm = fresh

    def finish(d, carry):
        grams = list(carry)
        for x in (2 * d, 2 * d + 1):
            a, b = (held[v, x] + size[v] * pole[v, x + 1] for v in range(VECTORS))
            answer[0, x], answer[1, x] = a, b
            grams = [grams[0] + a * a, grams[1] + a * b, grams[2] + b * b]
        return (*grams, carry[3] + gathered[d, GRAMS])

    *grams, packed = over(finish, (zero,) * 4)
    cells = (levels + 1) * width * sub * LANES
    one, mix, two = (
        (total(g) + jnp.sum(packed[i : i + 1], axis=1, keepdims=True)) / cells
        for i, g in enumerate(grams)
    )
    scale_one = jnp.sqrt(one + EPSILON)
    cross = mix / scale_one
    rest = two - 2.0 * cross * cross + cross * cross * one / (one + EPSILON)
    scale_two = jnp.sqrt(rest + EPSILON)
    over_one, over_two = 1.0 / scale_one, 1.0 / scale_two

    def scale(k, carry):
        unit = tracer[0, k] * over_one
        tracer_out[0, k] = unit
        tracer_out[1, k] = (tracer[1, k] - cross * unit) * over_two
        return carry

    lax.fori_loop(0, levels, scale, 0, unroll=steps(levels, 10))
    for c in range(2):
        x = 2 * me + c
        unit = answer[0, x] * over_one
        surface_out[0, pl.ds(c, sub, stride=2), :] = unit
        surface_out[1, pl.ds(c, sub, stride=2), :] = (answer[1, x] - cross * unit) * over_two
    for i, value in enumerate((scale_one, cross, scale_two)):
        growth[i] = value[0, 0]


def tiled(array):
    *lead, columns, rows = array.shape
    split = array.reshape(*lead, columns, rows // LANES, LANES)
    return jnp.swapaxes(split, -3, -2).reshape(*lead, rows // LANES * columns, LANES)


def untiled(array, columns):
    *lead, high, lanes = array.shape
    split = array.reshape(*lead, high // columns, columns, lanes)
    return jnp.swapaxes(split, -3, -2).reshape(*lead, columns, high // columns * lanes)


def swap(array, mask):
    count = lax.axis_size("lon")
    return lax.ppermute(array, "lon", [(i, i ^ mask) for i in range(count)])


def early_gather(rim):
    count = lax.axis_size("lon")
    pair = jnp.stack([rim, swap(rim, 1)])
    quad = jnp.concatenate([pair, swap(pair, 2)])
    size = quad.shape[0]
    groups = count // size
    far = []
    for j in range(groups // 2):
        masks = (2 * j + 1, 2 * j + 2)
        moves = [
            (i, i ^ (masks[i % 2] * size)) for i in range(count) if masks[i % 2] < groups
        ]
        far.append(lax.ppermute(quad, "lon", moves))
    far = jnp.stack(far)
    return quad, far, swap(far, 1)


def on_device(tracer_pert, surface_pert, zonal_flow, merid_flow, bottom_level):
    vectors, levels, columns, rows = tracer_pert.shape
    count = lax.axis_size("lon")
    sub = rows // LANES
    assert vectors == VECTORS and columns == 2 and rows % LANES == 0
    assert count >= 8 and count & (count - 1) == 0
    width = 2 * count
    f32 = jnp.float32
    vmem = pl.BlockSpec(memory_space=pltpu.VMEM)
    hbm = pl.BlockSpec(memory_space=pltpu.HBM)
    params = pltpu.CompilerParams(vmem_limit_bytes=24 * 2**20)

    def shaped(*shape):
        return jax.ShapeDtypeStruct((*shape, sub, LANES), f32)

    def held(*shape):
        return pltpu.VMEM((*shape, sub, LANES), f32)

    both = pltpu.VMEM((vectors, levels, sub * 2, LANES), f32)
    single = pltpu.VMEM((levels, sub * 2, LANES), f32)
    tracer_pert, zonal_flow, merid_flow = map(tiled, (tracer_pert, zonal_flow, merid_flow))
    outward = [(i, (i + 1) % count if i % 2 else (i - 1) % count) for i in range(count)]
    part = (levels + 1) // 2
    chunks = levels // steps(levels, 10)

    packed = (
        (vectors * 2, levels),
        (part,),
        (vectors * 2 + 1, levels),
        (RIM,),
    )
    cross, flow_half, mate, rim = pl.pallas_call(
        functools.partial(first_kernel, levels, sub),
        out_shape=tuple(shaped(*shape) for shape in packed),
        in_specs=[hbm] * 5,
        out_specs=(hbm,) * 4,
        scratch_shapes=[
            both,
            single,
            single,
            pltpu.VMEM((vectors, sub * 2, LANES), f32),
            pltpu.VMEM((sub * 2, LANES), jnp.int32),
            *(held(*shape) for shape in packed),
            pltpu.SemaphoreType.DMA((chunks + 1, 3)),
            pltpu.SemaphoreType.DMA((chunks + 2, 2)),
        ],
        compiler_params=pltpu.CompilerParams(vmem_limit_bytes=60 * 2**20),
        name="partial_step",
    )(tracer_pert, zonal_flow, merid_flow, tiled(surface_pert), tiled(bottom_level))
    flow_half = lax.ppermute(flow_half, "lon", outward)
    flow_other = lax.ppermute(flow_half, "grp", [(0, 1), (1, 0)])
    cross_far = lax.ppermute(cross, "lon", outward)
    mate_far = swap(mate, 1)
    fields = pl.pallas_call(
        functools.partial(surface_kernel, count),
        out_shape=(
            shaped(width),
            shaped(width + 1),
            shaped(width),
            shaped(width),
            shaped(vectors, width),
            shaped(vectors, width),
        ),
        in_specs=[vmem] * 3,
        out_specs=(vmem,) * 6,
        scratch_shapes=[held(vectors, width + 2)],
        compiler_params=params,
        name="surface_faces",
    )(*early_gather(rim))
    tracer, message = pl.pallas_call(
        functools.partial(second_kernel, levels, sub),
        out_shape=(
            jax.ShapeDtypeStruct((vectors, levels, sub * 2, LANES), f32),
            shaped(count, BLOCKS),
        ),
        in_specs=[vmem] * 9,
        out_specs=(vmem, vmem),
        scratch_shapes=[held(levels)],
        compiler_params=params,
        name="both_steps",
    )(cross, mate, cross_far, mate_far, flow_half, flow_other, zonal_flow, merid_flow, fields[0])
    gathered = lax.all_to_all(message, "lon", 0, 0)
    tracer_vec, surface_vec, growth = pl.pallas_call(
        functools.partial(third_kernel, levels, sub),
        out_shape=(
            jax.ShapeDtypeStruct((vectors, levels, sub * 2, LANES), f32),
            jax.ShapeDtypeStruct((vectors, sub * 2, LANES), f32),
            jax.ShapeDtypeStruct((3,), f32),
        ),
        in_specs=[vmem] * 7,
        out_specs=(vmem, vmem, pl.BlockSpec(memory_space=pltpu.SMEM)),
        scratch_shapes=[held(vectors, width + 2)] + [held(vectors, width)] * 3,
        compiler_params=pltpu.CompilerParams(vmem_limit_bytes=40 * 2**20),
        name="surface_and_scale",
    )(gathered, *fields[1:], tracer)
    return (untiled(tracer_vec, 2), untiled(surface_vec, 2), growth)


def solution(mesh):
    placed = (
        P("grp", None, "lon", None),
        P("grp", "lon", None),
        P(None, "lon", None),
        P(None, "lon", None),
        P("lon", None),
    )
    return jax.shard_map(
        on_device,
        mesh=mesh,
        in_specs=placed,
        out_specs=(P("grp", None, "lon", None), P("grp", "lon", None), P("grp")),
        check_vma=False,
    )
```

```python
import functools

import jax
import jax.numpy as jnp
from jax import lax
from jax.experimental import pallas as pl
from jax.experimental.pallas import tpu as pltpu
from jax.sharding import PartitionSpec as P

ITERS = 3


DIFFUSIVITY = 0.5
TIME_STEP = 0.2
SURFACE_COUPLING = 0.5
STERIC_GAIN = 2.0
EPSILON = 1e-06

LANES = 128
VECTORS = 2
SLOPE = 0.25 * TIME_STEP
SPREAD = TIME_STEP * DIFFUSIVITY
HEIGHTS = VECTORS * 2
DEPTHS = HEIGHTS + VECTORS * 2
GRAMS = DEPTHS + 2
BLOCKS = GRAMS + 1


def next_row(tile):
    turned = pltpu.roll(tile, LANES - 1, 1)
    carried = pltpu.roll(turned, tile.shape[0] - 1, 0)
    lane = lax.broadcasted_iota(jnp.int32, tile.shape, 1)
    return jnp.where(lane == LANES - 1, carried, turned)


def prior_row(tile):
    turned = pltpu.roll(tile, 1, 1)
    carried = pltpu.roll(turned, 1, 0)
    lane = lax.broadcasted_iota(jnp.int32, tile.shape, 1)
    return jnp.where(lane == 0, carried, turned)


def wall_depth(depth):
    subs, lane = (lax.broadcasted_iota(jnp.int32, depth.shape, axis) for axis in (0, 1))
    last = (subs == depth.shape[0] - 1) & (lane == LANES - 1)
    return jnp.where(last, jnp.zeros_like(depth), jnp.minimum(depth, next_row(depth)))


def face_pair(level, face_depth, flow_sum):
    slope = SLOPE * flow_sum
    open_face = level < face_depth
    return (
        jnp.where(open_face, slope + SPREAD, 0.0),
        jnp.where(open_face, slope - SPREAD, 0.0),
    )


def outflow(pair, near, far):
    return pair[0] * near + pair[1] * far


def side_pairs(level, depths, flow):
    return (
        face_pair(level, depths[0], flow + next_row(flow)),
        face_pair(level, depths[1], -(flow + prior_row(flow))),
    )


def divergence_y(pairs, tile):
    return outflow(pairs[0], tile, next_row(tile)) + outflow(pairs[1], tile, prior_row(tile))


def side_depths(depth):
    north = wall_depth(depth)
    return north, prior_row(north)


def orientation():
    outer = lax.rem(lax.axis_index("lon"), 2)
    return outer, 1 - outer, (2 * outer - 1).astype(jnp.float32)


def steps(count, most):
    return max(u for u in range(1, most + 1) if count % u == 0)


def share(levels):
    size = lax.axis_size("grp")
    assert size == 2
    part = (levels + 1) // 2
    return lax.axis_index("grp") * (levels - part), part


def edge_kernel(
    levels, sub, tracer_hbm, zonal_hbm, edge_hbm, tracer, zonal, edge, sems_in, sems_out
):
    outer, _, _ = orientation()
    start, part = share(levels)

    def move(source, target, sem):
        copy = pltpu.make_async_copy(source, target, sem)
        copy.start()
        return copy

    arrivals = [
        move(tracer_hbm.at[v], tracer.at[v], sems_in.at[v]) for v in range(VECTORS)
    ] + [move(zonal_hbm.at[pl.ds(start, part)], zonal, sems_in.at[VECTORS])]
    departures = []
    for v, arrival in enumerate(arrivals):
        number = part if v == VECTORS else levels
        arrival.wait()

        def body(k, carry, v=v):
            source = zonal if v == VECTORS else tracer.at[v]
            edge[v * levels + k] = source[k, pl.ds(outer, sub, stride=2), :]
            return carry

        lax.fori_loop(0, number, body, 0, unroll=steps(number, 10))
        rows = pl.ds(v * levels, number)
        departures.append(move(edge.at[rows], edge_hbm.at[rows], sems_out.at[v]))
    for departure in departures:
        departure.wait()


def first_kernel(
    levels, sub, edge, tracer, zonal, merid, bottom, cross, mate, raw, mate_raw, flow_in, mate_flow
):
    del edge
    outer, inner, sign = orientation()

    def column(ref, where, *lead):
        return ref[(*lead, pl.ds(where, sub, stride=2), slice(None))]

    depth = [column(bottom, where).astype(jnp.float32) for where in (outer, inner)]
    between = jnp.minimum(*depth)
    along = [side_depths(d) for d in depth]
    cross[VECTORS * levels] = depth[0]
    mate[VECTORS * levels] = depth[1]

    def body(k, carry):
        level = k.astype(jnp.float32)
        flow = [column(zonal, where, k) for where in (outer, inner)]
        turn = [column(merid, where, k) for where in (outer, inner)]
        middle = face_pair(level, between, -sign * (flow[0] + flow[1]))
        sides = [side_pairs(level, along[c], turn[c]) for c in range(2)]
        for v in range(VECTORS):
            cells = [column(tracer, where, v, k) for where in (outer, inner)]
            flux = outflow(middle, *cells)
            kept = [
                jnp.where(level < depth[c], cells[c], 0.0) - divergence_y(sides[c], cells[c])
                for c in range(2)
            ]
            cross[v * levels + k] = kept[0] - flux
            raw[v * levels + k] = cells[0]
            mate[v * levels + k] = kept[1] + flux
            mate_raw[v * levels + k] = cells[1]
        flow_in[k] = flow[0]
        mate_flow[k] = flow[1]
        return carry

    lax.fori_loop(0, levels, body, 0, unroll=steps(levels, 10))


def wrap(pole, width):
    for v in range(VECTORS):
        pole[v, 0] = pole[v, width]
        pole[v, width + 1] = pole[v, 1]


def spread(pole, face_x, face_y, face_z, v, x):
    west, centre, east = (pole[v, x + j] for j in range(3))
    return (face_x[x + 1] * (east - centre) - face_x[x] * (centre - west)) + (
        face_y[x] * (next_row(centre) - centre) - face_z[x] * (centre - prior_row(centre))
    )


def second_kernel(
    levels, sub, raw, cross, mate, mate_raw, flow_in, mate_flow,
    raw_far, cross_far, mate_far, mate_raw_far, mate_flow_far, flow_other,
    merid, surface, bottom, tracer, message, flow_far,
):
    outer, inner, sign = orientation()
    start, part = share(levels)
    last = VECTORS * levels

    def unpack(i, carry):
        flow_far[start + i] = raw_far[VECTORS * levels + i]
        flow_far[levels - part - start + i] = flow_other[i]
        return carry

    lax.fori_loop(0, part, unpack, 0, unroll=steps(part, 10))
    near = [(raw, cross), (mate_raw, mate)]
    far = [(raw_far, cross_far), (mate_raw_far, mate_far)]
    depth = [cross[last], mate[last]]
    beside = [jnp.minimum(depth[0], cross_far[last]), jnp.minimum(depth[1], mate_far[last])]
    between = jnp.minimum(*depth)
    along = [side_depths(d) for d in depth]
    zero = jnp.zeros_like(between)

    def body(k, carry):
        level = k.astype(jnp.float32)
        flow = [flow_in[k], mate_flow[k]]
        beyond = [flow_far[k], mate_flow_far[k]]
        turn = [merid[k, pl.ds(where, sub, stride=2), :] for where in (outer, inner)]
        middle = face_pair(level, between, -sign * (flow[0] + flow[1]))
        edges = [
            face_pair(level, beside[c], (sign, -sign)[c] * (flow[c] + beyond[c])) for c in range(2)
        ]
        sides = [side_pairs(level, along[c], turn[c]) for c in range(2)]
        totals, grams = list(carry[:4]), list(carry[4:])
        done = []
        for v in range(VECTORS):
            own, other = [], []
            for c in range(2):
                (first, kept), (first_far, kept_far) = near[c], far[c]
                row = v * levels + k
                flux = outflow(edges[c], first[row], first_far[row])
                own.append(kept[row] - flux)
                other.append(kept_far[row] + flux)
            crossing = outflow(middle, *own)
            fresh = []
            for c, where in enumerate((outer, inner)):
                gone = crossing if c == 0 else -crossing
                value = (
                    own[c]
                    - outflow(edges[c], own[c], other[c])
                    - gone
                    - divergence_y(sides[c], own[c])
                )
                tracer[v, k, pl.ds(where, sub, stride=2), :] = value
                totals[v * 2 + c] = totals[v * 2 + c] + value
                fresh.append(value)
            done.append(fresh)
        for c in range(2):
            a, b = done[0][c], done[1][c]
            grams = [grams[0] + a * a, grams[1] + a * b, grams[2] + b * b]
        return (*totals, *grams)

    sums = lax.fori_loop(0, levels, body, (zero,) * 7, unroll=steps(levels, 10))
    gain = STERIC_GAIN / levels
    subs = lax.broadcasted_iota(jnp.int32, zero.shape, 0)
    packed = zero
    for i, gram in enumerate(sums[4:]):
        packed = jnp.where(subs == i, jnp.sum(gram, axis=0, keepdims=True), packed)
    message[GRAMS] = packed
    for v in range(VECTORS):
        for c, where in enumerate((outer, inner)):
            message[v * 2 + where] = gain * sums[v * 2 + c]
            message[HEIGHTS + v * 2 + c] = surface[v, pl.ds(c, sub, stride=2), :]
    for c in range(2):
        message[DEPTHS + c] = bottom[pl.ds(c, sub, stride=2), :].astype(jnp.float32)


def total(tile):
    return jnp.sum(jnp.sum(tile, axis=0, keepdims=True), axis=1, keepdims=True)


def third_kernel(
    levels, sub, count, pair, fetched, fetched_mate, tracer, tracer_out, surface_out, growth,
    pole, residual, answer, image, height, depth, face_x, face_y, face_z, packed,
):
    width = 2 * count
    me = lax.axis_index("lon")
    core = lax.rem(me, 2)
    zero = jnp.zeros((sub, LANES), jnp.float32)
    none = (zero,) * VECTORS

    def place(owner, block):
        packed[owner] = block(GRAMS)
        for c in range(2):
            x = 2 * owner + c
            floor = block(DEPTHS + c)
            depth[x] = floor
            for v in range(VECTORS):
                tall = jnp.where(floor > 0, block(HEIGHTS + v * 2 + c), 0.0)
                height[v, x] = tall
                pole[v, x + 1] = tall
                residual[v, x] = block(v * 2 + c)

    for slot in range(2):
        place(me ^ slot, lambda row, slot=slot: pair[slot, row])
    for ref, flip in ((fetched, 0), (fetched_mate, 1)):
        for j, masks in enumerate(chip_masks(count)):
            mask = jnp.where((core ^ flip) == 0, *masks)
            for slot in range(2):
                owner = me ^ flip ^ slot ^ (2 * mask)

                def put(owner=owner, ref=ref, j=j, slot=slot):
                    place(owner, lambda row: ref[j, slot, row])

                if all(masks):
                    put()
                else:
                    pl.when(mask > 0)(put)

    def over(body, init):
        return lax.fori_loop(0, count, body, init, unroll=steps(count, 16))

    def each(d):
        return [(v, c, 2 * d + c) for v in range(VECTORS) for c in range(2)]

    def prepare(d, carry):
        for x in (2 * d, 2 * d + 1):
            here, after = depth[x], depth[lax.rem(x + 1, width)]
            face_x[x + 1] = SURFACE_COUPLING * jnp.minimum(here, after)
            north, south = side_depths(here)
            face_y[x] = SURFACE_COUPLING * north
            face_z[x] = SURFACE_COUPLING * south
        return carry

    over(prepare, 0)
    face_x[0] = face_x[width]
    wrap(pole, width)

    def start(d, carry):
        sums = list(carry)
        for v, _, x in each(d):
            value = residual[v, x] + spread(pole, face_x, face_y, face_z, v, x)
            residual[v, x] = value
            sums[v] = sums[v] + value * value
        return tuple(sums)

    norm = [total(t) for t in over(start, none)]

    def aim(d, carry):
        for v, _, x in each(d):
            pole[v, x + 1] = residual[v, x]
        return carry

    over(aim, 0)
    wrap(pole, width)

    def apply(d, carry):
        sums = list(carry)
        for v, _, x in each(d):
            centre = pole[v, x + 1]
            value = centre - spread(pole, face_x, face_y, face_z, v, x)
            image[v, x] = value
            sums[v] = sums[v] + centre * value
        return tuple(sums)

    for iteration in range(ITERS):
        energy = [total(t) for t in over(apply, none)]
        size = [n / e for n, e in zip(norm, energy)]
        held = height if iteration == 0 else answer
        if iteration + 1 < ITERS:

            def advance(d, carry, size=size, held=held):
                sums = list(carry)
                for v, _, x in each(d):
                    answer[v, x] = held[v, x] + size[v] * pole[v, x + 1]
                    value = residual[v, x] - size[v] * image[v, x]
                    residual[v, x] = value
                    sums[v] = sums[v] + value * value
                return tuple(sums)

            fresh = [total(t) for t in over(advance, none)]
            ratio = [f / n for f, n in zip(fresh, norm)]

            def turn(d, carry, ratio=ratio):
                for v, _, x in each(d):
                    pole[v, x + 1] = residual[v, x] + ratio[v] * pole[v, x + 1]
                return carry

            over(turn, 0)
            wrap(pole, width)
            norm = fresh

    def finish(d, carry):
        grams = list(carry)
        for x in (2 * d, 2 * d + 1):
            a, b = (held[v, x] + size[v] * pole[v, x + 1] for v in range(VECTORS))
            answer[0, x], answer[1, x] = a, b
            grams = [grams[0] + a * a, grams[1] + a * b, grams[2] + b * b]
        return (*grams, carry[3] + packed[d])

    *grams, share_of = over(finish, (zero,) * 4)
    cells = (levels + 1) * width * sub * LANES
    one, mix, two = (
        (total(g) + jnp.sum(share_of[i : i + 1], axis=1, keepdims=True)) / cells
        for i, g in enumerate(grams)
    )
    scale_one = jnp.sqrt(one + EPSILON)
    cross = mix / scale_one
    rest = two - 2.0 * cross * cross + cross * cross * one / (one + EPSILON)
    scale_two = jnp.sqrt(rest + EPSILON)
    over_one, over_two = 1.0 / scale_one, 1.0 / scale_two

    def scale(k, carry):
        unit = tracer[0, k] * over_one
        tracer_out[0, k] = unit
        tracer_out[1, k] = (tracer[1, k] - cross * unit) * over_two
        return carry

    lax.fori_loop(0, levels, scale, 0, unroll=steps(levels, 10))
    for c in range(2):
        x = 2 * me + c
        unit = answer[0, x] * over_one
        surface_out[0, pl.ds(c, sub, stride=2), :] = unit
        surface_out[1, pl.ds(c, sub, stride=2), :] = (answer[1, x] - cross * unit) * over_two
    for i, value in enumerate((scale_one, cross, scale_two)):
        growth[i] = value[0, 0]


def tiled(array):
    *lead, columns, rows = array.shape
    split = array.reshape(*lead, columns, rows // LANES, LANES)
    return jnp.swapaxes(split, -3, -2).reshape(*lead, rows // LANES * columns, LANES)


def untiled(array, columns):
    *lead, high, lanes = array.shape
    split = array.reshape(*lead, high // columns, columns, lanes)
    return jnp.swapaxes(split, -3, -2).reshape(*lead, columns, high // columns * lanes)


def swap(array, mask):
    count = lax.axis_size("lon")
    return lax.ppermute(array, "lon", [(i, i ^ mask) for i in range(count)])


def chip_masks(count):
    lists, loads = ([], []), [0, 0]
    for mask in range(count // 2 - 1, 0, -1):
        core = int(loads[1] < loads[0])
        lists[core].append(mask)
        loads[core] += mask % 2 + mask // 2
    longest = max(map(len, lists))
    return list(zip(*(one + [0] * (longest - len(one)) for one in lists)))


def gather(block):
    count = lax.axis_size("lon")
    pair = jnp.stack([block, swap(block, 1)])
    fetched = []
    for masks in chip_masks(count):
        moves = [(i, i ^ (2 * masks[i % 2])) for i in range(count) if masks[i % 2]]
        fetched.append(lax.ppermute(pair, "lon", moves))
    fetched = jnp.stack(fetched)
    return pair, fetched, swap(fetched, 1)


def on_device(tracer_pert, surface_pert, zonal_flow, merid_flow, bottom_level):
    vectors, levels, columns, rows = tracer_pert.shape
    count = lax.axis_size("lon")
    sub = rows // LANES
    assert vectors == VECTORS and columns == 2 and rows % LANES == 0
    assert count >= 8 and count & (count - 1) == 0
    width = 2 * count
    f32 = jnp.float32
    vmem = pl.BlockSpec(memory_space=pltpu.VMEM)
    hbm = pl.BlockSpec(memory_space=pltpu.HBM)
    params = pltpu.CompilerParams(vmem_limit_bytes=24 * 2**20)

    def shaped(*shape):
        return jax.ShapeDtypeStruct((*shape, sub, LANES), f32)

    def held(*shape):
        return pltpu.VMEM((*shape, sub, LANES), f32)

    both = pltpu.VMEM((vectors, levels, sub * 2, LANES), f32)
    tracer_pert, zonal_flow, merid_flow = map(tiled, (tracer_pert, zonal_flow, merid_flow))
    outward = [(i, (i + 1) % count if i % 2 else (i - 1) % count) for i in range(count)]
    part = (levels + 1) // 2
    bottom = tiled(bottom_level)
    edge_rows = VECTORS * levels + part

    edge = pl.pallas_call(
        functools.partial(edge_kernel, levels, sub),
        out_shape=shaped(edge_rows),
        in_specs=[hbm] * 2,
        out_specs=hbm,
        scratch_shapes=[
            both,
            pltpu.VMEM((part, sub * 2, LANES), f32),
            held(edge_rows),
            pltpu.SemaphoreType.DMA((VECTORS + 1,)),
            pltpu.SemaphoreType.DMA((VECTORS + 1,)),
        ],
        compiler_params=pltpu.CompilerParams(vmem_limit_bytes=60 * 2**20),
        name="edge_columns",
    )(tracer_pert, zonal_flow)
    edge_far = lax.ppermute(edge, "lon", outward)
    flow_other = lax.ppermute(edge_far[VECTORS * levels :], "grp", [(0, 1), (1, 0)])
    cross, mate, raw, mate_raw, flow_in, mate_flow = pl.pallas_call(
        functools.partial(first_kernel, levels, sub),
        out_shape=(
            shaped(VECTORS * levels + 1),
            shaped(VECTORS * levels + 1),
            shaped(VECTORS * levels),
            shaped(VECTORS * levels),
            shaped(levels),
            shaped(levels),
        ),
        in_specs=[pl.BlockSpec(memory_space=pl.ANY)] + [vmem] * 4,
        out_specs=(vmem,) * 6,
        compiler_params=params,
        name="partial_step",
    )(edge, tracer_pert, zonal_flow, merid_flow, bottom)
    cross_far = lax.ppermute(cross, "lon", outward)
    mate_far, mate_raw_far, mate_flow_far = (swap(x, 1) for x in (mate, mate_raw, mate_flow))
    tracer, message = pl.pallas_call(
        functools.partial(second_kernel, levels, sub),
        out_shape=(
            jax.ShapeDtypeStruct((vectors, levels, sub * 2, LANES), f32),
            shaped(BLOCKS),
        ),
        in_specs=[vmem] * 15,
        out_specs=(vmem, vmem),
        scratch_shapes=[held(levels)],
        compiler_params=params,
        name="both_steps",
    )(
        raw, cross, mate, mate_raw, flow_in, mate_flow,
        edge_far, cross_far, mate_far, mate_raw_far, mate_flow_far, flow_other,
        merid_flow, tiled(surface_pert), bottom,
    )
    tracer_vec, surface_vec, growth = pl.pallas_call(
        functools.partial(third_kernel, levels, sub, count),
        out_shape=(
            jax.ShapeDtypeStruct((vectors, levels, sub * 2, LANES), f32),
            jax.ShapeDtypeStruct((vectors, sub * 2, LANES), f32),
            jax.ShapeDtypeStruct((3,), f32),
        ),
        in_specs=[vmem] * 4,
        out_specs=(vmem, vmem, pl.BlockSpec(memory_space=pltpu.SMEM)),
        scratch_shapes=[
            held(vectors, width + 2),
            *[held(vectors, width)] * 4,
            held(width),
            held(width + 1),
            held(width),
            held(width),
            held(count),
        ],
        compiler_params=pltpu.CompilerParams(vmem_limit_bytes=32 * 2**20),
        name="surface_and_scale",
    )(*gather(message), tracer)
    return (untiled(tracer_vec, 2), untiled(surface_vec, 2), growth)


def solution(mesh):
    placed = (
        P("grp", None, "lon", None),
        P("grp", "lon", None),
        P(None, "lon", None),
        P(None, "lon", None),
        P("lon", None),
    )
    return jax.shard_map(
        on_device,
        mesh=mesh,
        in_specs=placed,
        out_specs=(P("grp", None, "lon", None), P("grp", "lon", None), P("grp")),
        check_vma=False,
    )
```

```python
import functools

import jax
import jax.numpy as jnp
from jax import lax
from jax.experimental import pallas as pl
from jax.experimental.pallas import tpu as pltpu
from jax.sharding import PartitionSpec as P

ITERS = 3


DIFFUSIVITY = 0.5
TIME_STEP = 0.2
SURFACE_COUPLING = 0.5
STERIC_GAIN = 2.0
EPSILON = 1e-06

LANES = 128
VECTORS = 2
SLOPE = 0.25 * TIME_STEP
SPREAD = TIME_STEP * DIFFUSIVITY
GRAMS = VECTORS * 2
SUMS = GRAMS + 1
DEPTHS = VECTORS * 2
RIM = DEPTHS + 2


def next_row(tile):
    turned = pltpu.roll(tile, LANES - 1, 1)
    carried = pltpu.roll(turned, tile.shape[0] - 1, 0)
    lane = lax.broadcasted_iota(jnp.int32, tile.shape, 1)
    return jnp.where(lane == LANES - 1, carried, turned)


def prior_row(tile):
    turned = pltpu.roll(tile, 1, 1)
    carried = pltpu.roll(turned, 1, 0)
    lane = lax.broadcasted_iota(jnp.int32, tile.shape, 1)
    return jnp.where(lane == 0, carried, turned)


def wall_depth(depth):
    subs, lane = (lax.broadcasted_iota(jnp.int32, depth.shape, axis) for axis in (0, 1))
    last = (subs == depth.shape[0] - 1) & (lane == LANES - 1)
    return jnp.where(last, jnp.zeros_like(depth), jnp.minimum(depth, next_row(depth)))


def face_pair(level, face_depth, flow_sum):
    slope = SLOPE * flow_sum
    open_face = level < face_depth
    return (
        jnp.where(open_face, slope + SPREAD, 0.0),
        jnp.where(open_face, slope - SPREAD, 0.0),
    )


def outflow(pair, near, far):
    return pair[0] * near + pair[1] * far


def side_pairs(level, depths, flow):
    return (
        face_pair(level, depths[0], flow + next_row(flow)),
        face_pair(level, depths[1], -(flow + prior_row(flow))),
    )


def divergence_y(pairs, tile):
    return outflow(pairs[0], tile, next_row(tile)) + outflow(pairs[1], tile, prior_row(tile))


def side_depths(depth):
    north = wall_depth(depth)
    return north, prior_row(north)


def orientation():
    outer = lax.rem(lax.axis_index("lon"), 2)
    return outer, 1 - outer, (2 * outer - 1).astype(jnp.float32)


def steps(count, most):
    return max(u for u in range(1, most + 1) if count % u == 0)


def share(levels):
    size = lax.axis_size("grp")
    assert size == 2
    part = (levels + 1) // 2
    return lax.axis_index("grp") * (levels - part), part


def edge_kernel(
    levels, sub, tracer_hbm, zonal_hbm, edge_hbm, tracer, zonal, edge, sems_in, sems_out
):
    outer, _, _ = orientation()
    start, part = share(levels)

    def move(source, target, sem):
        copy = pltpu.make_async_copy(source, target, sem)
        copy.start()
        return copy

    arrivals = [
        move(tracer_hbm.at[v], tracer.at[v], sems_in.at[v]) for v in range(VECTORS)
    ] + [move(zonal_hbm.at[pl.ds(start, part)], zonal, sems_in.at[VECTORS])]
    departures = []
    for v, arrival in enumerate(arrivals):
        number = part if v == VECTORS else levels
        arrival.wait()

        def body(k, carry, v=v):
            source = zonal if v == VECTORS else tracer.at[v]
            edge[v * levels + k] = source[k, pl.ds(outer, sub, stride=2), :]
            return carry

        lax.fori_loop(0, number, body, 0, unroll=steps(number, 10))
        rows = pl.ds(v * levels, number)
        departures.append(move(edge.at[rows], edge_hbm.at[rows], sems_out.at[v]))
    for departure in departures:
        departure.wait()


def first_kernel(
    levels, sub, edge, tracer, zonal, merid, surface, bottom,
    cross, mate, raw, mate_raw, flow_in, mate_flow,
):
    del edge
    outer, inner, sign = orientation()

    def column(ref, where, *lead):
        return ref[(*lead, pl.ds(where, sub, stride=2), slice(None))]

    depth = [column(bottom, where).astype(jnp.float32) for where in (outer, inner)]
    between = jnp.minimum(*depth)
    along = [side_depths(d) for d in depth]
    cross[VECTORS * levels] = depth[0]
    mate[VECTORS * levels] = depth[1]
    for c in range(2):
        for v in range(VECTORS):
            mate_flow[levels + v * 2 + c] = column(surface, c, v)
        mate_flow[levels + DEPTHS + c] = column(bottom, c).astype(jnp.float32)

    def body(k, carry):
        level = k.astype(jnp.float32)
        flow = [column(zonal, where, k) for where in (outer, inner)]
        turn = [column(merid, where, k) for where in (outer, inner)]
        middle = face_pair(level, between, -sign * (flow[0] + flow[1]))
        sides = [side_pairs(level, along[c], turn[c]) for c in range(2)]
        for v in range(VECTORS):
            cells = [column(tracer, where, v, k) for where in (outer, inner)]
            flux = outflow(middle, *cells)
            kept = [
                jnp.where(level < depth[c], cells[c], 0.0) - divergence_y(sides[c], cells[c])
                for c in range(2)
            ]
            cross[v * levels + k] = kept[0] - flux
            raw[v * levels + k] = cells[0]
            mate[v * levels + k] = kept[1] + flux
            mate_raw[v * levels + k] = cells[1]
        flow_in[k] = flow[0]
        mate_flow[k] = flow[1]
        return carry

    lax.fori_loop(0, levels, body, 0, unroll=steps(levels, 10))


def wrap(pole, width):
    for v in range(VECTORS):
        pole[v, 0] = pole[v, width]
        pole[v, width + 1] = pole[v, 1]


def spread(pole, face_x, face_y, face_z, v, x):
    west, centre, east = (pole[v, x + j] for j in range(3))
    return (face_x[x + 1] * (east - centre) - face_x[x] * (centre - west)) + (
        face_y[x] * (next_row(centre) - centre) - face_z[x] * (centre - prior_row(centre))
    )


def second_kernel(
    levels, sub, raw, cross, mate, mate_raw, flow_in, mate_flow,
    raw_far, cross_far, mate_far, mate_raw_far, mate_flow_far, flow_other,
    merid, tracer, late, early, flow_far,
):
    outer, inner, sign = orientation()
    start, part = share(levels)
    last = VECTORS * levels

    def unpack(i, carry):
        flow_far[start + i] = raw_far[VECTORS * levels + i]
        flow_far[levels - part - start + i] = flow_other[i]
        return carry

    lax.fori_loop(0, part, unpack, 0, unroll=steps(part, 10))
    near = [(raw, cross), (mate_raw, mate)]
    far = [(raw_far, cross_far), (mate_raw_far, mate_far)]
    depth = [cross[last], mate[last]]
    beside = [jnp.minimum(depth[0], cross_far[last]), jnp.minimum(depth[1], mate_far[last])]
    between = jnp.minimum(*depth)
    along = [side_depths(d) for d in depth]
    zero = jnp.zeros_like(between)

    def body(k, carry):
        level = k.astype(jnp.float32)
        flow = [flow_in[k], mate_flow[k]]
        beyond = [flow_far[k], mate_flow_far[k]]
        turn = [merid[k, pl.ds(where, sub, stride=2), :] for where in (outer, inner)]
        middle = face_pair(level, between, -sign * (flow[0] + flow[1]))
        edges = [
            face_pair(level, beside[c], (sign, -sign)[c] * (flow[c] + beyond[c])) for c in range(2)
        ]
        sides = [side_pairs(level, along[c], turn[c]) for c in range(2)]
        totals, grams = list(carry[:4]), list(carry[4:])
        done = []
        for v in range(VECTORS):
            own, other = [], []
            for c in range(2):
                (first, kept), (first_far, kept_far) = near[c], far[c]
                row = v * levels + k
                flux = outflow(edges[c], first[row], first_far[row])
                own.append(kept[row] - flux)
                other.append(kept_far[row] + flux)
            crossing = outflow(middle, *own)
            fresh = []
            for c, where in enumerate((outer, inner)):
                gone = crossing if c == 0 else -crossing
                value = (
                    own[c]
                    - outflow(edges[c], own[c], other[c])
                    - gone
                    - divergence_y(sides[c], own[c])
                )
                tracer[v, k, pl.ds(where, sub, stride=2), :] = value
                totals[v * 2 + c] = totals[v * 2 + c] + value
                fresh.append(value)
            done.append(fresh)
        for c in range(2):
            a, b = done[0][c], done[1][c]
            grams = [grams[0] + a * a, grams[1] + a * b, grams[2] + b * b]
        return (*totals, *grams)

    sums = lax.fori_loop(0, levels, body, (zero,) * 7, unroll=steps(levels, 10))
    gain = STERIC_GAIN / levels
    subs = lax.broadcasted_iota(jnp.int32, zero.shape, 0)
    packed = zero
    for i, gram in enumerate(sums[4:]):
        packed = jnp.where(subs == i, jnp.sum(gram, axis=0, keepdims=True), packed)
    late[GRAMS] = packed
    early[GRAMS] = packed
    for v in range(VECTORS):
        for c, where in enumerate((outer, inner)):
            late[v * 2 + where] = gain * sums[v * 2 + c]
            early[v * 2 + where] = gain * sums[v * 2 + c]
    for row in range(RIM):
        early[SUMS + row] = mate_flow[levels + row]
        early[SUMS + RIM + row] = mate_flow_far[levels + row]


def total(tile):
    return jnp.sum(jnp.sum(tile, axis=0, keepdims=True), axis=1, keepdims=True)


def early_of(chip):
    return 2 * chip + chip % 2


def late_of(chip):
    return 2 * chip + 1 - chip % 2


def third_kernel(levels, sub, count, *refs):
    chips = count // 2
    lates, (early, beside), around = refs[:chips], refs[chips : chips + 2], refs[chips + 2 : chips + 1 + chips // 2]
    (own, mates, pole, residual, answer, image, height, depth, face_x, face_y, face_z, packed) = refs[
        chips + 1 + chips // 2 :
    ]
    width = 2 * count
    chip = lax.axis_index("lon") // 2
    zero = jnp.zeros((sub, LANES), jnp.float32)
    none = (zero,) * VECTORS

    def device(of, mask):
        where = chip ^ mask
        odd = lax.rem(where, 2)
        return 2 * where + (odd if of is early_of else 1 - odd)

    def place_sums(owner, block):
        packed[owner] = block[GRAMS]
        for c in range(2):
            for v in range(VECTORS):
                residual[v, 2 * owner + c] = block[v * 2 + c]

    def place_rim(owner, block, base):
        for c in range(2):
            x = 2 * owner + c
            floor = block[base + DEPTHS + c]
            depth[x] = floor
            for v in range(VECTORS):
                tall = jnp.where(floor > 0, block[base + v * 2 + c], 0.0)
                height[v, x] = tall
                pole[v, x + 1] = tall

    for mask, block in enumerate(lates):
        place_sums(device(late_of, mask), block)
    pairs = [(early, beside)] + [(ref.at[0], ref.at[1]) for ref in around]
    for mask, pair in enumerate(pairs):
        for slot, block in enumerate(pair):
            place_sums(device(early_of, 2 * mask + slot), block)
            place_rim(device(early_of, 2 * mask + slot), block, SUMS)
            place_rim(device(late_of, 2 * mask + slot), block, SUMS + RIM)

    def over(body, init):
        return lax.fori_loop(0, count, body, init, unroll=steps(count, 16))

    def each(d):
        return [(v, c, 2 * d + c) for v in range(VECTORS) for c in range(2)]

    def prepare(d, carry):
        for x in (2 * d, 2 * d + 1):
            here, after = depth[x], depth[lax.rem(x + 1, width)]
            face_x[x + 1] = SURFACE_COUPLING * jnp.minimum(here, after)
            north, south = side_depths(here)
            face_y[x] = SURFACE_COUPLING * north
            face_z[x] = SURFACE_COUPLING * south
        return carry

    over(prepare, 0)
    face_x[0] = face_x[width]
    wrap(pole, width)

    def start(d, carry):
        sums = list(carry)
        for v, _, x in each(d):
            value = residual[v, x] + spread(pole, face_x, face_y, face_z, v, x)
            residual[v, x] = value
            sums[v] = sums[v] + value * value
        return tuple(sums)

    norm = [total(t) for t in over(start, none)]

    def aim(d, carry):
        for v, _, x in each(d):
            pole[v, x + 1] = residual[v, x]
        return carry

    over(aim, 0)
    wrap(pole, width)

    def apply(d, carry):
        sums = list(carry)
        for v, _, x in each(d):
            centre = pole[v, x + 1]
            value = centre - spread(pole, face_x, face_y, face_z, v, x)
            image[v, x] = value
            sums[v] = sums[v] + centre * value
        return tuple(sums)

    for iteration in range(ITERS):
        energy = [total(t) for t in over(apply, none)]
        size = [n / e for n, e in zip(norm, energy)]
        held = height if iteration == 0 else answer
        if iteration + 1 < ITERS:

            def advance(d, carry, size=size, held=held):
                sums = list(carry)
                for v, _, x in each(d):
                    answer[v, x] = held[v, x] + size[v] * pole[v, x + 1]
                    value = residual[v, x] - size[v] * image[v, x]
                    residual[v, x] = value
                    sums[v] = sums[v] + value * value
                return tuple(sums)

            fresh = [total(t) for t in over(advance, none)]
            ratio = [f / n for f, n in zip(fresh, norm)]

            def turn(d, carry, ratio=ratio):
                for v, _, x in each(d):
                    pole[v, x + 1] = residual[v, x] + ratio[v] * pole[v, x + 1]
                return carry

            over(turn, 0)
            wrap(pole, width)
            norm = fresh

    def finish(d, carry):
        grams = list(carry)
        for x in (2 * d, 2 * d + 1):
            a, b = (held[v, x] + size[v] * pole[v, x + 1] for v in range(VECTORS))
            answer[0, x], answer[1, x] = a, b
            grams = [grams[0] + a * a, grams[1] + a * b, grams[2] + b * b]
        return (*grams, carry[3] + packed[d])

    *grams, share_of = over(finish, (zero,) * 4)
    cells = (levels + 1) * width * sub * LANES
    one, mix, two = (
        (total(g) + jnp.sum(share_of[i : i + 1], axis=1, keepdims=True)) / cells
        for i, g in enumerate(grams)
    )
    scale_one = jnp.sqrt(one + EPSILON)
    cross = mix / scale_one
    rest = two - 2.0 * cross * cross + cross * cross * one / (one + EPSILON)
    scale_two = jnp.sqrt(rest + EPSILON)
    over_one, over_two = 1.0 / scale_one, 1.0 / scale_two

    factors = (over_one, cross, over_two, scale_one, scale_two)
    subs = lax.broadcasted_iota(jnp.int32, zero.shape, 0)
    listed = zero
    for i, factor in enumerate(factors):
        listed = jnp.where(subs == i, factor, listed)
    for of, result in ((early_of, own), (late_of, mates)):
        for v in range(VECTORS):
            for c in range(2):
                result[v * 2 + c] = answer[v, 2 * device(of, 0) + c]
        result[VECTORS * 2] = listed


def fourth_kernel(levels, sub, solved, told, tracer, tracer_out, surface_out, growth):
    me = lax.axis_index("lon")
    solver = lax.rem((me + 1) // 2, 2) == 0

    def known(row):
        return jnp.where(solver, solved[row], told[row])

    listed = known(VECTORS * 2)
    over_one, cross, over_two = (listed[i : i + 1, :1] for i in range(3))
    for i in range(3):
        growth[i] = listed[(3, 1, 4)[i], 0]
    for c in range(2):
        unit = known(c) * over_one
        surface_out[0, pl.ds(c, sub, stride=2), :] = unit
        surface_out[1, pl.ds(c, sub, stride=2), :] = (known(2 + c) - cross * unit) * over_two

    def scale(k, carry):
        unit = tracer[0, k] * over_one
        tracer_out[0, k] = unit
        tracer_out[1, k] = (tracer[1, k] - cross * unit) * over_two
        return carry

    lax.fori_loop(0, levels, scale, 0, unroll=steps(levels, 10))


def tiled(array):
    *lead, columns, rows = array.shape
    split = array.reshape(*lead, columns, rows // LANES, LANES)
    return jnp.swapaxes(split, -3, -2).reshape(*lead, rows // LANES * columns, LANES)


def untiled(array, columns):
    *lead, high, lanes = array.shape
    split = array.reshape(*lead, high // columns, columns, lanes)
    return jnp.swapaxes(split, -3, -2).reshape(*lead, columns, high // columns * lanes)


def swap(array, mask):
    count = lax.axis_size("lon")
    return lax.ppermute(array, "lon", [(i, i ^ mask) for i in range(count)])


def chip_moves(count, source, target, mask):
    return [(source(chip), target(chip ^ mask)) for chip in range(count // 2)]


def gather(late, early):
    count = lax.axis_size("lon")
    chips = count // 2
    lates = [
        lax.ppermute(late, "lon", chip_moves(count, late_of, early_of, mask)) for mask in range(chips)
    ]

    def exchange(block):
        beside = lax.ppermute(block, "lon", chip_moves(count, early_of, early_of, 1))
        pair = jnp.stack([block, beside])
        around = [
            lax.ppermute(pair, "lon", chip_moves(count, early_of, early_of, mask))
            for mask in range(2, chips, 2)
        ]
        return (beside, *around)

    def nothing(block):
        return (block, *[jnp.stack([block, block])] * (chips // 2 - 1))

    waits = ((lax.axis_index("lon") + 1) // 2) % 2 == 0
    beside, *around = lax.cond(waits, exchange, nothing, early)
    return [*lates, early, beside, *around]


def on_device(tracer_pert, surface_pert, zonal_flow, merid_flow, bottom_level):
    vectors, levels, columns, rows = tracer_pert.shape
    count = lax.axis_size("lon")
    sub = rows // LANES
    assert vectors == VECTORS and columns == 2 and rows % LANES == 0
    assert count >= 8 and count & (count - 1) == 0
    width = 2 * count
    f32 = jnp.float32
    vmem = pl.BlockSpec(memory_space=pltpu.VMEM)
    hbm = pl.BlockSpec(memory_space=pltpu.HBM)
    params = pltpu.CompilerParams(vmem_limit_bytes=24 * 2**20)

    def shaped(*shape):
        return jax.ShapeDtypeStruct((*shape, sub, LANES), f32)

    def held(*shape):
        return pltpu.VMEM((*shape, sub, LANES), f32)

    both = pltpu.VMEM((vectors, levels, sub * 2, LANES), f32)
    tracer_pert, zonal_flow, merid_flow = map(tiled, (tracer_pert, zonal_flow, merid_flow))
    outward = [(i, (i + 1) % count if i % 2 else (i - 1) % count) for i in range(count)]
    part = (levels + 1) // 2
    edge_rows = VECTORS * levels + part

    edge = pl.pallas_call(
        functools.partial(edge_kernel, levels, sub),
        out_shape=shaped(edge_rows),
        in_specs=[hbm] * 2,
        out_specs=hbm,
        scratch_shapes=[
            both,
            pltpu.VMEM((part, sub * 2, LANES), f32),
            held(edge_rows),
            pltpu.SemaphoreType.DMA((VECTORS + 1,)),
            pltpu.SemaphoreType.DMA((VECTORS + 1,)),
        ],
        compiler_params=pltpu.CompilerParams(vmem_limit_bytes=60 * 2**20),
        name="edge_columns",
    )(tracer_pert, zonal_flow)
    edge_far = lax.ppermute(edge, "lon", outward)
    flow_other = lax.ppermute(edge_far[VECTORS * levels :], "grp", [(0, 1), (1, 0)])
    cross, mate, raw, mate_raw, flow_in, mate_flow = pl.pallas_call(
        functools.partial(first_kernel, levels, sub),
        out_shape=(
            shaped(VECTORS * levels + 1),
            shaped(VECTORS * levels + 1),
            shaped(VECTORS * levels),
            shaped(VECTORS * levels),
            shaped(levels),
            shaped(levels + RIM),
        ),
        in_specs=[pl.BlockSpec(memory_space=pl.ANY)] + [vmem] * 5,
        out_specs=(vmem,) * 6,
        compiler_params=params,
        name="partial_step",
    )(edge, tracer_pert, zonal_flow, merid_flow, tiled(surface_pert), tiled(bottom_level))
    cross_far = lax.ppermute(cross, "lon", outward)
    mate_far, mate_raw_far, mate_flow_far = (swap(x, 1) for x in (mate, mate_raw, mate_flow))
    tracer, late, early = pl.pallas_call(
        functools.partial(second_kernel, levels, sub),
        out_shape=(
            jax.ShapeDtypeStruct((vectors, levels, sub * 2, LANES), f32),
            shaped(SUMS),
            shaped(SUMS + 2 * RIM),
        ),
        in_specs=[vmem] * 13,
        out_specs=(vmem,) * 3,
        scratch_shapes=[held(levels)],
        compiler_params=params,
        name="both_steps",
    )(
        raw, cross, mate, mate_raw, flow_in, mate_flow,
        edge_far, cross_far, mate_far, mate_raw_far, mate_flow_far, flow_other,
        merid_flow,
    )
    blocks = gather(late, early)
    result = shaped(SUMS)
    solved, solved_mate = pl.pallas_call(
        functools.partial(third_kernel, levels, sub, count),
        out_shape=(result, result),
        in_specs=[vmem] * len(blocks),
        out_specs=(vmem, vmem),
        scratch_shapes=[
            held(vectors, width + 2),
            *[held(vectors, width)] * 4,
            held(width),
            held(width + 1),
            held(width),
            held(width),
            held(count),
        ],
        compiler_params=pltpu.CompilerParams(vmem_limit_bytes=32 * 2**20),
        name="surface_solve",
    )(*blocks)
    told = lax.ppermute(solved_mate, "lon", chip_moves(count, early_of, late_of, 0))
    tracer_vec, surface_vec, growth = pl.pallas_call(
        functools.partial(fourth_kernel, levels, sub),
        out_shape=(
            jax.ShapeDtypeStruct((vectors, levels, sub * 2, LANES), f32),
            jax.ShapeDtypeStruct((vectors, sub * 2, LANES), f32),
            jax.ShapeDtypeStruct((3,), f32),
        ),
        in_specs=[vmem] * 3,
        out_specs=(vmem, vmem, pl.BlockSpec(memory_space=pltpu.SMEM)),
        compiler_params=params,
        name="scale",
    )(solved, told, tracer)
    return (untiled(tracer_vec, 2), untiled(surface_vec, 2), growth)


def solution(mesh):
    placed = (
        P("grp", None, "lon", None),
        P("grp", "lon", None),
        P(None, "lon", None),
        P(None, "lon", None),
        P("lon", None),
    )
    return jax.shard_map(
        on_device,
        mesh=mesh,
        in_specs=placed,
        out_specs=(P("grp", None, "lon", None), P("grp", "lon", None), P("grp")),
        check_vma=False,
    )
```

```python
import functools

import jax
import jax.numpy as jnp
from jax import lax
from jax.experimental import pallas as pl
from jax.experimental.pallas import tpu as pltpu
from jax.sharding import PartitionSpec as P

ITERS = 3


DIFFUSIVITY = 0.5
TIME_STEP = 0.2
SURFACE_COUPLING = 0.5
STERIC_GAIN = 2.0
EPSILON = 1e-06

LANES = 128
VECTORS = 2
SLOPE = 0.25 * TIME_STEP
SPREAD = TIME_STEP * DIFFUSIVITY
HEIGHTS = VECTORS * 2
DEPTHS = HEIGHTS + VECTORS * 2
GRAMS = DEPTHS + 2
BLOCKS = GRAMS + 1


def next_row(tile):
    turned = pltpu.roll(tile, LANES - 1, 1)
    carried = pltpu.roll(turned, tile.shape[0] - 1, 0)
    lane = lax.broadcasted_iota(jnp.int32, tile.shape, 1)
    return jnp.where(lane == LANES - 1, carried, turned)


def prior_row(tile):
    turned = pltpu.roll(tile, 1, 1)
    carried = pltpu.roll(turned, 1, 0)
    lane = lax.broadcasted_iota(jnp.int32, tile.shape, 1)
    return jnp.where(lane == 0, carried, turned)


def wall_depth(depth):
    subs, lane = (lax.broadcasted_iota(jnp.int32, depth.shape, axis) for axis in (0, 1))
    last = (subs == depth.shape[0] - 1) & (lane == LANES - 1)
    return jnp.where(last, jnp.zeros_like(depth), jnp.minimum(depth, next_row(depth)))


def face_pair(level, face_depth, flow_sum):
    slope = SLOPE * flow_sum
    open_face = level < face_depth
    return (
        jnp.where(open_face, slope + SPREAD, 0.0),
        jnp.where(open_face, slope - SPREAD, 0.0),
    )


def outflow(pair, near, far):
    return pair[0] * near + pair[1] * far


def side_pairs(level, depths, flow):
    return (
        face_pair(level, depths[0], flow + next_row(flow)),
        face_pair(level, depths[1], -(flow + prior_row(flow))),
    )


def divergence_y(pairs, tile):
    return outflow(pairs[0], tile, next_row(tile)) + outflow(pairs[1], tile, prior_row(tile))


def side_depths(depth):
    north = wall_depth(depth)
    return north, prior_row(north)


def orientation():
    outer = lax.rem(lax.axis_index("lon"), 2)
    return outer, 1 - outer, (2 * outer - 1).astype(jnp.float32)


def steps(count, most):
    return max(u for u in range(1, most + 1) if count % u == 0)


def share(levels):
    size = lax.axis_size("grp")
    assert size == 2
    part = (levels + 1) // 2
    return lax.axis_index("grp") * (levels - part), part


def edge_kernel(
    levels, sub, tracer_hbm, zonal_hbm, edge_hbm, tracer, zonal, edge, sems_in, sems_out
):
    outer, _, _ = orientation()
    start, part = share(levels)

    def move(source, target, sem):
        copy = pltpu.make_async_copy(source, target, sem)
        copy.start()
        return copy

    arrivals = [
        move(tracer_hbm.at[v], tracer.at[v], sems_in.at[v]) for v in range(VECTORS)
    ] + [move(zonal_hbm.at[pl.ds(start, part)], zonal, sems_in.at[VECTORS])]
    departures = []
    for v, arrival in enumerate(arrivals):
        number = part if v == VECTORS else levels
        arrival.wait()

        def body(k, carry, v=v):
            source = zonal if v == VECTORS else tracer.at[v]
            edge[v * levels + k] = source[k, pl.ds(outer, sub, stride=2), :]
            return carry

        lax.fori_loop(0, number, body, 0, unroll=steps(number, 10))
        rows = pl.ds(v * levels, number)
        departures.append(move(edge.at[rows], edge_hbm.at[rows], sems_out.at[v]))
    for departure in departures:
        departure.wait()


def first_kernel(
    levels, sub, edge, tracer, zonal, merid, bottom, cross, mate, raw, mate_raw, flow_in, mate_flow
):
    del edge
    outer, inner, sign = orientation()

    def column(ref, where, *lead):
        return ref[(*lead, pl.ds(where, sub, stride=2), slice(None))]

    depth = [column(bottom, where).astype(jnp.float32) for where in (outer, inner)]
    between = jnp.minimum(*depth)
    along = [side_depths(d) for d in depth]
    cross[VECTORS * levels] = depth[0]
    mate[VECTORS * levels] = depth[1]

    def body(k, carry):
        level = k.astype(jnp.float32)
        flow = [column(zonal, where, k) for where in (outer, inner)]
        turn = [column(merid, where, k) for where in (outer, inner)]
        middle = face_pair(level, between, -sign * (flow[0] + flow[1]))
        sides = [side_pairs(level, along[c], turn[c]) for c in range(2)]
        for v in range(VECTORS):
            cells = [column(tracer, where, v, k) for where in (outer, inner)]
            flux = outflow(middle, *cells)
            kept = [
                jnp.where(level < depth[c], cells[c], 0.0) - divergence_y(sides[c], cells[c])
                for c in range(2)
            ]
            cross[v * levels + k] = kept[0] - flux
            raw[v * levels + k] = cells[0]
            mate[v * levels + k] = kept[1] + flux
            mate_raw[v * levels + k] = cells[1]
        flow_in[k] = flow[0]
        mate_flow[k] = flow[1]
        return carry

    lax.fori_loop(0, levels, body, 0, unroll=steps(levels, 10))


def wrap(pole, width):
    for v in range(VECTORS):
        pole[v, 0] = pole[v, width]
        pole[v, width + 1] = pole[v, 1]


def spread(pole, face_x, face_y, face_z, v, x):
    west, centre, east = (pole[v, x + j] for j in range(3))
    return (face_x[x + 1] * (east - centre) - face_x[x] * (centre - west)) + (
        face_y[x] * (next_row(centre) - centre) - face_z[x] * (centre - prior_row(centre))
    )


def second_kernel(
    levels, sub, raw, cross, mate, mate_raw, flow_in, mate_flow,
    raw_far, cross_far, mate_far, mate_raw_far, mate_flow_far, flow_other,
    merid, surface, bottom, tracer, message, flow_far,
):
    outer, inner, sign = orientation()
    start, part = share(levels)
    last = VECTORS * levels

    def unpack(i, carry):
        flow_far[start + i] = raw_far[VECTORS * levels + i]
        flow_far[levels - part - start + i] = flow_other[i]
        return carry

    lax.fori_loop(0, part, unpack, 0, unroll=steps(part, 10))
    near = [(raw, cross), (mate_raw, mate)]
    far = [(raw_far, cross_far), (mate_raw_far, mate_far)]
    depth = [cross[last], mate[last]]
    beside = [jnp.minimum(depth[0], cross_far[last]), jnp.minimum(depth[1], mate_far[last])]
    between = jnp.minimum(*depth)
    along = [side_depths(d) for d in depth]
    zero = jnp.zeros_like(between)

    def body(k, carry):
        level = k.astype(jnp.float32)
        flow = [flow_in[k], mate_flow[k]]
        beyond = [flow_far[k], mate_flow_far[k]]
        turn = [merid[k, pl.ds(where, sub, stride=2), :] for where in (outer, inner)]
        middle = face_pair(level, between, -sign * (flow[0] + flow[1]))
        edges = [
            face_pair(level, beside[c], (sign, -sign)[c] * (flow[c] + beyond[c])) for c in range(2)
        ]
        sides = [side_pairs(level, along[c], turn[c]) for c in range(2)]
        totals, grams = list(carry[:4]), list(carry[4:])
        done = []
        for v in range(VECTORS):
            own, other = [], []
            for c in range(2):
                (first, kept), (first_far, kept_far) = near[c], far[c]
                row = v * levels + k
                flux = outflow(edges[c], first[row], first_far[row])
                own.append(kept[row] - flux)
                other.append(kept_far[row] + flux)
            crossing = outflow(middle, *own)
            fresh = []
            for c, where in enumerate((outer, inner)):
                gone = crossing if c == 0 else -crossing
                value = (
                    own[c]
                    - outflow(edges[c], own[c], other[c])
                    - gone
                    - divergence_y(sides[c], own[c])
                )
                tracer[v, k, pl.ds(where, sub, stride=2), :] = value
                totals[v * 2 + c] = totals[v * 2 + c] + value
                fresh.append(value)
            done.append(fresh)
        for c in range(2):
            a, b = done[0][c], done[1][c]
            grams = [grams[0] + a * a, grams[1] + a * b, grams[2] + b * b]
        return (*totals, *grams)

    sums = lax.fori_loop(0, levels, body, (zero,) * 7, unroll=steps(levels, 10))
    gain = STERIC_GAIN / levels
    subs = lax.broadcasted_iota(jnp.int32, zero.shape, 0)
    packed = zero
    for i, gram in enumerate(sums[4:]):
        packed = jnp.where(subs == i, jnp.sum(gram, axis=0, keepdims=True), packed)
    message[GRAMS] = packed
    for v in range(VECTORS):
        for c, where in enumerate((outer, inner)):
            message[v * 2 + where] = gain * sums[v * 2 + c]
            message[HEIGHTS + v * 2 + c] = surface[v, pl.ds(c, sub, stride=2), :]
    for c in range(2):
        message[DEPTHS + c] = bottom[pl.ds(c, sub, stride=2), :].astype(jnp.float32)


def total(tile):
    return jnp.sum(jnp.sum(tile, axis=0, keepdims=True), axis=1, keepdims=True)


def third_kernel(
    levels, sub, count, pair, fetched, fetched_mate, tracer, tracer_out, surface_out, growth,
    pole, residual, answer, image, height, depth, face_x, face_y, face_z, packed,
):
    width = 2 * count
    me = lax.axis_index("lon")
    core = lax.rem(me, 2)
    zero = jnp.zeros((sub, LANES), jnp.float32)
    none = (zero,) * VECTORS

    def place(owner, block):
        packed[owner] = block(GRAMS)
        for c in range(2):
            x = 2 * owner + c
            floor = block(DEPTHS + c)
            depth[x] = floor
            for v in range(VECTORS):
                tall = jnp.where(floor > 0, block(HEIGHTS + v * 2 + c), 0.0)
                height[v, x] = tall
                pole[v, x + 1] = tall
                residual[v, x] = block(v * 2 + c)

    for slot in range(2):
        place(me ^ slot, lambda row, slot=slot: pair[slot, row])
    for ref, flip in ((fetched, 0), (fetched_mate, 1)):
        for j, masks in enumerate(chip_masks(count)):
            mask = jnp.where((core ^ flip) == 0, *masks)
            for slot in range(2):
                owner = me ^ flip ^ slot ^ (2 * mask)

                def put(owner=owner, ref=ref, j=j, slot=slot):
                    place(owner, lambda row: ref[j, slot, row])

                if all(masks):
                    put()
                else:
                    pl.when(mask > 0)(put)

    def over(body, init):
        return lax.fori_loop(0, count, body, init, unroll=steps(count, 16))

    def each(d):
        return [(v, c, 2 * d + c) for v in range(VECTORS) for c in range(2)]

    def prepare(d, carry):
        for x in (2 * d, 2 * d + 1):
            here, after = depth[x], depth[lax.rem(x + 1, width)]
            face_x[x + 1] = SURFACE_COUPLING * jnp.minimum(here, after)
            north, south = side_depths(here)
            face_y[x] = SURFACE_COUPLING * north
            face_z[x] = SURFACE_COUPLING * south
        return carry

    over(prepare, 0)
    face_x[0] = face_x[width]
    wrap(pole, width)

    def start(d, carry):
        sums = list(carry)
        for v, _, x in each(d):
            value = residual[v, x] + spread(pole, face_x, face_y, face_z, v, x)
            residual[v, x] = value
            sums[v] = sums[v] + value * value
        return tuple(sums)

    norm = [total(t) for t in over(start, none)]

    def aim(d, carry):
        for v, _, x in each(d):
            pole[v, x + 1] = residual[v, x]
        return carry

    over(aim, 0)
    wrap(pole, width)

    def apply(d, carry):
        sums = list(carry)
        for v, _, x in each(d):
            centre = pole[v, x + 1]
            value = centre - spread(pole, face_x, face_y, face_z, v, x)
            image[v, x] = value
            sums[v] = sums[v] + centre * value
        return tuple(sums)

    for iteration in range(ITERS):
        energy = [total(t) for t in over(apply, none)]
        size = [n / e for n, e in zip(norm, energy)]
        held = height if iteration == 0 else answer
        if iteration + 1 < ITERS:

            def advance(d, carry, size=size, held=held):
                sums = list(carry)
                for v, _, x in each(d):
                    answer[v, x] = held[v, x] + size[v] * pole[v, x + 1]
                    value = residual[v, x] - size[v] * image[v, x]
                    residual[v, x] = value
                    sums[v] = sums[v] + value * value
                return tuple(sums)

            fresh = [total(t) for t in over(advance, none)]
            ratio = [f / n for f, n in zip(fresh, norm)]

            def turn(d, carry, ratio=ratio):
                for v, _, x in each(d):
                    pole[v, x + 1] = residual[v, x] + ratio[v] * pole[v, x + 1]
                return carry

            over(turn, 0)
            wrap(pole, width)
            norm = fresh

    def finish(d, carry):
        grams = list(carry)
        for x in (2 * d, 2 * d + 1):
            a, b = (held[v, x] + size[v] * pole[v, x + 1] for v in range(VECTORS))
            answer[0, x], answer[1, x] = a, b
            grams = [grams[0] + a * a, grams[1] + a * b, grams[2] + b * b]
        return (*grams, carry[3] + packed[d])

    *grams, share_of = over(finish, (zero,) * 4)
    cells = (levels + 1) * width * sub * LANES
    one, mix, two = (
        (total(g) + jnp.sum(share_of[i : i + 1], axis=1, keepdims=True)) / cells
        for i, g in enumerate(grams)
    )
    scale_one = jnp.sqrt(one + EPSILON)
    cross = mix / scale_one
    rest = two - 2.0 * cross * cross + cross * cross * one / (one + EPSILON)
    scale_two = jnp.sqrt(rest + EPSILON)
    over_one, over_two = 1.0 / scale_one, 1.0 / scale_two

    def scale(k, carry):
        unit = tracer[0, k] * over_one
        tracer_out[0, k] = unit
        tracer_out[1, k] = (tracer[1, k] - cross * unit) * over_two
        return carry

    lax.fori_loop(0, levels, scale, 0, unroll=steps(levels, 10))
    for c in range(2):
        x = 2 * me + c
        unit = answer[0, x] * over_one
        surface_out[0, pl.ds(c, sub, stride=2), :] = unit
        surface_out[1, pl.ds(c, sub, stride=2), :] = (answer[1, x] - cross * unit) * over_two
    for i, value in enumerate((scale_one, cross, scale_two)):
        growth[i] = value[0, 0]


def tiled(array):
    *lead, columns, rows = array.shape
    split = array.reshape(*lead, columns, rows // LANES, LANES)
    return jnp.swapaxes(split, -3, -2).reshape(*lead, rows // LANES * columns, LANES)


def untiled(array, columns):
    *lead, high, lanes = array.shape
    split = array.reshape(*lead, high // columns, columns, lanes)
    return jnp.swapaxes(split, -3, -2).reshape(*lead, columns, high // columns * lanes)


def swap(array, mask):
    count = lax.axis_size("lon")
    return lax.ppermute(array, "lon", [(i, i ^ mask) for i in range(count)])


def chip_masks(count):
    lists, loads = ([], []), [0, 0]
    for mask in range(count // 2 - 1, 0, -1):
        core = int(loads[1] < loads[0])
        lists[core].append(mask)
        loads[core] += mask % 2 + mask // 2
    longest = max(map(len, lists))
    return list(zip(*([0] * (longest - len(one)) + one[::-1] for one in lists)))


def gather(block):
    count = lax.axis_size("lon")
    pair = jnp.stack([block, swap(block, 1)])
    fetched = []
    for masks in chip_masks(count):
        moves = [(i, i ^ (2 * masks[i % 2])) for i in range(count) if masks[i % 2]]
        fetched.append(lax.ppermute(pair, "lon", moves))
    fetched = jnp.stack(fetched)
    return pair, fetched, swap(fetched, 1)


def on_device(tracer_pert, surface_pert, zonal_flow, merid_flow, bottom_level):
    vectors, levels, columns, rows = tracer_pert.shape
    count = lax.axis_size("lon")
    sub = rows // LANES
    assert vectors == VECTORS and columns == 2 and rows % LANES == 0
    assert count >= 8 and count & (count - 1) == 0
    width = 2 * count
    f32 = jnp.float32
    vmem = pl.BlockSpec(memory_space=pltpu.VMEM)
    hbm = pl.BlockSpec(memory_space=pltpu.HBM)
    params = pltpu.CompilerParams(vmem_limit_bytes=24 * 2**20)

    def shaped(*shape):
        return jax.ShapeDtypeStruct((*shape, sub, LANES), f32)

    def held(*shape):
        return pltpu.VMEM((*shape, sub, LANES), f32)

    both = pltpu.VMEM((vectors, levels, sub * 2, LANES), f32)
    tracer_pert, zonal_flow, merid_flow = map(tiled, (tracer_pert, zonal_flow, merid_flow))
    outward = [(i, (i + 1) % count if i % 2 else (i - 1) % count) for i in range(count)]
    part = (levels + 1) // 2
    bottom = tiled(bottom_level)
    edge_rows = VECTORS * levels + part

    edge = pl.pallas_call(
        functools.partial(edge_kernel, levels, sub),
        out_shape=shaped(edge_rows),
        in_specs=[hbm] * 2,
        out_specs=hbm,
        scratch_shapes=[
            both,
            pltpu.VMEM((part, sub * 2, LANES), f32),
            held(edge_rows),
            pltpu.SemaphoreType.DMA((VECTORS + 1,)),
            pltpu.SemaphoreType.DMA((VECTORS + 1,)),
        ],
        compiler_params=pltpu.CompilerParams(vmem_limit_bytes=60 * 2**20),
        name="edge_columns",
    )(tracer_pert, zonal_flow)
    edge_far = lax.ppermute(edge, "lon", outward)
    flow_other = lax.ppermute(edge_far[VECTORS * levels :], "grp", [(0, 1), (1, 0)])
    cross, mate, raw, mate_raw, flow_in, mate_flow = pl.pallas_call(
        functools.partial(first_kernel, levels, sub),
        out_shape=(
            shaped(VECTORS * levels + 1),
            shaped(VECTORS * levels + 1),
            shaped(VECTORS * levels),
            shaped(VECTORS * levels),
            shaped(levels),
            shaped(levels),
        ),
        in_specs=[pl.BlockSpec(memory_space=pl.ANY)] + [vmem] * 4,
        out_specs=(vmem,) * 6,
        compiler_params=params,
        name="partial_step",
    )(edge, tracer_pert, zonal_flow, merid_flow, bottom)
    cross_far = lax.ppermute(cross, "lon", outward)
    mate_far, mate_raw_far, mate_flow_far = (swap(x, 1) for x in (mate, mate_raw, mate_flow))
    tracer, message = pl.pallas_call(
        functools.partial(second_kernel, levels, sub),
        out_shape=(
            jax.ShapeDtypeStruct((vectors, levels, sub * 2, LANES), f32),
            shaped(BLOCKS),
        ),
        in_specs=[vmem] * 15,
        out_specs=(vmem, vmem),
        scratch_shapes=[held(levels)],
        compiler_params=params,
        name="both_steps",
    )(
        raw, cross, mate, mate_raw, flow_in, mate_flow,
        edge_far, cross_far, mate_far, mate_raw_far, mate_flow_far, flow_other,
        merid_flow, tiled(surface_pert), bottom,
    )
    tracer_vec, surface_vec, growth = pl.pallas_call(
        functools.partial(third_kernel, levels, sub, count),
        out_shape=(
            jax.ShapeDtypeStruct((vectors, levels, sub * 2, LANES), f32),
            jax.ShapeDtypeStruct((vectors, sub * 2, LANES), f32),
            jax.ShapeDtypeStruct((3,), f32),
        ),
        in_specs=[vmem] * 4,
        out_specs=(vmem, vmem, pl.BlockSpec(memory_space=pltpu.SMEM)),
        scratch_shapes=[
            held(vectors, width + 2),
            *[held(vectors, width)] * 4,
            held(width),
            held(width + 1),
            held(width),
            held(width),
            held(count),
        ],
        compiler_params=pltpu.CompilerParams(vmem_limit_bytes=32 * 2**20),
        name="surface_and_scale",
    )(*gather(message), tracer)
    return (untiled(tracer_vec, 2), untiled(surface_vec, 2), growth)


def solution(mesh):
    placed = (
        P("grp", None, "lon", None),
        P("grp", "lon", None),
        P(None, "lon", None),
        P(None, "lon", None),
        P("lon", None),
    )
    return jax.shard_map(
        on_device,
        mesh=mesh,
        in_specs=placed,
        out_specs=(P("grp", None, "lon", None), P("grp", "lon", None), P("grp")),
        check_vma=False,
    )
```

```python
import functools

import jax
import jax.numpy as jnp
from jax import lax
from jax.experimental import pallas as pl
from jax.experimental.pallas import tpu as pltpu
from jax.sharding import PartitionSpec as P

ITERS = 3


DIFFUSIVITY = 0.5
TIME_STEP = 0.2
SURFACE_COUPLING = 0.5
STERIC_GAIN = 2.0
EPSILON = 1e-06

LANES = 128
VECTORS = 2
SLOPE = 0.25 * TIME_STEP
SPREAD = TIME_STEP * DIFFUSIVITY
DEPTHS = VECTORS * 2
RIM = DEPTHS + 2
GRAMS = RIM
BLOCKS = GRAMS + 1
POWERS = ITERS


def next_row(tile):
    turned = pltpu.roll(tile, LANES - 1, 1)
    carried = pltpu.roll(turned, tile.shape[0] - 1, 0)
    lane = lax.broadcasted_iota(jnp.int32, tile.shape, 1)
    return jnp.where(lane == LANES - 1, carried, turned)


def prior_row(tile):
    turned = pltpu.roll(tile, 1, 1)
    carried = pltpu.roll(turned, 1, 0)
    lane = lax.broadcasted_iota(jnp.int32, tile.shape, 1)
    return jnp.where(lane == 0, carried, turned)


def wall_depth(depth):
    subs, lane = (lax.broadcasted_iota(jnp.int32, depth.shape, axis) for axis in (0, 1))
    last = (subs == depth.shape[0] - 1) & (lane == LANES - 1)
    return jnp.where(last, jnp.zeros_like(depth), jnp.minimum(depth, next_row(depth)))


def face_pair(level, face_depth, flow_sum):
    slope = SLOPE * flow_sum
    open_face = level < face_depth
    return (
        jnp.where(open_face, slope + SPREAD, 0.0),
        jnp.where(open_face, slope - SPREAD, 0.0),
    )


def outflow(pair, near, far):
    return pair[0] * near + pair[1] * far


def side_pairs(level, depths, flow):
    return (
        face_pair(level, depths[0], flow + next_row(flow)),
        face_pair(level, depths[1], -(flow + prior_row(flow))),
    )


def divergence_y(pairs, tile):
    return outflow(pairs[0], tile, next_row(tile)) + outflow(pairs[1], tile, prior_row(tile))


def side_depths(depth):
    north = wall_depth(depth)
    return north, prior_row(north)


def orientation():
    outer = lax.rem(lax.axis_index("lon"), 2)
    return outer, 1 - outer, (2 * outer - 1).astype(jnp.float32)


def steps(count, most):
    return max(u for u in range(1, most + 1) if count % u == 0)


def share(levels):
    size = lax.axis_size("grp")
    assert size == 2
    part = (levels + 1) // 2
    return lax.axis_index("grp") * (levels - part), part


def pack_rim(sub, surface, bottom, target, base):
    for c in range(2):
        for v in range(VECTORS):
            target[base + v * 2 + c] = surface[v, pl.ds(c, sub, stride=2), :]
        target[base + DEPTHS + c] = bottom[pl.ds(c, sub, stride=2), :].astype(jnp.float32)


def edge_kernel(
    levels, sub, tracer_hbm, zonal_hbm, surface_hbm, bottom_hbm, edge_hbm,
    tracer, zonal, surface, bottom, edge, sems_in, sems_out,
):
    outer, _, _ = orientation()
    start, part = share(levels)

    def move(source, target, sem):
        copy = pltpu.make_async_copy(source, target, sem)
        copy.start()
        return copy

    arrivals = [
        move(tracer_hbm.at[v], tracer.at[v], sems_in.at[v]) for v in range(VECTORS)
    ] + [move(zonal_hbm.at[pl.ds(start, part)], zonal, sems_in.at[VECTORS])]
    small = [
        move(surface_hbm, surface, sems_in.at[VECTORS + 1]),
        move(bottom_hbm, bottom, sems_in.at[VECTORS + 2]),
    ]
    departures = []
    for v, arrival in enumerate(arrivals):
        number = part if v == VECTORS else levels
        arrival.wait()
        if v == VECTORS:
            for copy in small:
                copy.wait()
            pack_rim(sub, surface, bottom, edge, v * levels + number)

        def body(k, carry, v=v):
            source = zonal if v == VECTORS else tracer.at[v]
            edge[v * levels + k] = source[k, pl.ds(outer, sub, stride=2), :]
            return carry

        lax.fori_loop(0, number, body, 0, unroll=steps(number, 10))
        rows = pl.ds(v * levels, number + (RIM if v == VECTORS else 0))
        departures.append(move(edge.at[rows], edge_hbm.at[rows], sems_out.at[v]))
    for departure in departures:
        departure.wait()


def first_kernel(
    levels, sub, edge, tracer, zonal, merid, surface, bottom,
    cross, mate, raw, mate_raw, flow_in, mate_flow,
):
    del edge
    outer, inner, sign = orientation()

    def column(ref, where, *lead):
        return ref[(*lead, pl.ds(where, sub, stride=2), slice(None))]

    depth = [column(bottom, where).astype(jnp.float32) for where in (outer, inner)]
    between = jnp.minimum(*depth)
    along = [side_depths(d) for d in depth]
    cross[VECTORS * levels] = depth[0]
    mate[VECTORS * levels] = depth[1]
    pack_rim(sub, surface, bottom, mate_flow, levels)

    def body(k, carry):
        level = k.astype(jnp.float32)
        flow = [column(zonal, where, k) for where in (outer, inner)]
        turn = [column(merid, where, k) for where in (outer, inner)]
        middle = face_pair(level, between, -sign * (flow[0] + flow[1]))
        sides = [side_pairs(level, along[c], turn[c]) for c in range(2)]
        for v in range(VECTORS):
            cells = [column(tracer, where, v, k) for where in (outer, inner)]
            flux = outflow(middle, *cells)
            kept = [
                jnp.where(level < depth[c], cells[c], 0.0) - divergence_y(sides[c], cells[c])
                for c in range(2)
            ]
            cross[v * levels + k] = kept[0] - flux
            raw[v * levels + k] = cells[0]
            mate[v * levels + k] = kept[1] + flux
            mate_raw[v * levels + k] = cells[1]
        flow_in[k] = flow[0]
        mate_flow[k] = flow[1]
        return carry

    lax.fori_loop(0, levels, body, 0, unroll=steps(levels, 10))


def wrap(pole, width):
    for v in range(VECTORS):
        pole[v, 0] = pole[v, width]
        pole[v, width + 1] = pole[v, 1]


def spread(pole, face_x, face_y, face_z, v, x):
    west, centre, east = (pole[v, x + j] for j in range(3))
    return (face_x[x + 1] * (east - centre) - face_x[x] * (centre - west)) + (
        face_y[x] * (next_row(centre) - centre) - face_z[x] * (centre - prior_row(centre))
    )


def second_kernel(
    levels, sub, raw, cross, mate, mate_raw, flow_in, mate_flow,
    raw_far, cross_far, mate_far, mate_raw_far, mate_flow_far, flow_other,
    merid, tracer, message, flow_far, powers,
):
    outer, inner, sign = orientation()
    start, part = share(levels)
    last = VECTORS * levels

    def unpack(i, carry):
        flow_far[start + i] = raw_far[VECTORS * levels + i]
        flow_far[levels - part - start + i] = flow_other[i]
        return carry

    lax.fori_loop(0, part, unpack, 0, unroll=steps(part, 10))
    powers_of_heights(levels, part, mate_flow, mate_flow_far, raw_far, powers)
    near = [(raw, cross), (mate_raw, mate)]
    far = [(raw_far, cross_far), (mate_raw_far, mate_far)]
    depth = [cross[last], mate[last]]
    beside = [jnp.minimum(depth[0], cross_far[last]), jnp.minimum(depth[1], mate_far[last])]
    between = jnp.minimum(*depth)
    along = [side_depths(d) for d in depth]
    zero = jnp.zeros_like(between)

    def body(k, carry):
        level = k.astype(jnp.float32)
        flow = [flow_in[k], mate_flow[k]]
        beyond = [flow_far[k], mate_flow_far[k]]
        turn = [merid[k, pl.ds(where, sub, stride=2), :] for where in (outer, inner)]
        middle = face_pair(level, between, -sign * (flow[0] + flow[1]))
        edges = [
            face_pair(level, beside[c], (sign, -sign)[c] * (flow[c] + beyond[c])) for c in range(2)
        ]
        sides = [side_pairs(level, along[c], turn[c]) for c in range(2)]
        totals, grams = list(carry[:4]), list(carry[4:])
        done = []
        for v in range(VECTORS):
            own, other = [], []
            for c in range(2):
                (first, kept), (first_far, kept_far) = near[c], far[c]
                row = v * levels + k
                flux = outflow(edges[c], first[row], first_far[row])
                own.append(kept[row] - flux)
                other.append(kept_far[row] + flux)
            crossing = outflow(middle, *own)
            fresh = []
            for c, where in enumerate((outer, inner)):
                gone = crossing if c == 0 else -crossing
                value = (
                    own[c]
                    - outflow(edges[c], own[c], other[c])
                    - gone
                    - divergence_y(sides[c], own[c])
                )
                tracer[v, k, pl.ds(where, sub, stride=2), :] = value
                totals[v * 2 + c] = totals[v * 2 + c] + value
                fresh.append(value)
            done.append(fresh)
        for c in range(2):
            a, b = done[0][c], done[1][c]
            grams = [grams[0] + a * a, grams[1] + a * b, grams[2] + b * b]
        return (*totals, *grams)

    sums = lax.fori_loop(0, levels, body, (zero,) * 7, unroll=steps(levels, 10))
    gain = STERIC_GAIN / levels
    rows = list(sums[4:])
    residual = []
    for v in range(VECTORS):
        residual.append([gain * sums[v * 2 + c] + powers[POWERS, v, c] for c in range(2)])
        for c, where in enumerate((outer, inner)):
            message[v * 2 + where] = residual[v][c]

    def product(one, two):
        return one[0] * two[0] + one[1] * two[1]

    heights = [[powers[0, v, c] for c in range(2)] for v in range(VECTORS)]
    for n, (i, j) in enumerate(((0, 0), (0, 1), (1, 1))):
        rows[n] = rows[n] + product(heights[i], heights[j])
    for i in range(VECTORS):
        for j in range(VECTORS):
            for m in range(POWERS):
                rows.append(product([powers[m, i, c] for c in range(2)], residual[j]))
    message[GRAMS] = pack_rows(rows)
    for c in range(2):
        message[DEPTHS + c] = mate_flow[levels + DEPTHS + c]


def pack_rows(tiles):
    shape = tiles[0].shape
    sub, lane = (lax.broadcasted_iota(jnp.int32, shape, axis) for axis in (0, 1))
    half = shape[1] // 2
    packed = jnp.zeros(shape, jnp.float32)
    for n, tile in enumerate(tiles):
        row = jnp.sum(tile, axis=0, keepdims=True)
        row = row + pltpu.roll(row, half, 1)
        place = (sub == n % shape[0]) & ((lane < half) == (n < shape[0]))
        packed = jnp.where(place, row, packed)
    return packed


def unpack_rows(packed, count):
    lane = lax.broadcasted_iota(jnp.int32, packed.shape, 1)
    low = lane < packed.shape[1] // 2
    sums = [
        jnp.sum(jnp.where(side, packed, 0.0), axis=1, keepdims=True)
        for side in (low, jnp.logical_not(low))
    ]
    size = packed.shape[0]
    return [sums[n // size][n % size : n % size + 1] for n in range(count)]


def powers_of_heights(levels, part, mate_flow, mate_flow_far, raw_far, powers):
    outer, inner, _ = orientation()
    cross_base = VECTORS * levels + part
    line = [
        (mate_flow_far, levels, inner),
        (mate_flow_far, levels, outer),
        (mate_flow, levels, inner),
        (mate_flow, levels, outer),
        (raw_far, cross_base, inner),
        (raw_far, cross_base, outer),
    ]
    depth = [ref[base + DEPTHS + where] for ref, base, where in line]
    faces = [SURFACE_COUPLING * jnp.minimum(a, b) for a, b in zip(depth, depth[1:])]
    sides = [side_depths(SURFACE_COUPLING * d) for d in depth[1:5]]
    for v in range(VECTORS):
        field = [
            jnp.where(d > 0, ref[base + v * 2 + where], 0.0)
            for d, (ref, base, where) in zip(depth, line)
        ]

        def bend(field, first, last):
            found = []
            for j in range(first, last):
                west, centre, east = field[j - 1 : j + 2]
                north, south = sides[j - 1]
                found.append(
                    (faces[j] * (east - centre) - faces[j - 1] * (centre - west))
                    + (north * (next_row(centre) - centre) - south * (centre - prior_row(centre)))
                )
            return found

        lap = bend(field, 1, 5)
        image = [None] + [h - p for h, p in zip(field[1:5], lap)]
        again = [p - q for p, q in zip(image[2:4], bend(image, 2, 4))]
        for c, where in enumerate((3, 2)):
            powers[0, v, c] = field[where]
            powers[1, v, c] = image[where]
            powers[2, v, c] = again[where - 2]
            powers[POWERS, v, c] = lap[where - 1]


def total(tile):
    return jnp.sum(jnp.sum(tile, axis=0, keepdims=True), axis=1, keepdims=True)


def combine(one, factor, two):
    longest = max(len(one), len(two))
    one, two = (list(c) + [0.0] * (longest - len(c)) for c in (one, two))
    return [a + factor * b for a, b in zip(one, two)]


def third_kernel(
    levels, sub, count, pair, fetched, fetched_mate, surface, tracer, tracer_out, surface_out, growth,
    pole, residual, answer, image, depth, face_x, face_y, face_z, packed,
):
    width = 2 * count
    me = lax.axis_index("lon")
    core = lax.rem(me, 2)
    zero = jnp.zeros((sub, LANES), jnp.float32)
    none = (zero,) * VECTORS

    def place(owner, block):
        packed[owner] = block(GRAMS)
        for c in range(2):
            x = 2 * owner + c
            depth[x] = block(DEPTHS + c)
            for v in range(VECTORS):
                value = block(v * 2 + c)
                residual[v, x] = value
                pole[v, x + 1] = value

    for slot in range(2):
        place(me ^ slot, lambda row, slot=slot: pair[slot, row])
    for ref, flip in ((fetched, 0), (fetched_mate, 1)):
        for j, masks in enumerate(chip_masks(count)):
            mask = jnp.where((core ^ flip) == 0, *masks)
            for slot in range(2):
                owner = me ^ flip ^ slot ^ (2 * mask)

                def put(owner=owner, ref=ref, j=j, slot=slot):
                    place(owner, lambda row: ref[j, slot, row])

                if all(masks):
                    put()
                else:
                    pl.when(mask > 0)(put)

    def over(body, init):
        return lax.fori_loop(0, count, body, init, unroll=steps(count, 16))

    def each(d):
        return [(v, c, 2 * d + c) for v in range(VECTORS) for c in range(2)]

    def prepare(d, carry):
        for x in (2 * d, 2 * d + 1):
            here, after = depth[x], depth[lax.rem(x + 1, width)]
            face_x[x + 1] = SURFACE_COUPLING * jnp.minimum(here, after)
            north, south = side_depths(here)
            face_y[x] = SURFACE_COUPLING * north
            face_z[x] = SURFACE_COUPLING * south
        return carry

    over(prepare, 0)
    face_x[0] = face_x[width]
    wrap(pole, width)

    def start(d, carry):
        sums = list(carry)
        for v, _, x in each(d):
            sums[v] = sums[v] + residual[v, x] * residual[v, x]
        return tuple(sums)

    norm = [total(t) for t in over(start, none)]
    share, left, aim = ([[v for _ in range(VECTORS)] for v in ([], [1.0], [1.0])])

    def apply(d, carry):
        sums = list(carry)
        for v, _, x in each(d):
            centre = pole[v, x + 1]
            value = centre - spread(pole, face_x, face_y, face_z, v, x)
            image[v, x] = value
            sums[v] = sums[v] + centre * value
        return tuple(sums)

    for iteration in range(ITERS):
        energy = [total(t) for t in over(apply, none)]
        size = [n / e for n, e in zip(norm, energy)]
        share = [combine(s, z, a) for s, z, a in zip(share, size, aim)]
        if iteration + 1 < ITERS:

            def advance(d, carry, size=size, first=iteration == 0):
                sums = list(carry)
                for v, _, x in each(d):
                    gone = size[v] * pole[v, x + 1]
                    answer[v, x] = gone if first else answer[v, x] + gone
                    value = residual[v, x] - size[v] * image[v, x]
                    residual[v, x] = value
                    sums[v] = sums[v] + value * value
                return tuple(sums)

            fresh = [total(t) for t in over(advance, none)]
            ratio = [f / n for f, n in zip(fresh, norm)]
            left = [combine(l, -z, [0.0] + a) for l, z, a in zip(left, size, aim)]
            aim = [combine(l, q, a) for l, q, a in zip(left, ratio, aim)]

            def turn(d, carry, ratio=ratio):
                for v, _, x in each(d):
                    pole[v, x + 1] = residual[v, x] + ratio[v] * pole[v, x + 1]
                return carry

            over(turn, 0)
            wrap(pole, width)
            norm = fresh

    def finish(d, carry):
        grams = list(carry)
        for x in (2 * d, 2 * d + 1):
            a, b = (answer[v, x] + size[v] * pole[v, x + 1] for v in range(VECTORS))
            answer[0, x], answer[1, x] = a, b
            grams = [grams[0] + a * a, grams[1] + a * b, grams[2] + b * b]
        return (*grams, carry[3] + packed[d])

    *grams, packed_sums = over(finish, (zero,) * 4)
    sums = unpack_rows(packed_sums, 3 + VECTORS * VECTORS * POWERS)

    def heights_with(i, j):
        first = 3 + (i * VECTORS + j) * POWERS
        return sum(c * t for c, t in zip(share[j], sums[first : first + POWERS]))

    cells = (levels + 1) * width * sub * LANES
    one, mix, two = (
        (sums[n] + total(grams[n]) + (heights_with(i, j) + heights_with(j, i))) / cells
        for n, (i, j) in enumerate(((0, 0), (0, 1), (1, 1)))
    )
    scale_one = jnp.sqrt(one + EPSILON)
    cross = mix / scale_one
    rest = two - 2.0 * cross * cross + cross * cross * one / (one + EPSILON)
    scale_two = jnp.sqrt(rest + EPSILON)
    over_one, over_two = 1.0 / scale_one, 1.0 / scale_two

    def scale(k, carry):
        unit = tracer[0, k] * over_one
        tracer_out[0, k] = unit
        tracer_out[1, k] = (tracer[1, k] - cross * unit) * over_two
        return carry

    lax.fori_loop(0, levels, scale, 0, unroll=steps(levels, 10))
    for c in range(2):
        x = 2 * me + c
        first, second = (
            jnp.where(depth[x] > 0, surface[v, pl.ds(c, sub, stride=2), :], 0.0) + answer[v, x]
            for v in range(VECTORS)
        )
        unit = first * over_one
        surface_out[0, pl.ds(c, sub, stride=2), :] = unit
        surface_out[1, pl.ds(c, sub, stride=2), :] = (second - cross * unit) * over_two
    for i, value in enumerate((scale_one, cross, scale_two)):
        growth[i] = value[0, 0]


def tiled(array):
    *lead, columns, rows = array.shape
    split = array.reshape(*lead, columns, rows // LANES, LANES)
    return jnp.swapaxes(split, -3, -2).reshape(*lead, rows // LANES * columns, LANES)


def untiled(array, columns):
    *lead, high, lanes = array.shape
    split = array.reshape(*lead, high // columns, columns, lanes)
    return jnp.swapaxes(split, -3, -2).reshape(*lead, columns, high // columns * lanes)


def swap(array, mask):
    count = lax.axis_size("lon")
    return lax.ppermute(array, "lon", [(i, i ^ mask) for i in range(count)])


def chip_masks(count):
    lists, loads = ([], []), [0, 0]
    for mask in range(count // 2 - 1, 0, -1):
        core = int(loads[1] < loads[0])
        lists[core].append(mask)
        loads[core] += mask % 2 + mask // 2
    longest = max(map(len, lists))
    return list(zip(*([0] * (longest - len(one)) + one[::-1] for one in lists)))


def gather(block):
    count = lax.axis_size("lon")
    pair = jnp.stack([block, swap(block, 1)])
    fetched = []
    for masks in chip_masks(count):
        moves = [(i, i ^ (2 * masks[i % 2])) for i in range(count) if masks[i % 2]]
        fetched.append(lax.ppermute(pair, "lon", moves))
    fetched = jnp.stack(fetched)
    return pair, fetched, swap(fetched, 1)


def on_device(tracer_pert, surface_pert, zonal_flow, merid_flow, bottom_level):
    vectors, levels, columns, rows = tracer_pert.shape
    count = lax.axis_size("lon")
    sub = rows // LANES
    assert vectors == VECTORS and columns == 2 and rows % LANES == 0
    assert count >= 8 and count & (count - 1) == 0
    width = 2 * count
    f32 = jnp.float32
    vmem = pl.BlockSpec(memory_space=pltpu.VMEM)
    hbm = pl.BlockSpec(memory_space=pltpu.HBM)
    params = pltpu.CompilerParams(vmem_limit_bytes=24 * 2**20)

    def shaped(*shape):
        return jax.ShapeDtypeStruct((*shape, sub, LANES), f32)

    def held(*shape):
        return pltpu.VMEM((*shape, sub, LANES), f32)

    both = pltpu.VMEM((vectors, levels, sub * 2, LANES), f32)
    tracer_pert, zonal_flow, merid_flow = map(tiled, (tracer_pert, zonal_flow, merid_flow))
    outward = [(i, (i + 1) % count if i % 2 else (i - 1) % count) for i in range(count)]
    part = (levels + 1) // 2
    surface, bottom = tiled(surface_pert), tiled(bottom_level)
    edge_rows = VECTORS * levels + part + RIM

    edge = pl.pallas_call(
        functools.partial(edge_kernel, levels, sub),
        out_shape=shaped(edge_rows),
        in_specs=[hbm] * 4,
        out_specs=hbm,
        scratch_shapes=[
            both,
            pltpu.VMEM((part, sub * 2, LANES), f32),
            pltpu.VMEM((vectors, sub * 2, LANES), f32),
            pltpu.VMEM((sub * 2, LANES), jnp.int32),
            held(edge_rows),
            pltpu.SemaphoreType.DMA((VECTORS + 3,)),
            pltpu.SemaphoreType.DMA((VECTORS + 1,)),
        ],
        compiler_params=pltpu.CompilerParams(vmem_limit_bytes=60 * 2**20),
        name="edge_columns",
    )(tracer_pert, zonal_flow, surface, bottom)
    edge_far = lax.ppermute(edge, "lon", outward)
    flow_other = lax.ppermute(edge_far[VECTORS * levels : edge_rows - RIM], "grp", [(0, 1), (1, 0)])
    cross, mate, raw, mate_raw, flow_in, mate_flow = pl.pallas_call(
        functools.partial(first_kernel, levels, sub),
        out_shape=(
            shaped(VECTORS * levels + 1),
            shaped(VECTORS * levels + 1),
            shaped(VECTORS * levels),
            shaped(VECTORS * levels),
            shaped(levels),
            shaped(levels + RIM),
        ),
        in_specs=[pl.BlockSpec(memory_space=pl.ANY)] + [vmem] * 5,
        out_specs=(vmem,) * 6,
        compiler_params=params,
        name="partial_step",
    )(edge, tracer_pert, zonal_flow, merid_flow, surface, bottom)
    cross_far = lax.ppermute(cross, "lon", outward)
    mate_far, mate_raw_far, mate_flow_far = (swap(x, 1) for x in (mate, mate_raw, mate_flow))
    tracer, message = pl.pallas_call(
        functools.partial(second_kernel, levels, sub),
        out_shape=(
            jax.ShapeDtypeStruct((vectors, levels, sub * 2, LANES), f32),
            shaped(BLOCKS),
        ),
        in_specs=[vmem] * 13,
        out_specs=(vmem, vmem),
        scratch_shapes=[held(levels), held(POWERS + 1, vectors, 2)],
        compiler_params=params,
        name="both_steps",
    )(
        raw, cross, mate, mate_raw, flow_in, mate_flow,
        edge_far, cross_far, mate_far, mate_raw_far, mate_flow_far, flow_other,
        merid_flow,
    )
    tracer_vec, surface_vec, growth = pl.pallas_call(
        functools.partial(third_kernel, levels, sub, count),
        out_shape=(
            jax.ShapeDtypeStruct((vectors, levels, sub * 2, LANES), f32),
            jax.ShapeDtypeStruct((vectors, sub * 2, LANES), f32),
            jax.ShapeDtypeStruct((3,), f32),
        ),
        in_specs=[vmem] * 5,
        out_specs=(vmem, vmem, pl.BlockSpec(memory_space=pltpu.SMEM)),
        scratch_shapes=[
            held(vectors, width + 2),
            *[held(vectors, width)] * 3,
            held(width),
            held(width + 1),
            held(width),
            held(width),
            held(count),
        ],
        compiler_params=pltpu.CompilerParams(vmem_limit_bytes=32 * 2**20),
        name="surface_and_scale",
    )(*gather(message), surface, tracer)
    return (untiled(tracer_vec, 2), untiled(surface_vec, 2), growth)


def solution(mesh):
    placed = (
        P("grp", None, "lon", None),
        P("grp", "lon", None),
        P(None, "lon", None),
        P(None, "lon", None),
        P("lon", None),
    )
    return jax.shard_map(
        on_device,
        mesh=mesh,
        in_specs=placed,
        out_specs=(P("grp", None, "lon", None), P("grp", "lon", None), P("grp")),
        check_vma=False,
    )
```

```python
import functools

import jax
import jax.numpy as jnp
from jax import lax
from jax.experimental import pallas as pl
from jax.experimental.pallas import tpu as pltpu
from jax.sharding import PartitionSpec as P

ITERS = 3


DIFFUSIVITY = 0.5
TIME_STEP = 0.2
SURFACE_COUPLING = 0.5
STERIC_GAIN = 2.0
EPSILON = 1e-06

LANES = 128
VECTORS = 2
SLOPE = 0.25 * TIME_STEP
SPREAD = TIME_STEP * DIFFUSIVITY
DEPTHS = VECTORS * 2
RIM = DEPTHS + 2
GRAMS = RIM
BLOCKS = GRAMS + 1
POWERS = ITERS


def next_row(tile):
    turned = pltpu.roll(tile, LANES - 1, 1)
    carried = pltpu.roll(turned, tile.shape[0] - 1, 0)
    lane = lax.broadcasted_iota(jnp.int32, tile.shape, 1)
    return jnp.where(lane == LANES - 1, carried, turned)


def prior_row(tile):
    turned = pltpu.roll(tile, 1, 1)
    carried = pltpu.roll(turned, 1, 0)
    lane = lax.broadcasted_iota(jnp.int32, tile.shape, 1)
    return jnp.where(lane == 0, carried, turned)


def wall_depth(depth):
    subs, lane = (lax.broadcasted_iota(jnp.int32, depth.shape, axis) for axis in (0, 1))
    last = (subs == depth.shape[0] - 1) & (lane == LANES - 1)
    return jnp.where(last, jnp.zeros_like(depth), jnp.minimum(depth, next_row(depth)))


def face_pair(level, face_depth, flow_sum):
    slope = SLOPE * flow_sum
    open_face = level < face_depth
    return (
        jnp.where(open_face, slope + SPREAD, 0.0),
        jnp.where(open_face, slope - SPREAD, 0.0),
    )


def outflow(pair, near, far):
    return pair[0] * near + pair[1] * far


def side_pairs(level, depths, flow):
    return (
        face_pair(level, depths[0], flow + next_row(flow)),
        face_pair(level, depths[1], -(flow + prior_row(flow))),
    )


def divergence_y(pairs, tile):
    return outflow(pairs[0], tile, next_row(tile)) + outflow(pairs[1], tile, prior_row(tile))


def side_depths(depth):
    north = wall_depth(depth)
    return north, prior_row(north)


def orientation():
    outer = lax.rem(lax.axis_index("lon"), 2)
    return outer, 1 - outer, (2 * outer - 1).astype(jnp.float32)


def steps(count, most):
    return max(u for u in range(1, most + 1) if count % u == 0)


def share(levels):
    assert lax.axis_size("grp") == 2 and levels % 2 == 0
    part = levels // 2
    return lax.axis_index("grp") * (levels - part), part


def pack_rim(sub, surface, bottom, target, base):
    for c in range(2):
        for v in range(VECTORS):
            target[base + v * 2 + c] = surface[v, pl.ds(c, sub, stride=2), :]
        target[base + DEPTHS + c] = bottom[pl.ds(c, sub, stride=2), :].astype(jnp.float32)


def edge_kernel(
    levels, sub, tracer_hbm, zonal_hbm, surface_hbm, bottom_hbm, edge_hbm,
    tracer, zonal, surface, bottom, edge, sems_in, sems_out,
):
    outer, _, _ = orientation()
    start, part = share(levels)

    def move(source, target, sem):
        copy = pltpu.make_async_copy(source, target, sem)
        copy.start()
        return copy

    arrivals = [
        move(tracer_hbm.at[v], tracer.at[v], sems_in.at[v]) for v in range(VECTORS)
    ] + [move(zonal_hbm.at[pl.ds(start, part)], zonal, sems_in.at[VECTORS])]
    small = [
        move(surface_hbm, surface, sems_in.at[VECTORS + 1]),
        move(bottom_hbm, bottom, sems_in.at[VECTORS + 2]),
    ]
    departures = []
    for v, arrival in enumerate(arrivals):
        number = part if v == VECTORS else levels
        arrival.wait()
        if v == VECTORS:
            for copy in small:
                copy.wait()
            pack_rim(sub, surface, bottom, edge, v * levels + number)

        def body(k, carry, v=v):
            source = zonal if v == VECTORS else tracer.at[v]
            edge[v * levels + k] = source[k, pl.ds(outer, sub, stride=2), :]
            return carry

        lax.fori_loop(0, number, body, 0, unroll=steps(number, 10))
        rows = pl.ds(v * levels, number + (RIM if v == VECTORS else 0))
        departures.append(move(edge.at[rows], edge_hbm.at[rows], sems_out.at[v]))
    for departure in departures:
        departure.wait()


def first_kernel(
    levels, sub, edge, tracer, zonal, merid, surface, bottom,
    cross, mate, raw, mate_raw, flow_in, mate_flow,
):
    del edge
    outer, inner, sign = orientation()

    def column(ref, where, *lead):
        return ref[(*lead, pl.ds(where, sub, stride=2), slice(None))]

    depth = [column(bottom, where).astype(jnp.float32) for where in (outer, inner)]
    between = jnp.minimum(*depth)
    along = [side_depths(d) for d in depth]
    pack_rim(sub, surface, bottom, mate_flow, levels)

    def body(k, carry):
        level = k.astype(jnp.float32)
        flow = [column(zonal, where, k) for where in (outer, inner)]
        turn = [column(merid, where, k) for where in (outer, inner)]
        middle = face_pair(level, between, -sign * (flow[0] + flow[1]))
        sides = [side_pairs(level, along[c], turn[c]) for c in range(2)]
        for v in range(VECTORS):
            cells = [column(tracer, where, v, k) for where in (outer, inner)]
            flux = outflow(middle, *cells)
            kept = [
                jnp.where(level < depth[c], cells[c], 0.0) - divergence_y(sides[c], cells[c])
                for c in range(2)
            ]
            cross[v * levels + k] = kept[0] - flux
            raw[v * levels + k] = cells[0]
            mate[v * levels + k] = kept[1] + flux
            mate_raw[v * levels + k] = cells[1]
        flow_in[k] = flow[0]
        mate_flow[k] = flow[1]
        return carry

    lax.fori_loop(0, levels, body, 0, unroll=steps(levels, 10))


def wrap(pole, width):
    for v in range(VECTORS):
        pole[v, 0] = pole[v, width]
        pole[v, width + 1] = pole[v, 1]


def spread(pole, face_x, face_y, face_z, v, x):
    west, centre, east = (pole[v, x + j] for j in range(3))
    return (face_x[x + 1] * (east - centre) - face_x[x] * (centre - west)) + (
        face_y[x] * (next_row(centre) - centre) - face_z[x] * (centre - prior_row(centre))
    )


def halo_kernel(
    levels, sub, own, raw, cross, mate, mate_raw, flow_in, mate_flow,
    raw_far, mate_far, mate_raw_far, mate_flow_far, merid, *refs,
):
    outer, inner, sign = orientation()
    start, part = share(levels)
    first = start if own else levels - part - start
    if own:
        done, base, weight, sums, powers = refs
        powers_of_heights(levels, part, mate_flow, mate_flow_far, raw_far, powers)
        flow_far = raw_far.at[pl.ds(VECTORS * levels, part)]
    else:
        flow_far, done, base, weight, sums = refs
    near, far = (raw, mate_raw), (raw_far, mate_raw_far)
    rim = levels + DEPTHS
    depth = [mate_flow[rim + where] for where in (outer, inner)]
    beside = [
        jnp.minimum(depth[0], raw_far[VECTORS * levels + part + DEPTHS + inner]),
        jnp.minimum(depth[1], mate_flow_far[rim + outer]),
    ]
    between = jnp.minimum(*depth)
    along = [side_depths(d) for d in depth]
    zero = jnp.zeros_like(between)

    def body(i, carry):
        k = first + i
        level = k.astype(jnp.float32)
        flow = [flow_in[k], mate_flow[k]]
        beyond = [flow_far[i], mate_flow_far[k]]
        turn = [merid[k, pl.ds(where, sub, stride=2), :] for where in (outer, inner)]
        middle = face_pair(level, between, -sign * (flow[0] + flow[1]))
        edges = [
            face_pair(level, beside[c], (sign, -sign)[c] * (flow[c] + beyond[c])) for c in range(2)
        ]
        sides = [side_pairs(level, along[c], turn[c]) for c in range(2)]
        weight[i] = edges[0][1]
        totals, grams = list(carry[:VECTORS]), list(carry[VECTORS:])
        fresh = []
        for v in range(VECTORS):
            row = v * levels + k
            flux = [outflow(edges[c], near[c][row], far[c][row]) for c in range(2)]
            outside, inside = cross[row] - flux[0], mate[row] - flux[1]
            other = mate_far[row] + flux[1]
            crossing = outflow(middle, outside, inside)
            base[v, i] = (
                outside
                - outflow(edges[0], outside, flux[0])
                - crossing
                - divergence_y(sides[0], outside)
            )
            value = (
                inside - outflow(edges[1], inside, other) + crossing - divergence_y(sides[1], inside)
            )
            done[v, i] = value
            totals[v] = totals[v] + value
            fresh.append(value)
        return (*totals, *add_products(grams, *fresh))

    found = lax.fori_loop(0, part, body, (zero,) * (VECTORS + 3), unroll=steps(part, 10))
    for row, tile in enumerate(found):
        sums[row] = tile


def add_products(grams, a, b):
    return [grams[0] + a * a, grams[1] + a * b, grams[2] + b * b]


def second_kernel(
    levels, sub, cross_far, *refs,
):
    outer, inner, _ = orientation()
    start, part = share(levels)
    parts = refs[:3], refs[3:6]
    powers, mate_flow, column, message = refs[6:]
    zero = jnp.zeros(powers.shape[-2:], jnp.float32)
    carry = (zero,) * (VECTORS + 3)
    for first, (base, weight, _) in zip((start, levels - part - start), parts):

        def body(i, carry, first=first, base=base, weight=weight):
            totals, fresh = [], []
            for v in range(VECTORS):
                value = base[v, i] - weight[i] * cross_far[v * levels + first + i]
                column[v, first + i] = value
                totals.append(carry[v] + value)
                fresh.append(value)
            return (*totals, *add_products(carry[VECTORS:], *fresh))

        carry = lax.fori_loop(0, part, body, carry, unroll=steps(part, 10))
    inside = [parts[0][2][row] + parts[1][2][row] for row in range(VECTORS + 3)]
    gain = STERIC_GAIN / levels
    rows = [a + b for a, b in zip(carry[VECTORS:], inside[VECTORS:])]
    residual = []
    for v in range(VECTORS):
        residual.append(
            [gain * total_of + powers[POWERS, v, c] for c, total_of in enumerate((carry[v], inside[v]))]
        )
        for c, where in enumerate((outer, inner)):
            message[v * 2 + where] = residual[v][c]

    def product(one, two):
        return one[0] * two[0] + one[1] * two[1]

    heights = [[powers[0, v, c] for c in range(2)] for v in range(VECTORS)]
    for n, (i, j) in enumerate(((0, 0), (0, 1), (1, 1))):
        rows[n] = rows[n] + product(heights[i], heights[j])
    for i in range(VECTORS):
        for j in range(VECTORS):
            for m in range(POWERS):
                rows.append(product([powers[m, i, c] for c in range(2)], residual[j]))
    message[GRAMS] = pack_rows(rows)
    for c in range(2):
        message[DEPTHS + c] = mate_flow[levels + DEPTHS + c]


def pack_rows(tiles):
    shape = tiles[0].shape
    sub, lane = (lax.broadcasted_iota(jnp.int32, shape, axis) for axis in (0, 1))
    half = shape[1] // 2
    packed = jnp.zeros(shape, jnp.float32)
    for n, tile in enumerate(tiles):
        row = jnp.sum(tile, axis=0, keepdims=True)
        row = row + pltpu.roll(row, half, 1)
        place = (sub == n % shape[0]) & ((lane < half) == (n < shape[0]))
        packed = jnp.where(place, row, packed)
    return packed


def unpack_rows(packed, count):
    lane = lax.broadcasted_iota(jnp.int32, packed.shape, 1)
    low = lane < packed.shape[1] // 2
    sums = [
        jnp.sum(jnp.where(side, packed, 0.0), axis=1, keepdims=True)
        for side in (low, jnp.logical_not(low))
    ]
    size = packed.shape[0]
    return [sums[n // size][n % size : n % size + 1] for n in range(count)]


def powers_of_heights(levels, part, mate_flow, mate_flow_far, raw_far, powers):
    outer, inner, _ = orientation()
    cross_base = VECTORS * levels + part
    line = [
        (mate_flow_far, levels, inner),
        (mate_flow_far, levels, outer),
        (mate_flow, levels, inner),
        (mate_flow, levels, outer),
        (raw_far, cross_base, inner),
        (raw_far, cross_base, outer),
    ]
    depth = [ref[base + DEPTHS + where] for ref, base, where in line]
    faces = [SURFACE_COUPLING * jnp.minimum(a, b) for a, b in zip(depth, depth[1:])]
    sides = [side_depths(SURFACE_COUPLING * d) for d in depth[1:5]]
    for v in range(VECTORS):
        field = [
            jnp.where(d > 0, ref[base + v * 2 + where], 0.0)
            for d, (ref, base, where) in zip(depth, line)
        ]

        def bend(field, first, last):
            found = []
            for j in range(first, last):
                west, centre, east = field[j - 1 : j + 2]
                north, south = sides[j - 1]
                found.append(
                    (faces[j] * (east - centre) - faces[j - 1] * (centre - west))
                    + (north * (next_row(centre) - centre) - south * (centre - prior_row(centre)))
                )
            return found

        lap = bend(field, 1, 5)
        image = [None] + [h - p for h, p in zip(field[1:5], lap)]
        again = [p - q for p, q in zip(image[2:4], bend(image, 2, 4))]
        for c, where in enumerate((3, 2)):
            powers[0, v, c] = field[where]
            powers[1, v, c] = image[where]
            powers[2, v, c] = again[where - 2]
            powers[POWERS, v, c] = lap[where - 1]


def total(tile):
    return jnp.sum(jnp.sum(tile, axis=0, keepdims=True), axis=1, keepdims=True)


def combine(one, factor, two):
    longest = max(len(one), len(two))
    one, two = (list(c) + [0.0] * (longest - len(c)) for c in (one, two))
    return [a + factor * b for a, b in zip(one, two)]


def third_kernel(
    levels, sub, count, pair, fetched, fetched_mate, surface, column, done, done_other,
    tracer_hbm, surface_out, growth, tracer, sems, pole, residual, answer, image, depth, face_x, face_y, face_z, packed,
):
    width = 2 * count
    me = lax.axis_index("lon")
    core = lax.rem(me, 2)
    zero = jnp.zeros((sub, LANES), jnp.float32)
    none = (zero,) * VECTORS

    def place(owner, block):
        packed[owner] = block(GRAMS)
        for c in range(2):
            x = 2 * owner + c
            depth[x] = block(DEPTHS + c)
            for v in range(VECTORS):
                value = block(v * 2 + c)
                residual[v, x] = value
                pole[v, x + 1] = value

    for slot in range(2):
        place(me ^ slot, lambda row, slot=slot: pair[slot, row])
    for ref, flip in ((fetched, 0), (fetched_mate, 1)):
        for j, masks in enumerate(chip_masks(count)):
            mask = jnp.where((core ^ flip) == 0, *masks)
            for slot in range(2):
                owner = me ^ flip ^ slot ^ (2 * mask)

                def put(owner=owner, ref=ref, j=j, slot=slot):
                    place(owner, lambda row: ref[j, slot, row])

                if all(masks):
                    put()
                else:
                    pl.when(mask > 0)(put)

    def over(body, init):
        return lax.fori_loop(0, count, body, init, unroll=steps(count, 16))

    def each(d):
        return [(v, c, 2 * d + c) for v in range(VECTORS) for c in range(2)]

    def prepare(d, carry):
        for x in (2 * d, 2 * d + 1):
            here, after = depth[x], depth[lax.rem(x + 1, width)]
            face_x[x + 1] = SURFACE_COUPLING * jnp.minimum(here, after)
            north, south = side_depths(here)
            face_y[x] = SURFACE_COUPLING * north
            face_z[x] = SURFACE_COUPLING * south
        return carry

    over(prepare, 0)
    face_x[0] = face_x[width]
    wrap(pole, width)

    def start(d, carry):
        sums = list(carry)
        for v, _, x in each(d):
            sums[v] = sums[v] + residual[v, x] * residual[v, x]
        return tuple(sums)

    norm = [total(t) for t in over(start, none)]
    taken, left, aim = ([[v for _ in range(VECTORS)] for v in ([], [1.0], [1.0])])

    def apply(d, carry):
        sums = list(carry)
        for v, _, x in each(d):
            centre = pole[v, x + 1]
            value = centre - spread(pole, face_x, face_y, face_z, v, x)
            image[v, x] = value
            sums[v] = sums[v] + centre * value
        return tuple(sums)

    for iteration in range(ITERS):
        energy = [total(t) for t in over(apply, none)]
        size = [n / e for n, e in zip(norm, energy)]
        taken = [combine(s, z, a) for s, z, a in zip(taken, size, aim)]
        if iteration + 1 < ITERS:

            def advance(d, carry, size=size, first=iteration == 0):
                sums = list(carry)
                for v, _, x in each(d):
                    gone = size[v] * pole[v, x + 1]
                    answer[v, x] = gone if first else answer[v, x] + gone
                    value = residual[v, x] - size[v] * image[v, x]
                    residual[v, x] = value
                    sums[v] = sums[v] + value * value
                return tuple(sums)

            fresh = [total(t) for t in over(advance, none)]
            ratio = [f / n for f, n in zip(fresh, norm)]
            left = [combine(l, -z, [0.0] + a) for l, z, a in zip(left, size, aim)]
            aim = [combine(l, q, a) for l, q, a in zip(left, ratio, aim)]

            def turn(d, carry, ratio=ratio):
                for v, _, x in each(d):
                    pole[v, x + 1] = residual[v, x] + ratio[v] * pole[v, x + 1]
                return carry

            over(turn, 0)
            wrap(pole, width)
            norm = fresh

    def finish(d, carry):
        grams = list(carry)
        for x in (2 * d, 2 * d + 1):
            a, b = (answer[v, x] + size[v] * pole[v, x + 1] for v in range(VECTORS))
            answer[0, x], answer[1, x] = a, b
            grams = [grams[0] + a * a, grams[1] + a * b, grams[2] + b * b]
        return (*grams, carry[3] + packed[d])

    *grams, packed_sums = over(finish, (zero,) * 4)
    sums = unpack_rows(packed_sums, 3 + VECTORS * VECTORS * POWERS)

    def heights_with(i, j):
        first = 3 + (i * VECTORS + j) * POWERS
        return sum(c * t for c, t in zip(taken[j], sums[first : first + POWERS]))

    cells = (levels + 1) * width * sub * LANES
    one, mix, two = (
        (sums[n] + total(grams[n]) + (heights_with(i, j) + heights_with(j, i))) / cells
        for n, (i, j) in enumerate(((0, 0), (0, 1), (1, 1)))
    )
    scale_one = jnp.sqrt(one + EPSILON)
    cross = mix / scale_one
    rest = two - 2.0 * cross * cross + cross * cross * one / (one + EPSILON)
    scale_two = jnp.sqrt(rest + EPSILON)
    over_one, over_two = 1.0 / scale_one, 1.0 / scale_two

    outer, inner, _ = orientation()
    begin, part = share(levels)
    departures = []
    for half, (first, source) in enumerate(((begin, done), (levels - part - begin, done_other))):

        def scale(i, carry, first=first, source=source):
            k = first + i
            for where, one, two in (
                (outer, column[0, k], column[1, k]),
                (inner, source[0, i], source[1, i]),
            ):
                unit = one * over_one
                place = pl.ds(where, sub, stride=2)
                tracer[0, k, place, :] = unit
                tracer[1, k, place, :] = (two - cross * unit) * over_two
            return carry

        lax.fori_loop(0, part, scale, 0, unroll=steps(part, 10))
        rows = pl.ds(first, part)
        departure = pltpu.make_async_copy(tracer.at[:, rows], tracer_hbm.at[:, rows], sems.at[half])
        departure.start()
        departures.append(departure)
    for c in range(2):
        x = 2 * me + c
        first, second = (
            jnp.where(depth[x] > 0, surface[v, pl.ds(c, sub, stride=2), :], 0.0) + answer[v, x]
            for v in range(VECTORS)
        )
        unit = first * over_one
        surface_out[0, pl.ds(c, sub, stride=2), :] = unit
        surface_out[1, pl.ds(c, sub, stride=2), :] = (second - cross * unit) * over_two
    for i, value in enumerate((scale_one, cross, scale_two)):
        growth[i] = value[0, 0]
    for departure in departures:
        departure.wait()


def tiled(array):
    *lead, columns, rows = array.shape
    split = array.reshape(*lead, columns, rows // LANES, LANES)
    return jnp.swapaxes(split, -3, -2).reshape(*lead, rows // LANES * columns, LANES)


def untiled(array, columns):
    *lead, high, lanes = array.shape
    split = array.reshape(*lead, high // columns, columns, lanes)
    return jnp.swapaxes(split, -3, -2).reshape(*lead, columns, high // columns * lanes)


def swap(array, mask):
    count = lax.axis_size("lon")
    return lax.ppermute(array, "lon", [(i, i ^ mask) for i in range(count)])


def chip_masks(count):
    lists, loads = ([], []), [0, 0]
    for mask in range(count // 2 - 1, 0, -1):
        core = int(loads[1] < loads[0])
        lists[core].append(mask)
        loads[core] += mask % 2 + mask // 2
    longest = max(map(len, lists))
    return list(zip(*([0] * (longest - len(one)) + one[::-1] for one in lists)))


def gather(block):
    count = lax.axis_size("lon")
    pair = jnp.stack([block, swap(block, 1)])
    fetched = []
    for masks in chip_masks(count):
        moves = [(i, i ^ (2 * masks[i % 2])) for i in range(count) if masks[i % 2]]
        fetched.append(lax.ppermute(pair, "lon", moves))
    fetched = jnp.stack(fetched)
    return pair, fetched, swap(fetched, 1)


def on_device(tracer_pert, surface_pert, zonal_flow, merid_flow, bottom_level):
    vectors, levels, columns, rows = tracer_pert.shape
    count = lax.axis_size("lon")
    sub = rows // LANES
    assert vectors == VECTORS and columns == 2 and rows % LANES == 0
    assert count >= 8 and count & (count - 1) == 0
    width = 2 * count
    f32 = jnp.float32
    vmem = pl.BlockSpec(memory_space=pltpu.VMEM)
    hbm = pl.BlockSpec(memory_space=pltpu.HBM)
    params = pltpu.CompilerParams(vmem_limit_bytes=24 * 2**20)

    def shaped(*shape):
        return jax.ShapeDtypeStruct((*shape, sub, LANES), f32)

    def held(*shape):
        return pltpu.VMEM((*shape, sub, LANES), f32)

    both = pltpu.VMEM((vectors, levels, sub * 2, LANES), f32)
    tracer_pert, zonal_flow, merid_flow = map(tiled, (tracer_pert, zonal_flow, merid_flow))
    outward = [(i, (i + 1) % count if i % 2 else (i - 1) % count) for i in range(count)]
    part = levels // 2
    surface, bottom = tiled(surface_pert), tiled(bottom_level)
    edge_rows = VECTORS * levels + part + RIM

    edge = pl.pallas_call(
        functools.partial(edge_kernel, levels, sub),
        out_shape=shaped(edge_rows),
        in_specs=[hbm] * 4,
        out_specs=hbm,
        scratch_shapes=[
            both,
            pltpu.VMEM((part, sub * 2, LANES), f32),
            pltpu.VMEM((vectors, sub * 2, LANES), f32),
            pltpu.VMEM((sub * 2, LANES), jnp.int32),
            held(edge_rows),
            pltpu.SemaphoreType.DMA((VECTORS + 3,)),
            pltpu.SemaphoreType.DMA((VECTORS + 1,)),
        ],
        compiler_params=pltpu.CompilerParams(vmem_limit_bytes=60 * 2**20),
        name="edge_columns",
    )(tracer_pert, zonal_flow, surface, bottom)
    edge_far = lax.ppermute(edge, "lon", outward)
    flow_other = lax.ppermute(edge_far[VECTORS * levels : edge_rows - RIM], "grp", [(0, 1), (1, 0)])
    cross, mate, raw, mate_raw, flow_in, mate_flow = pl.pallas_call(
        functools.partial(first_kernel, levels, sub),
        out_shape=(
            shaped(VECTORS * levels),
            shaped(VECTORS * levels),
            shaped(VECTORS * levels),
            shaped(VECTORS * levels),
            shaped(levels),
            shaped(levels + RIM),
        ),
        in_specs=[pl.BlockSpec(memory_space=pl.ANY)] + [vmem] * 5,
        out_specs=(vmem,) * 6,
        compiler_params=params,
        name="partial_step",
    )(edge, tracer_pert, zonal_flow, merid_flow, surface, bottom)
    cross_far = lax.ppermute(cross, "lon", outward)
    mate_far, mate_raw_far, mate_flow_far = (swap(x, 1) for x in (mate, mate_raw, mate_flow))
    arrived = (
        raw, cross, mate, mate_raw, flow_in, mate_flow,
        edge_far, mate_far, mate_raw_far, mate_flow_far, merid_flow,
    )
    halves = (
        shaped(vectors, part),
        shaped(vectors, part),
        shaped(part),
        shaped(VECTORS + 3),
    )

    def halo(own, *operands):
        shapes = halves + ((shaped(POWERS + 1, vectors, 2),) if own else ())
        return pl.pallas_call(
            functools.partial(halo_kernel, levels, sub, own),
            out_shape=shapes,
            in_specs=[vmem] * len(operands),
            out_specs=(vmem,) * len(shapes),
            compiler_params=params,
            name="own_levels" if own else "other_levels",
        )(*operands)

    done, *near_half, powers = halo(True, *arrived)
    done_other, *far_half = halo(False, *arrived, flow_other)
    column, message = pl.pallas_call(
        functools.partial(second_kernel, levels, sub),
        out_shape=(shaped(vectors, levels), shaped(BLOCKS)),
        in_specs=[vmem] * 9,
        out_specs=(vmem, vmem),
        compiler_params=params,
        name="outer_column",
    )(cross_far, *near_half, *far_half, powers, mate_flow)
    tracer_vec, surface_vec, growth = pl.pallas_call(
        functools.partial(third_kernel, levels, sub, count),
        out_shape=(
            jax.ShapeDtypeStruct((vectors, levels, sub * 2, LANES), f32),
            jax.ShapeDtypeStruct((vectors, sub * 2, LANES), f32),
            jax.ShapeDtypeStruct((3,), f32),
        ),
        in_specs=[vmem] * 7,
        out_specs=(hbm, vmem, pl.BlockSpec(memory_space=pltpu.SMEM)),
        scratch_shapes=[
            both,
            pltpu.SemaphoreType.DMA((2,)),
            held(vectors, width + 2),
            *[held(vectors, width)] * 3,
            held(width),
            held(width + 1),
            held(width),
            held(width),
            held(count),
        ],
        compiler_params=pltpu.CompilerParams(vmem_limit_bytes=32 * 2**20),
        name="surface_and_scale",
    )(*gather(message), surface, column, done, done_other)
    return (untiled(tracer_vec, 2), untiled(surface_vec, 2), growth)


def solution(mesh):
    placed = (
        P("grp", None, "lon", None),
        P("grp", "lon", None),
        P(None, "lon", None),
        P(None, "lon", None),
        P("lon", None),
    )
    return jax.shard_map(
        on_device,
        mesh=mesh,
        in_specs=placed,
        out_specs=(P("grp", None, "lon", None), P("grp", "lon", None), P("grp")),
        check_vma=False,
    )
```

```python
import functools

import jax
import jax.numpy as jnp
from jax import lax
from jax.experimental import pallas as pl
from jax.experimental.pallas import tpu as pltpu
from jax.sharding import PartitionSpec as P

ITERS = 3


DIFFUSIVITY = 0.5
TIME_STEP = 0.2
SURFACE_COUPLING = 0.5
STERIC_GAIN = 2.0
EPSILON = 1e-06

LANES = 128
VECTORS = 2
SLOPE = 0.25 * TIME_STEP
SPREAD = TIME_STEP * DIFFUSIVITY
DEPTHS = VECTORS * 2
RIM = DEPTHS + 2
GRAMS = RIM
BLOCKS = GRAMS + 1
POWERS = ITERS


def next_row(tile):
    turned = pltpu.roll(tile, LANES - 1, 1)
    carried = pltpu.roll(turned, tile.shape[0] - 1, 0)
    lane = lax.broadcasted_iota(jnp.int32, tile.shape, 1)
    return jnp.where(lane == LANES - 1, carried, turned)


def prior_row(tile):
    turned = pltpu.roll(tile, 1, 1)
    carried = pltpu.roll(turned, 1, 0)
    lane = lax.broadcasted_iota(jnp.int32, tile.shape, 1)
    return jnp.where(lane == 0, carried, turned)


def wall_depth(depth):
    subs, lane = (lax.broadcasted_iota(jnp.int32, depth.shape, axis) for axis in (0, 1))
    last = (subs == depth.shape[0] - 1) & (lane == LANES - 1)
    return jnp.where(last, jnp.zeros_like(depth), jnp.minimum(depth, next_row(depth)))


def face_pair(level, face_depth, flow_sum):
    slope = SLOPE * flow_sum
    open_face = level < face_depth
    return (
        jnp.where(open_face, slope + SPREAD, 0.0),
        jnp.where(open_face, slope - SPREAD, 0.0),
    )


def outflow(pair, near, far):
    return pair[0] * near + pair[1] * far


def side_pairs(level, depths, flow):
    return (
        face_pair(level, depths[0], flow + next_row(flow)),
        face_pair(level, depths[1], -(flow + prior_row(flow))),
    )


def divergence_y(pairs, tile):
    return outflow(pairs[0], tile, next_row(tile)) + outflow(pairs[1], tile, prior_row(tile))


def side_depths(depth):
    north = wall_depth(depth)
    return north, prior_row(north)


def orientation():
    outer = lax.rem(lax.axis_index("lon"), 2)
    return outer, 1 - outer, (2 * outer - 1).astype(jnp.float32)


def steps(count, most):
    return max(u for u in range(1, most + 1) if count % u == 0)


def share(levels):
    assert lax.axis_size("grp") == 2 and levels % 2 == 0
    part = levels // 2
    return lax.axis_index("grp") * (levels - part), part


def pack_rim(sub, surface, bottom, target, base):
    for c in range(2):
        for v in range(VECTORS):
            target[base + v * 2 + c] = surface[v, pl.ds(c, sub, stride=2), :]
        target[base + DEPTHS + c] = bottom[pl.ds(c, sub, stride=2), :].astype(jnp.float32)


def edge_kernel(
    levels, sub, tracer_hbm, zonal_hbm, surface_hbm, bottom_hbm, edge_hbm,
    tracer, zonal, surface, bottom, edge, sems_in, sems_out,
):
    outer, _, _ = orientation()
    start, part = share(levels)

    def move(source, target, sem):
        copy = pltpu.make_async_copy(source, target, sem)
        copy.start()
        return copy

    arrivals = [
        move(tracer_hbm.at[v], tracer.at[v], sems_in.at[v]) for v in range(VECTORS)
    ] + [move(zonal_hbm.at[pl.ds(start, part)], zonal, sems_in.at[VECTORS])]
    small = [
        move(surface_hbm, surface, sems_in.at[VECTORS + 1]),
        move(bottom_hbm, bottom, sems_in.at[VECTORS + 2]),
    ]
    departures = []
    for v, arrival in enumerate(arrivals):
        number = part if v == VECTORS else levels
        arrival.wait()
        if v == VECTORS:
            for copy in small:
                copy.wait()
            pack_rim(sub, surface, bottom, edge, v * levels + number)

        def body(k, carry, v=v):
            source = zonal if v == VECTORS else tracer.at[v]
            edge[v * levels + k] = source[k, pl.ds(outer, sub, stride=2), :]
            return carry

        lax.fori_loop(0, number, body, 0, unroll=steps(number, 10))
        rows = pl.ds(v * levels, number + (RIM if v == VECTORS else 0))
        departures.append(move(edge.at[rows], edge_hbm.at[rows], sems_out.at[v]))
    for departure in departures:
        departure.wait()


def first_kernel(
    levels, sub, edge, tracer, zonal, merid, surface, bottom,
    cross, mate, raw, mate_raw, flow_in, mate_flow,
):
    del edge
    outer, inner, sign = orientation()

    def column(ref, where, *lead):
        return ref[(*lead, pl.ds(where, sub, stride=2), slice(None))]

    depth = [column(bottom, where).astype(jnp.float32) for where in (outer, inner)]
    between = jnp.minimum(*depth)
    along = [side_depths(d) for d in depth]
    pack_rim(sub, surface, bottom, mate_flow, levels)

    def body(k, carry):
        level = k.astype(jnp.float32)
        flow = [column(zonal, where, k) for where in (outer, inner)]
        turn = [column(merid, where, k) for where in (outer, inner)]
        middle = face_pair(level, between, -sign * (flow[0] + flow[1]))
        sides = [side_pairs(level, along[c], turn[c]) for c in range(2)]
        for v in range(VECTORS):
            cells = [column(tracer, where, v, k) for where in (outer, inner)]
            flux = outflow(middle, *cells)
            kept = [
                jnp.where(level < depth[c], cells[c], 0.0) - divergence_y(sides[c], cells[c])
                for c in range(2)
            ]
            cross[v * levels + k] = kept[0] - flux
            raw[v * levels + k] = cells[0]
            mate[v * levels + k] = kept[1] + flux
            mate_raw[v * levels + k] = cells[1]
        flow_in[k] = flow[0]
        mate_flow[k] = flow[1]
        return carry

    lax.fori_loop(0, levels, body, 0, unroll=steps(levels, 10))


def wrap(pole, width):
    for v in range(VECTORS):
        pole[v, 0] = pole[v, width]
        pole[v, width + 1] = pole[v, 1]


def spread(pole, face_x, face_y, face_z, v, x):
    west, centre, east = (pole[v, x + j] for j in range(3))
    return (face_x[x + 1] * (east - centre) - face_x[x] * (centre - west)) + (
        face_y[x] * (next_row(centre) - centre) - face_z[x] * (centre - prior_row(centre))
    )


def halo_kernel(
    levels, sub, own, raw, cross, mate, mate_raw, flow_in, mate_flow,
    raw_far, mate_far, mate_raw_far, mate_flow_far, merid, *refs,
):
    outer, inner, sign = orientation()
    start, part = share(levels)
    first = start if own else levels - part - start
    if own:
        done, base, weight, sums, powers = refs
        powers_of_heights(levels, part, mate_flow, mate_flow_far, raw_far, powers)
        flow_far = raw_far.at[pl.ds(VECTORS * levels, part)]
    else:
        flow_far, done, base, weight, sums = refs
    near, far = (raw, mate_raw), (raw_far, mate_raw_far)
    rim = levels + DEPTHS
    depth = [mate_flow[rim + where] for where in (outer, inner)]
    beside = [
        jnp.minimum(depth[0], raw_far[VECTORS * levels + part + DEPTHS + inner]),
        jnp.minimum(depth[1], mate_flow_far[rim + outer]),
    ]
    between = jnp.minimum(*depth)
    along = [side_depths(d) for d in depth]
    zero = jnp.zeros_like(between)

    def body(i, carry):
        k = first + i
        level = k.astype(jnp.float32)
        flow = [flow_in[k], mate_flow[k]]
        beyond = [flow_far[i], mate_flow_far[k]]
        turn = [merid[k, pl.ds(where, sub, stride=2), :] for where in (outer, inner)]
        middle = face_pair(level, between, -sign * (flow[0] + flow[1]))
        edges = [
            face_pair(level, beside[c], (sign, -sign)[c] * (flow[c] + beyond[c])) for c in range(2)
        ]
        sides = [side_pairs(level, along[c], turn[c]) for c in range(2)]
        weight[i] = edges[0][1]
        totals, grams = list(carry[:VECTORS]), list(carry[VECTORS:])
        fresh = []
        for v in range(VECTORS):
            row = v * levels + k
            flux = [outflow(edges[c], near[c][row], far[c][row]) for c in range(2)]
            outside, inside = cross[row] - flux[0], mate[row] - flux[1]
            other = mate_far[row] + flux[1]
            crossing = outflow(middle, outside, inside)
            base[v, i] = (
                outside
                - outflow(edges[0], outside, flux[0])
                - crossing
                - divergence_y(sides[0], outside)
            )
            value = (
                inside - outflow(edges[1], inside, other) + crossing - divergence_y(sides[1], inside)
            )
            done[v, i] = value
            totals[v] = totals[v] + value
            fresh.append(value)
        return (*totals, *add_products(grams, *fresh))

    found = lax.fori_loop(0, part, body, (zero,) * (VECTORS + 3), unroll=steps(part, 10))
    for row, tile in enumerate(found):
        sums[row] = tile


def add_products(grams, a, b):
    return [grams[0] + a * a, grams[1] + a * b, grams[2] + b * b]


def second_kernel(
    levels, sub, cross_far, *refs,
):
    outer, inner, _ = orientation()
    start, part = share(levels)
    parts = refs[:3], refs[3:6]
    powers, mate_flow, column, message = refs[6:]
    zero = jnp.zeros(powers.shape[-2:], jnp.float32)
    carry = (zero,) * (VECTORS + 3)
    for first, (base, weight, _) in zip((start, levels - part - start), parts):

        def body(i, carry, first=first, base=base, weight=weight):
            totals, fresh = [], []
            for v in range(VECTORS):
                value = base[v, i] - weight[i] * cross_far[v * levels + first + i]
                column[v, first + i] = value
                totals.append(carry[v] + value)
                fresh.append(value)
            return (*totals, *add_products(carry[VECTORS:], *fresh))

        carry = lax.fori_loop(0, part, body, carry, unroll=steps(part, 10))
    inside = [parts[0][2][row] + parts[1][2][row] for row in range(VECTORS + 3)]
    gain = STERIC_GAIN / levels
    rows = [a + b for a, b in zip(carry[VECTORS:], inside[VECTORS:])]
    residual = []
    for v in range(VECTORS):
        residual.append(
            [gain * total_of + powers[POWERS, v, c] for c, total_of in enumerate((carry[v], inside[v]))]
        )
        for c, where in enumerate((outer, inner)):
            message[v * 2 + where] = residual[v][c]

    def product(one, two):
        return one[0] * two[0] + one[1] * two[1]

    heights = [[powers[0, v, c] for c in range(2)] for v in range(VECTORS)]
    for n, (i, j) in enumerate(((0, 0), (0, 1), (1, 1))):
        rows[n] = rows[n] + product(heights[i], heights[j])
    for i in range(VECTORS):
        for j in range(VECTORS):
            for m in range(POWERS):
                rows.append(product([powers[m, i, c] for c in range(2)], residual[j]))
    message[GRAMS] = pack_rows(rows)
    for c in range(2):
        message[DEPTHS + c] = mate_flow[levels + DEPTHS + c]


def pack_rows(tiles):
    shape = tiles[0].shape
    sub, lane = (lax.broadcasted_iota(jnp.int32, shape, axis) for axis in (0, 1))
    half = shape[1] // 2
    packed = jnp.zeros(shape, jnp.float32)
    for n, tile in enumerate(tiles):
        row = jnp.sum(tile, axis=0, keepdims=True)
        row = row + pltpu.roll(row, half, 1)
        place = (sub == n % shape[0]) & ((lane < half) == (n < shape[0]))
        packed = jnp.where(place, row, packed)
    return packed


def unpack_rows(packed, count):
    lane = lax.broadcasted_iota(jnp.int32, packed.shape, 1)
    low = lane < packed.shape[1] // 2
    sums = [
        jnp.sum(jnp.where(side, packed, 0.0), axis=1, keepdims=True)
        for side in (low, jnp.logical_not(low))
    ]
    size = packed.shape[0]
    return [sums[n // size][n % size : n % size + 1] for n in range(count)]


def powers_of_heights(levels, part, mate_flow, mate_flow_far, raw_far, powers):
    outer, inner, _ = orientation()
    cross_base = VECTORS * levels + part
    line = [
        (mate_flow_far, levels, inner),
        (mate_flow_far, levels, outer),
        (mate_flow, levels, inner),
        (mate_flow, levels, outer),
        (raw_far, cross_base, inner),
        (raw_far, cross_base, outer),
    ]
    depth = [ref[base + DEPTHS + where] for ref, base, where in line]
    faces = [SURFACE_COUPLING * jnp.minimum(a, b) for a, b in zip(depth, depth[1:])]
    sides = [side_depths(SURFACE_COUPLING * d) for d in depth[1:5]]
    for v in range(VECTORS):
        field = [
            jnp.where(d > 0, ref[base + v * 2 + where], 0.0)
            for d, (ref, base, where) in zip(depth, line)
        ]

        def bend(field, first, last):
            found = []
            for j in range(first, last):
                west, centre, east = field[j - 1 : j + 2]
                north, south = sides[j - 1]
                found.append(
                    (faces[j] * (east - centre) - faces[j - 1] * (centre - west))
                    + (north * (next_row(centre) - centre) - south * (centre - prior_row(centre)))
                )
            return found

        lap = bend(field, 1, 5)
        image = [None] + [h - p for h, p in zip(field[1:5], lap)]
        again = [p - q for p, q in zip(image[2:4], bend(image, 2, 4))]
        for c, where in enumerate((3, 2)):
            powers[0, v, c] = field[where]
            powers[1, v, c] = image[where]
            powers[2, v, c] = again[where - 2]
            powers[POWERS, v, c] = lap[where - 1]


def total(tile):
    return jnp.sum(jnp.sum(tile, axis=0, keepdims=True), axis=1, keepdims=True)


def combine(one, factor, two):
    longest = max(len(one), len(two))
    one, two = (list(c) + [0.0] * (longest - len(c)) for c in (one, two))
    return [a + factor * b for a, b in zip(one, two)]


def third_kernel(
    levels, sub, count, pair, fetched, fetched_mate, surface, column, done, done_other,
    tracer_hbm, surface_out, growth, tracer, sems, pole, residual, answer, image, depth, face_x, face_y, face_z, packed,
):
    width = 2 * count
    me = lax.axis_index("lon")
    core = lax.rem(me, 2)
    zero = jnp.zeros((sub, LANES), jnp.float32)
    none = (zero,) * VECTORS

    def place(owner, block):
        packed[owner] = block(GRAMS)
        for c in range(2):
            x = 2 * owner + c
            depth[x] = block(DEPTHS + c)
            for v in range(VECTORS):
                value = block(v * 2 + c)
                residual[v, x] = value
                pole[v, x + 1] = value

    for slot in range(2):
        place(me ^ slot, lambda row, slot=slot: pair[slot, row])
    for ref, flip in ((fetched, 0), (fetched_mate, 1)):
        for j, masks in enumerate(chip_masks(count)):
            mask = jnp.where((core ^ flip) == 0, *masks)
            for slot in range(2):
                owner = me ^ flip ^ slot ^ (2 * mask)

                def put(owner=owner, ref=ref, j=j, slot=slot):
                    place(owner, lambda row: ref[j, slot, row])

                if all(masks):
                    put()
                else:
                    pl.when(mask > 0)(put)

    def over(body, init):
        return lax.fori_loop(0, count, body, init, unroll=steps(count, 16))

    def each(d):
        return [(v, c, 2 * d + c) for v in range(VECTORS) for c in range(2)]

    def prepare(d, carry):
        for x in (2 * d, 2 * d + 1):
            here, after = depth[x], depth[lax.rem(x + 1, width)]
            face_x[x + 1] = SURFACE_COUPLING * jnp.minimum(here, after)
            north, south = side_depths(here)
            face_y[x] = SURFACE_COUPLING * north
            face_z[x] = SURFACE_COUPLING * south
        return carry

    over(prepare, 0)
    face_x[0] = face_x[width]
    wrap(pole, width)

    def start(d, carry):
        sums = list(carry)
        for v, _, x in each(d):
            sums[v] = sums[v] + residual[v, x] * residual[v, x]
        return tuple(sums)

    norm = [total(t) for t in over(start, none)]
    taken, left, aim = ([[v for _ in range(VECTORS)] for v in ([], [1.0], [1.0])])

    def apply(d, carry):
        sums = list(carry)
        for v, _, x in each(d):
            centre = pole[v, x + 1]
            value = centre - spread(pole, face_x, face_y, face_z, v, x)
            image[v, x] = value
            sums[v] = sums[v] + centre * value
        return tuple(sums)

    for iteration in range(ITERS):
        energy = [total(t) for t in over(apply, none)]
        size = [n / e for n, e in zip(norm, energy)]
        taken = [combine(s, z, a) for s, z, a in zip(taken, size, aim)]
        if iteration + 1 < ITERS:

            def advance(d, carry, size=size, first=iteration == 0):
                sums = list(carry)
                for v, _, x in each(d):
                    gone = size[v] * pole[v, x + 1]
                    answer[v, x] = gone if first else answer[v, x] + gone
                    value = residual[v, x] - size[v] * image[v, x]
                    residual[v, x] = value
                    sums[v] = sums[v] + value * value
                return tuple(sums)

            fresh = [total(t) for t in over(advance, none)]
            ratio = [f / n for f, n in zip(fresh, norm)]
            left = [combine(l, -z, [0.0] + a) for l, z, a in zip(left, size, aim)]
            aim = [combine(l, q, a) for l, q, a in zip(left, ratio, aim)]

            def turn(d, carry, ratio=ratio):
                for v, _, x in each(d):
                    pole[v, x + 1] = residual[v, x] + ratio[v] * pole[v, x + 1]
                return carry

            over(turn, 0)
            wrap(pole, width)
            norm = fresh

    def finish(d, carry):
        grams = list(carry)
        for x in (2 * d, 2 * d + 1):
            a, b = (answer[v, x] + size[v] * pole[v, x + 1] for v in range(VECTORS))
            answer[0, x], answer[1, x] = a, b
            grams = [grams[0] + a * a, grams[1] + a * b, grams[2] + b * b]
        return (*grams, carry[3] + packed[d])

    *grams, packed_sums = over(finish, (zero,) * 4)
    sums = unpack_rows(packed_sums, 3 + VECTORS * VECTORS * POWERS)

    def heights_with(i, j):
        first = 3 + (i * VECTORS + j) * POWERS
        return sum(c * t for c, t in zip(taken[j], sums[first : first + POWERS]))

    cells = (levels + 1) * width * sub * LANES
    one, mix, two = (
        (sums[n] + total(grams[n]) + (heights_with(i, j) + heights_with(j, i))) / cells
        for n, (i, j) in enumerate(((0, 0), (0, 1), (1, 1)))
    )
    scale_one = jnp.sqrt(one + EPSILON)
    cross = mix / scale_one
    rest = two - 2.0 * cross * cross + cross * cross * one / (one + EPSILON)
    scale_two = jnp.sqrt(rest + EPSILON)
    over_one, over_two = 1.0 / scale_one, 1.0 / scale_two

    outer, inner, _ = orientation()
    begin, part = share(levels)
    departures = []
    for half, (first, source) in enumerate(((begin, done), (levels - part - begin, done_other))):

        def scale(i, carry, first=first, source=source):
            k = first + i
            for where, one, two in (
                (outer, column[0, k], column[1, k]),
                (inner, source[0, i], source[1, i]),
            ):
                unit = one * over_one
                place = pl.ds(where, sub, stride=2)
                tracer[0, k, place, :] = unit
                tracer[1, k, place, :] = (two - cross * unit) * over_two
            return carry

        lax.fori_loop(0, part, scale, 0, unroll=steps(part, 10))
        rows = pl.ds(first, part)
        departure = pltpu.make_async_copy(tracer.at[:, rows], tracer_hbm.at[:, rows], sems.at[half])
        departure.start()
        departures.append(departure)
    for c in range(2):
        x = 2 * me + c
        first, second = (
            jnp.where(depth[x] > 0, surface[v, pl.ds(c, sub, stride=2), :], 0.0) + answer[v, x]
            for v in range(VECTORS)
        )
        unit = first * over_one
        surface_out[0, pl.ds(c, sub, stride=2), :] = unit
        surface_out[1, pl.ds(c, sub, stride=2), :] = (second - cross * unit) * over_two
    for i, value in enumerate((scale_one, cross, scale_two)):
        growth[i] = value[0, 0]
    for departure in departures:
        departure.wait()


def tiled(array):
    *lead, columns, rows = array.shape
    split = array.reshape(*lead, columns, rows // LANES, LANES)
    return jnp.swapaxes(split, -3, -2).reshape(*lead, rows // LANES * columns, LANES)


def untiled(array, columns):
    *lead, high, lanes = array.shape
    split = array.reshape(*lead, high // columns, columns, lanes)
    return jnp.swapaxes(split, -3, -2).reshape(*lead, columns, high // columns * lanes)


def swap(array, mask):
    count = lax.axis_size("lon")
    return lax.ppermute(array, "lon", [(i, i ^ mask) for i in range(count)])


def chip_masks(count):
    lists, loads = ([], []), [0, 0]
    for mask in range(count // 2 - 1, 0, -1):
        core = int(loads[1] < loads[0])
        lists[core].append(mask)
        loads[core] += mask % 2 + mask // 2
    longest = max(map(len, lists))
    return list(zip(*(one + [0] * (longest - len(one)) for one in lists)))


def gather(block):
    count = lax.axis_size("lon")
    pair = jnp.stack([block, swap(block, 1)])
    fetched = []
    for masks in chip_masks(count):
        moves = [(i, i ^ (2 * masks[i % 2])) for i in range(count) if masks[i % 2]]
        fetched.append(lax.ppermute(pair, "lon", moves))
    fetched = jnp.stack(fetched)
    return pair, fetched, swap(fetched, 1)


def on_device(tracer_pert, surface_pert, zonal_flow, merid_flow, bottom_level):
    vectors, levels, columns, rows = tracer_pert.shape
    count = lax.axis_size("lon")
    sub = rows // LANES
    assert vectors == VECTORS and columns == 2 and rows % LANES == 0
    assert count >= 8 and count & (count - 1) == 0
    width = 2 * count
    f32 = jnp.float32
    vmem = pl.BlockSpec(memory_space=pltpu.VMEM)
    hbm = pl.BlockSpec(memory_space=pltpu.HBM)
    params = pltpu.CompilerParams(vmem_limit_bytes=24 * 2**20)

    def shaped(*shape):
        return jax.ShapeDtypeStruct((*shape, sub, LANES), f32)

    def held(*shape):
        return pltpu.VMEM((*shape, sub, LANES), f32)

    both = pltpu.VMEM((vectors, levels, sub * 2, LANES), f32)
    tracer_pert, zonal_flow, merid_flow = map(tiled, (tracer_pert, zonal_flow, merid_flow))
    outward = [(i, (i + 1) % count if i % 2 else (i - 1) % count) for i in range(count)]
    part = levels // 2
    surface, bottom = tiled(surface_pert), tiled(bottom_level)
    edge_rows = VECTORS * levels + part + RIM

    edge = pl.pallas_call(
        functools.partial(edge_kernel, levels, sub),
        out_shape=shaped(edge_rows),
        in_specs=[hbm] * 4,
        out_specs=hbm,
        scratch_shapes=[
            both,
            pltpu.VMEM((part, sub * 2, LANES), f32),
            pltpu.VMEM((vectors, sub * 2, LANES), f32),
            pltpu.VMEM((sub * 2, LANES), jnp.int32),
            held(edge_rows),
            pltpu.SemaphoreType.DMA((VECTORS + 3,)),
            pltpu.SemaphoreType.DMA((VECTORS + 1,)),
        ],
        compiler_params=pltpu.CompilerParams(vmem_limit_bytes=60 * 2**20),
        name="edge_columns",
    )(tracer_pert, zonal_flow, surface, bottom)
    edge_far = lax.ppermute(edge, "lon", outward)
    flow_other = lax.ppermute(edge_far[VECTORS * levels : edge_rows - RIM], "grp", [(0, 1), (1, 0)])
    cross, mate, raw, mate_raw, flow_in, mate_flow = pl.pallas_call(
        functools.partial(first_kernel, levels, sub),
        out_shape=(
            shaped(VECTORS * levels),
            shaped(VECTORS * levels),
            shaped(VECTORS * levels),
            shaped(VECTORS * levels),
            shaped(levels),
            shaped(levels + RIM),
        ),
        in_specs=[pl.BlockSpec(memory_space=pl.ANY)] + [vmem] * 5,
        out_specs=(vmem,) * 6,
        compiler_params=params,
        name="partial_step",
    )(edge, tracer_pert, zonal_flow, merid_flow, surface, bottom)
    cross_far = lax.ppermute(cross, "lon", outward)
    mate_far, mate_raw_far, mate_flow_far = (swap(x, 1) for x in (mate, mate_raw, mate_flow))
    arrived = (
        raw, cross, mate, mate_raw, flow_in, mate_flow,
        edge_far, mate_far, mate_raw_far, mate_flow_far, merid_flow,
    )
    halves = (
        shaped(vectors, part),
        shaped(vectors, part),
        shaped(part),
        shaped(VECTORS + 3),
    )

    def halo(own, *operands):
        shapes = halves + ((shaped(POWERS + 1, vectors, 2),) if own else ())
        return pl.pallas_call(
            functools.partial(halo_kernel, levels, sub, own),
            out_shape=shapes,
            in_specs=[vmem] * len(operands),
            out_specs=(vmem,) * len(shapes),
            compiler_params=params,
            name="own_levels" if own else "other_levels",
        )(*operands)

    done, *near_half, powers = halo(True, *arrived)
    done_other, *far_half = halo(False, *arrived, flow_other)
    column, message = pl.pallas_call(
        functools.partial(second_kernel, levels, sub),
        out_shape=(shaped(vectors, levels), shaped(BLOCKS)),
        in_specs=[vmem] * 9,
        out_specs=(vmem, vmem),
        compiler_params=params,
        name="outer_column",
    )(cross_far, *near_half, *far_half, powers, mate_flow)
    tracer_vec, surface_vec, growth = pl.pallas_call(
        functools.partial(third_kernel, levels, sub, count),
        out_shape=(
            jax.ShapeDtypeStruct((vectors, levels, sub * 2, LANES), f32),
            jax.ShapeDtypeStruct((vectors, sub * 2, LANES), f32),
            jax.ShapeDtypeStruct((3,), f32),
        ),
        in_specs=[vmem] * 7,
        out_specs=(hbm, vmem, pl.BlockSpec(memory_space=pltpu.SMEM)),
        scratch_shapes=[
            both,
            pltpu.SemaphoreType.DMA((2,)),
            held(vectors, width + 2),
            *[held(vectors, width)] * 3,
            held(width),
            held(width + 1),
            held(width),
            held(width),
            held(count),
        ],
        compiler_params=pltpu.CompilerParams(vmem_limit_bytes=32 * 2**20),
        name="surface_and_scale",
    )(*gather(message), surface, column, done, done_other)
    return (untiled(tracer_vec, 2), untiled(surface_vec, 2), growth)


def solution(mesh):
    placed = (
        P("grp", None, "lon", None),
        P("grp", "lon", None),
        P(None, "lon", None),
        P(None, "lon", None),
        P("lon", None),
    )
    return jax.shard_map(
        on_device,
        mesh=mesh,
        in_specs=placed,
        out_specs=(P("grp", None, "lon", None), P("grp", "lon", None), P("grp")),
        check_vma=False,
    )
```

```python
import functools

import jax
import jax.numpy as jnp
from jax import lax
from jax.experimental import pallas as pl
from jax.experimental.pallas import tpu as pltpu
from jax.sharding import PartitionSpec as P

ITERS = 3


DIFFUSIVITY = 0.5
TIME_STEP = 0.2
SURFACE_COUPLING = 0.5
STERIC_GAIN = 2.0
EPSILON = 1e-06

LANES = 128
VECTORS = 2
SLOPE = 0.25 * TIME_STEP
SPREAD = TIME_STEP * DIFFUSIVITY
DEPTHS = VECTORS * 2
RIM = DEPTHS + 2
GRAMS = RIM
BLOCKS = GRAMS + 1
POWERS = ITERS


def next_row(tile):
    turned = pltpu.roll(tile, LANES - 1, 1)
    carried = pltpu.roll(turned, tile.shape[0] - 1, 0)
    lane = lax.broadcasted_iota(jnp.int32, tile.shape, 1)
    return jnp.where(lane == LANES - 1, carried, turned)


def prior_row(tile):
    turned = pltpu.roll(tile, 1, 1)
    carried = pltpu.roll(turned, 1, 0)
    lane = lax.broadcasted_iota(jnp.int32, tile.shape, 1)
    return jnp.where(lane == 0, carried, turned)


def wall_depth(depth):
    subs, lane = (lax.broadcasted_iota(jnp.int32, depth.shape, axis) for axis in (0, 1))
    last = (subs == depth.shape[0] - 1) & (lane == LANES - 1)
    return jnp.where(last, jnp.zeros_like(depth), jnp.minimum(depth, next_row(depth)))


def face_pair(level, face_depth, flow_sum):
    slope = SLOPE * flow_sum
    open_face = level < face_depth
    return (
        jnp.where(open_face, slope + SPREAD, 0.0),
        jnp.where(open_face, slope - SPREAD, 0.0),
    )


def outflow(pair, near, far):
    return pair[0] * near + pair[1] * far


def side_pairs(level, depths, flow):
    return (
        face_pair(level, depths[0], flow + next_row(flow)),
        face_pair(level, depths[1], -(flow + prior_row(flow))),
    )


def divergence_y(pairs, tile):
    return outflow(pairs[0], tile, next_row(tile)) + outflow(pairs[1], tile, prior_row(tile))


def side_depths(depth):
    north = wall_depth(depth)
    return north, prior_row(north)


def orientation():
    outer = lax.rem(lax.axis_index("lon"), 2)
    return outer, 1 - outer, (2 * outer - 1).astype(jnp.float32)


def steps(count, most):
    return max(u for u in range(1, most + 1) if count % u == 0)


def share(levels):
    assert lax.axis_size("grp") == 2 and levels % 2 == 0
    part = levels // 2
    return lax.axis_index("grp") * (levels - part), part


def pack_rim(sub, surface, bottom, target, base):
    for c in range(2):
        for v in range(VECTORS):
            target[base + v * 2 + c] = surface[v, pl.ds(c, sub, stride=2), :]
        target[base + DEPTHS + c] = bottom[pl.ds(c, sub, stride=2), :].astype(jnp.float32)


def edge_kernel(
    levels, sub, tracer_hbm, zonal_hbm, surface_hbm, bottom_hbm, edge_hbm, flow_hbm,
    tracer, zonal, surface, bottom, edge, flow, sems_in, sems_out,
):
    outer, _, _ = orientation()
    start, part = share(levels)

    def move(source, target, sem):
        copy = pltpu.make_async_copy(source, target, sem)
        copy.start()
        return copy

    first = [
        move(zonal_hbm.at[pl.ds(start, part)], zonal, sems_in.at[0]),
        move(surface_hbm, surface, sems_in.at[1]),
        move(bottom_hbm, bottom, sems_in.at[2]),
    ]
    arrivals = [move(tracer_hbm.at[v], tracer.at[v], sems_in.at[3 + v]) for v in range(VECTORS)]
    for copy in first:
        copy.wait()

    def take(k, carry):
        flow[k] = zonal[k, pl.ds(outer, sub, stride=2), :]
        return carry

    lax.fori_loop(0, part, take, 0, unroll=steps(part, 10))
    departures = [move(flow, flow_hbm, sems_out.at[VECTORS])]
    pack_rim(sub, surface, bottom, edge, VECTORS * levels)
    for v, arrival in enumerate(arrivals):
        arrival.wait()

        def body(k, carry, v=v):
            edge[v * levels + k] = tracer[v, k, pl.ds(outer, sub, stride=2), :]
            return carry

        lax.fori_loop(0, levels, body, 0, unroll=steps(levels, 10))
        rows = pl.ds(v * levels, levels + (RIM if v == VECTORS - 1 else 0))
        departures.append(move(edge.at[rows], edge_hbm.at[rows], sems_out.at[v]))
    for departure in departures:
        departure.wait()


def first_kernel(
    levels, sub, edge, tracer, zonal, merid, surface, bottom,
    cross, mate, raw, mate_raw, flow_in, mate_flow,
):
    del edge
    outer, inner, sign = orientation()

    def column(ref, where, *lead):
        return ref[(*lead, pl.ds(where, sub, stride=2), slice(None))]

    depth = [column(bottom, where).astype(jnp.float32) for where in (outer, inner)]
    between = jnp.minimum(*depth)
    along = [side_depths(d) for d in depth]
    pack_rim(sub, surface, bottom, mate_flow, levels)

    def body(k, carry):
        level = k.astype(jnp.float32)
        flow = [column(zonal, where, k) for where in (outer, inner)]
        turn = [column(merid, where, k) for where in (outer, inner)]
        middle = face_pair(level, between, -sign * (flow[0] + flow[1]))
        sides = [side_pairs(level, along[c], turn[c]) for c in range(2)]
        for v in range(VECTORS):
            cells = [column(tracer, where, v, k) for where in (outer, inner)]
            flux = outflow(middle, *cells)
            kept = [
                jnp.where(level < depth[c], cells[c], 0.0) - divergence_y(sides[c], cells[c])
                for c in range(2)
            ]
            cross[v * levels + k] = kept[0] - flux
            raw[v * levels + k] = cells[0]
            mate[v * levels + k] = kept[1] + flux
            mate_raw[v * levels + k] = cells[1]
        flow_in[k] = flow[0]
        mate_flow[k] = flow[1]
        return carry

    lax.fori_loop(0, levels, body, 0, unroll=steps(levels, 10))


def wrap(pole, width):
    for v in range(VECTORS):
        pole[v, 0] = pole[v, width]
        pole[v, width + 1] = pole[v, 1]


def spread(pole, face_x, face_y, face_z, v, x):
    west, centre, east = (pole[v, x + j] for j in range(3))
    return (face_x[x + 1] * (east - centre) - face_x[x] * (centre - west)) + (
        face_y[x] * (next_row(centre) - centre) - face_z[x] * (centre - prior_row(centre))
    )


def halo_kernel(
    levels, sub, raw, cross, mate, mate_raw, flow_in, mate_flow,
    raw_far, mate_far, mate_raw_far, mate_flow_far, flow_half, flow_other, merid,
    done, base, weight, sums, powers, flow_far,
):
    outer, inner, sign = orientation()
    start, part = share(levels)

    def unpack(i, carry):
        flow_far[start + i] = flow_half[i]
        flow_far[levels - part - start + i] = flow_other[i]
        return carry

    lax.fori_loop(0, part, unpack, 0, unroll=steps(part, 10))
    powers_of_heights(levels, mate_flow, mate_flow_far, raw_far, powers)
    near, far = (raw, mate_raw), (raw_far, mate_raw_far)
    rim = levels + DEPTHS
    depth = [mate_flow[rim + where] for where in (outer, inner)]
    beside = [
        jnp.minimum(depth[0], raw_far[VECTORS * levels + DEPTHS + inner]),
        jnp.minimum(depth[1], mate_flow_far[rim + outer]),
    ]
    between = jnp.minimum(*depth)
    along = [side_depths(d) for d in depth]
    zero = jnp.zeros_like(between)

    def body(k, carry):
        level = k.astype(jnp.float32)
        flow = [flow_in[k], mate_flow[k]]
        beyond = [flow_far[k], mate_flow_far[k]]
        turn = [merid[k, pl.ds(where, sub, stride=2), :] for where in (outer, inner)]
        middle = face_pair(level, between, -sign * (flow[0] + flow[1]))
        edges = [
            face_pair(level, beside[c], (sign, -sign)[c] * (flow[c] + beyond[c])) for c in range(2)
        ]
        sides = [side_pairs(level, along[c], turn[c]) for c in range(2)]
        weight[k] = edges[0][1]
        totals, grams = list(carry[:VECTORS]), list(carry[VECTORS:])
        fresh = []
        for v in range(VECTORS):
            row = v * levels + k
            flux = [outflow(edges[c], near[c][row], far[c][row]) for c in range(2)]
            outside, inside = cross[row] - flux[0], mate[row] - flux[1]
            other = mate_far[row] + flux[1]
            crossing = outflow(middle, outside, inside)
            base[v, k] = (
                outside
                - outflow(edges[0], outside, flux[0])
                - crossing
                - divergence_y(sides[0], outside)
            )
            value = (
                inside - outflow(edges[1], inside, other) + crossing - divergence_y(sides[1], inside)
            )
            done[v, k] = value
            totals[v] = totals[v] + value
            fresh.append(value)
        return (*totals, *add_products(grams, *fresh))

    found = lax.fori_loop(0, levels, body, (zero,) * (VECTORS + 3), unroll=steps(levels, 10))
    for row, tile in enumerate(found):
        sums[row] = tile


def interleave_kernel(levels, sub, column, done, tracer):
    outer, inner, _ = orientation()

    def body(k, carry):
        for v in range(VECTORS):
            tracer[v, k, pl.ds(outer, sub, stride=2), :] = column[v, k]
            tracer[v, k, pl.ds(inner, sub, stride=2), :] = done[v, k]
        return carry

    lax.fori_loop(0, levels, body, 0, unroll=steps(levels, 10))


def add_products(grams, a, b):
    return [grams[0] + a * a, grams[1] + a * b, grams[2] + b * b]


def second_kernel(levels, cross_far, base, weight, inside, powers, mate_flow, column, message):
    outer, inner, _ = orientation()
    zero = jnp.zeros(powers.shape[-2:], jnp.float32)

    def body(k, carry):
        totals, fresh = [], []
        for v in range(VECTORS):
            value = base[v, k] - weight[k] * cross_far[v * levels + k]
            column[v, k] = value
            totals.append(carry[v] + value)
            fresh.append(value)
        return (*totals, *add_products(carry[VECTORS:], *fresh))

    carry = lax.fori_loop(0, levels, body, (zero,) * (VECTORS + 3), unroll=steps(levels, 10))
    gain = STERIC_GAIN / levels
    rows = [a + inside[VECTORS + n] for n, a in enumerate(carry[VECTORS:])]
    residual = []
    for v in range(VECTORS):
        residual.append(
            [gain * total_of + powers[POWERS, v, c] for c, total_of in enumerate((carry[v], inside[v]))]
        )
        for c, where in enumerate((outer, inner)):
            message[v * 2 + where] = residual[v][c]

    def product(one, two):
        return one[0] * two[0] + one[1] * two[1]

    heights = [[powers[0, v, c] for c in range(2)] for v in range(VECTORS)]
    for n, (i, j) in enumerate(((0, 0), (0, 1), (1, 1))):
        rows[n] = rows[n] + product(heights[i], heights[j])
    for i in range(VECTORS):
        for j in range(VECTORS):
            for m in range(POWERS):
                rows.append(product([powers[m, i, c] for c in range(2)], residual[j]))
    message[GRAMS] = pack_rows(rows)
    for c in range(2):
        message[DEPTHS + c] = mate_flow[levels + DEPTHS + c]


def pack_rows(tiles):
    shape = tiles[0].shape
    sub, lane = (lax.broadcasted_iota(jnp.int32, shape, axis) for axis in (0, 1))
    half = shape[1] // 2
    packed = jnp.zeros(shape, jnp.float32)
    for n, tile in enumerate(tiles):
        row = jnp.sum(tile, axis=0, keepdims=True)
        row = row + pltpu.roll(row, half, 1)
        place = (sub == n % shape[0]) & ((lane < half) == (n < shape[0]))
        packed = jnp.where(place, row, packed)
    return packed


def unpack_rows(packed, count):
    lane = lax.broadcasted_iota(jnp.int32, packed.shape, 1)
    low = lane < packed.shape[1] // 2
    sums = [
        jnp.sum(jnp.where(side, packed, 0.0), axis=1, keepdims=True)
        for side in (low, jnp.logical_not(low))
    ]
    size = packed.shape[0]
    return [sums[n // size][n % size : n % size + 1] for n in range(count)]


def powers_of_heights(levels, mate_flow, mate_flow_far, raw_far, powers):
    outer, inner, _ = orientation()
    line = [
        (mate_flow_far, levels, inner),
        (mate_flow_far, levels, outer),
        (mate_flow, levels, inner),
        (mate_flow, levels, outer),
        (raw_far, VECTORS * levels, inner),
        (raw_far, VECTORS * levels, outer),
    ]
    depth = [ref[base + DEPTHS + where] for ref, base, where in line]
    faces = [SURFACE_COUPLING * jnp.minimum(a, b) for a, b in zip(depth, depth[1:])]
    sides = [side_depths(SURFACE_COUPLING * d) for d in depth[1:5]]
    for v in range(VECTORS):
        field = [
            jnp.where(d > 0, ref[base + v * 2 + where], 0.0)
            for d, (ref, base, where) in zip(depth, line)
        ]

        def bend(field, first, last):
            found = []
            for j in range(first, last):
                west, centre, east = field[j - 1 : j + 2]
                north, south = sides[j - 1]
                found.append(
                    (faces[j] * (east - centre) - faces[j - 1] * (centre - west))
                    + (north * (next_row(centre) - centre) - south * (centre - prior_row(centre)))
                )
            return found

        lap = bend(field, 1, 5)
        image = [None] + [h - p for h, p in zip(field[1:5], lap)]
        again = [p - q for p, q in zip(image[2:4], bend(image, 2, 4))]
        for c, where in enumerate((3, 2)):
            powers[0, v, c] = field[where]
            powers[1, v, c] = image[where]
            powers[2, v, c] = again[where - 2]
            powers[POWERS, v, c] = lap[where - 1]


def total(tile):
    return jnp.sum(jnp.sum(tile, axis=0, keepdims=True), axis=1, keepdims=True)


def combine(one, factor, two):
    longest = max(len(one), len(two))
    one, two = (list(c) + [0.0] * (longest - len(c)) for c in (one, two))
    return [a + factor * b for a, b in zip(one, two)]


def third_kernel(
    levels, sub, count, pair, fetched, fetched_mate, surface, tracer,
    tracer_hbm, surface_out, growth, scaled, sems, pole, residual, answer, image, depth, face_x, face_y, face_z, packed,
):
    width = 2 * count
    me = lax.axis_index("lon")
    core = lax.rem(me, 2)
    zero = jnp.zeros((sub, LANES), jnp.float32)
    none = (zero,) * VECTORS

    def place(owner, block):
        packed[owner] = block(GRAMS)
        for c in range(2):
            x = 2 * owner + c
            depth[x] = block(DEPTHS + c)
            for v in range(VECTORS):
                value = block(v * 2 + c)
                residual[v, x] = value
                pole[v, x + 1] = value

    for slot in range(2):
        place(me ^ slot, lambda row, slot=slot: pair[slot, row])
    for ref, flip in ((fetched, 0), (fetched_mate, 1)):
        for j, masks in enumerate(chip_masks(count)):
            mask = jnp.where((core ^ flip) == 0, *masks)
            for slot in range(2):
                owner = me ^ flip ^ slot ^ (2 * mask)

                def put(owner=owner, ref=ref, j=j, slot=slot):
                    place(owner, lambda row: ref[j, slot, row])

                if all(masks):
                    put()
                else:
                    pl.when(mask > 0)(put)

    def over(body, init):
        return lax.fori_loop(0, count, body, init, unroll=steps(count, 16))

    def each(d):
        return [(v, c, 2 * d + c) for v in range(VECTORS) for c in range(2)]

    def prepare(d, carry):
        for x in (2 * d, 2 * d + 1):
            here, after = depth[x], depth[lax.rem(x + 1, width)]
            face_x[x + 1] = SURFACE_COUPLING * jnp.minimum(here, after)
            north, south = side_depths(here)
            face_y[x] = SURFACE_COUPLING * north
            face_z[x] = SURFACE_COUPLING * south
        return carry

    over(prepare, 0)
    face_x[0] = face_x[width]
    wrap(pole, width)

    def start(d, carry):
        sums = list(carry)
        for v, _, x in each(d):
            sums[v] = sums[v] + residual[v, x] * residual[v, x]
        return tuple(sums)

    norm = [total(t) for t in over(start, none)]
    taken, left, aim = ([[v for _ in range(VECTORS)] for v in ([], [1.0], [1.0])])

    def apply(d, carry):
        sums = list(carry)
        for v, _, x in each(d):
            centre = pole[v, x + 1]
            value = centre - spread(pole, face_x, face_y, face_z, v, x)
            image[v, x] = value
            sums[v] = sums[v] + centre * value
        return tuple(sums)

    for iteration in range(ITERS):
        energy = [total(t) for t in over(apply, none)]
        size = [n / e for n, e in zip(norm, energy)]
        taken = [combine(s, z, a) for s, z, a in zip(taken, size, aim)]
        if iteration + 1 < ITERS:

            def advance(d, carry, size=size, first=iteration == 0):
                sums = list(carry)
                for v, _, x in each(d):
                    gone = size[v] * pole[v, x + 1]
                    answer[v, x] = gone if first else answer[v, x] + gone
                    value = residual[v, x] - size[v] * image[v, x]
                    residual[v, x] = value
                    sums[v] = sums[v] + value * value
                return tuple(sums)

            fresh = [total(t) for t in over(advance, none)]
            ratio = [f / n for f, n in zip(fresh, norm)]
            left = [combine(l, -z, [0.0] + a) for l, z, a in zip(left, size, aim)]
            aim = [combine(l, q, a) for l, q, a in zip(left, ratio, aim)]

            def turn(d, carry, ratio=ratio):
                for v, _, x in each(d):
                    pole[v, x + 1] = residual[v, x] + ratio[v] * pole[v, x + 1]
                return carry

            over(turn, 0)
            wrap(pole, width)
            norm = fresh

    def finish(d, carry):
        grams = list(carry)
        for x in (2 * d, 2 * d + 1):
            a, b = (answer[v, x] + size[v] * pole[v, x + 1] for v in range(VECTORS))
            answer[0, x], answer[1, x] = a, b
            grams = [grams[0] + a * a, grams[1] + a * b, grams[2] + b * b]
        return (*grams, carry[3] + packed[d])

    *grams, packed_sums = over(finish, (zero,) * 4)
    sums = unpack_rows(packed_sums, 3 + VECTORS * VECTORS * POWERS)

    def heights_with(i, j):
        first = 3 + (i * VECTORS + j) * POWERS
        return sum(c * t for c, t in zip(taken[j], sums[first : first + POWERS]))

    cells = (levels + 1) * width * sub * LANES
    one, mix, two = (
        (sums[n] + total(grams[n]) + (heights_with(i, j) + heights_with(j, i))) / cells
        for n, (i, j) in enumerate(((0, 0), (0, 1), (1, 1)))
    )
    scale_one = jnp.sqrt(one + EPSILON)
    cross = mix / scale_one
    rest = two - 2.0 * cross * cross + cross * cross * one / (one + EPSILON)
    scale_two = jnp.sqrt(rest + EPSILON)
    over_one, over_two = 1.0 / scale_one, 1.0 / scale_two

    chunk = steps(levels, 10)
    departures = []

    def scale(k, carry):
        unit = tracer[0, k] * over_one
        scaled[0, k] = unit
        scaled[1, k] = (tracer[1, k] - cross * unit) * over_two
        return carry

    for n in range(levels // chunk):
        lax.fori_loop(n * chunk, (n + 1) * chunk, scale, 0, unroll=chunk)
        rows = pl.ds(n * chunk, chunk)
        departure = pltpu.make_async_copy(scaled.at[:, rows], tracer_hbm.at[:, rows], sems.at[n])
        departure.start()
        departures.append(departure)
    for c in range(2):
        x = 2 * me + c
        first, second = (
            jnp.where(depth[x] > 0, surface[v, pl.ds(c, sub, stride=2), :], 0.0) + answer[v, x]
            for v in range(VECTORS)
        )
        unit = first * over_one
        surface_out[0, pl.ds(c, sub, stride=2), :] = unit
        surface_out[1, pl.ds(c, sub, stride=2), :] = (second - cross * unit) * over_two
    for i, value in enumerate((scale_one, cross, scale_two)):
        growth[i] = value[0, 0]
    for departure in departures:
        departure.wait()


def tiled(array):
    *lead, columns, rows = array.shape
    split = array.reshape(*lead, columns, rows // LANES, LANES)
    return jnp.swapaxes(split, -3, -2).reshape(*lead, rows // LANES * columns, LANES)


def untiled(array, columns):
    *lead, high, lanes = array.shape
    split = array.reshape(*lead, high // columns, columns, lanes)
    return jnp.swapaxes(split, -3, -2).reshape(*lead, columns, high // columns * lanes)


def swap(array, mask):
    count = lax.axis_size("lon")
    return lax.ppermute(array, "lon", [(i, i ^ mask) for i in range(count)])


def chip_masks(count):
    lists, loads = ([], []), [0, 0]
    for mask in range(count // 2 - 1, 0, -1):
        core = int(loads[1] < loads[0])
        lists[core].append(mask)
        loads[core] += mask % 2 + mask // 2
    longest = max(map(len, lists))
    return list(zip(*(one + [0] * (longest - len(one)) for one in lists)))


def gather(block):
    count = lax.axis_size("lon")
    pair = jnp.stack([block, swap(block, 1)])
    fetched = []
    for masks in chip_masks(count):
        moves = [(i, i ^ (2 * masks[i % 2])) for i in range(count) if masks[i % 2]]
        fetched.append(lax.ppermute(pair, "lon", moves))
    fetched = jnp.stack(fetched)
    return pair, fetched, swap(fetched, 1)


def on_device(tracer_pert, surface_pert, zonal_flow, merid_flow, bottom_level):
    vectors, levels, columns, rows = tracer_pert.shape
    count = lax.axis_size("lon")
    sub = rows // LANES
    assert vectors == VECTORS and columns == 2 and rows % LANES == 0
    assert count >= 8 and count & (count - 1) == 0
    width = 2 * count
    f32 = jnp.float32
    vmem = pl.BlockSpec(memory_space=pltpu.VMEM)
    hbm = pl.BlockSpec(memory_space=pltpu.HBM)
    params = pltpu.CompilerParams(vmem_limit_bytes=24 * 2**20)

    def shaped(*shape):
        return jax.ShapeDtypeStruct((*shape, sub, LANES), f32)

    def held(*shape):
        return pltpu.VMEM((*shape, sub, LANES), f32)

    both = pltpu.VMEM((vectors, levels, sub * 2, LANES), f32)
    tracer_pert, zonal_flow, merid_flow = map(tiled, (tracer_pert, zonal_flow, merid_flow))
    outward = [(i, (i + 1) % count if i % 2 else (i - 1) % count) for i in range(count)]
    part = levels // 2
    surface, bottom = tiled(surface_pert), tiled(bottom_level)

    packed = shaped(VECTORS * levels + RIM), shaped(part)
    edge, flow_edge = pl.pallas_call(
        functools.partial(edge_kernel, levels, sub),
        out_shape=packed,
        in_specs=[hbm] * 4,
        out_specs=(hbm, hbm),
        scratch_shapes=[
            both,
            pltpu.VMEM((part, sub * 2, LANES), f32),
            pltpu.VMEM((vectors, sub * 2, LANES), f32),
            pltpu.VMEM((sub * 2, LANES), jnp.int32),
            held(VECTORS * levels + RIM),
            held(part),
            pltpu.SemaphoreType.DMA((VECTORS + 3,)),
            pltpu.SemaphoreType.DMA((VECTORS + 1,)),
        ],
        compiler_params=pltpu.CompilerParams(vmem_limit_bytes=60 * 2**20),
        name="edge_columns",
    )(tracer_pert, zonal_flow, surface, bottom)
    flow_half = lax.ppermute(flow_edge, "lon", outward)
    edge_far = lax.ppermute(edge, "lon", outward)
    flow_other = lax.ppermute(flow_half, "grp", [(0, 1), (1, 0)])
    cross, mate, raw, mate_raw, flow_in, mate_flow = pl.pallas_call(
        functools.partial(first_kernel, levels, sub),
        out_shape=(
            shaped(VECTORS * levels),
            shaped(VECTORS * levels),
            shaped(VECTORS * levels),
            shaped(VECTORS * levels),
            shaped(levels),
            shaped(levels + RIM),
        ),
        in_specs=[pl.BlockSpec(memory_space=pl.ANY)] + [vmem] * 5,
        out_specs=(vmem,) * 6,
        compiler_params=params,
        name="partial_step",
    )(edge, tracer_pert, zonal_flow, merid_flow, surface, bottom)
    cross_far = lax.ppermute(cross, "lon", outward)
    mate_far, mate_raw_far, mate_flow_far = (swap(x, 1) for x in (mate, mate_raw, mate_flow))
    done, *rest = pl.pallas_call(
        functools.partial(halo_kernel, levels, sub),
        out_shape=(
            shaped(vectors, levels),
            shaped(vectors, levels),
            shaped(levels),
            shaped(VECTORS + 3),
            shaped(POWERS + 1, vectors, 2),
        ),
        in_specs=[vmem] * 13,
        out_specs=(vmem,) * 5,
        scratch_shapes=[held(levels)],
        compiler_params=params,
        name="both_steps",
    )(
        raw, cross, mate, mate_raw, flow_in, mate_flow,
        edge_far, mate_far, mate_raw_far, mate_flow_far, flow_half, flow_other, merid_flow,
    )
    column, message = pl.pallas_call(
        functools.partial(second_kernel, levels),
        out_shape=(shaped(vectors, levels), shaped(BLOCKS)),
        in_specs=[vmem] * 6,
        out_specs=(vmem, vmem),
        compiler_params=params,
        name="outer_column",
    )(cross_far, *rest, mate_flow)
    tracer = pl.pallas_call(
        functools.partial(interleave_kernel, levels, sub),
        out_shape=jax.ShapeDtypeStruct((vectors, levels, sub * 2, LANES), f32),
        in_specs=[vmem] * 2,
        out_specs=vmem,
        compiler_params=params,
        name="interleave",
    )(column, done)
    tracer_vec, surface_vec, growth = pl.pallas_call(
        functools.partial(third_kernel, levels, sub, count),
        out_shape=(
            jax.ShapeDtypeStruct((vectors, levels, sub * 2, LANES), f32),
            jax.ShapeDtypeStruct((vectors, sub * 2, LANES), f32),
            jax.ShapeDtypeStruct((3,), f32),
        ),
        in_specs=[vmem] * 5,
        out_specs=(hbm, vmem, pl.BlockSpec(memory_space=pltpu.SMEM)),
        scratch_shapes=[
            both,
            pltpu.SemaphoreType.DMA((levels // steps(levels, 10),)),
            held(vectors, width + 2),
            *[held(vectors, width)] * 3,
            held(width),
            held(width + 1),
            held(width),
            held(width),
            held(count),
        ],
        compiler_params=pltpu.CompilerParams(vmem_limit_bytes=32 * 2**20),
        name="surface_and_scale",
    )(*gather(message), surface, tracer)
    return (untiled(tracer_vec, 2), untiled(surface_vec, 2), growth)


def solution(mesh):
    placed = (
        P("grp", None, "lon", None),
        P("grp", "lon", None),
        P(None, "lon", None),
        P(None, "lon", None),
        P("lon", None),
    )
    return jax.shard_map(
        on_device,
        mesh=mesh,
        in_specs=placed,
        out_specs=(P("grp", None, "lon", None), P("grp", "lon", None), P("grp")),
        check_vma=False,
    )
```

```python
import functools

import jax
import jax.numpy as jnp
from jax import lax
from jax.experimental import pallas as pl
from jax.experimental.pallas import tpu as pltpu
from jax.sharding import PartitionSpec as P

ITERS = 3


DIFFUSIVITY = 0.5
TIME_STEP = 0.2
SURFACE_COUPLING = 0.5
STERIC_GAIN = 2.0
EPSILON = 1e-06

LANES = 128
VECTORS = 2
SLOPE = 0.25 * TIME_STEP
SPREAD = TIME_STEP * DIFFUSIVITY
DEPTHS = VECTORS * 2
RIM = DEPTHS + 2
GRAMS = RIM
BLOCKS = GRAMS + 1
POWERS = ITERS


def next_row(tile):
    turned = pltpu.roll(tile, LANES - 1, 1)
    carried = pltpu.roll(turned, tile.shape[0] - 1, 0)
    lane = lax.broadcasted_iota(jnp.int32, tile.shape, 1)
    return jnp.where(lane == LANES - 1, carried, turned)


def prior_row(tile):
    turned = pltpu.roll(tile, 1, 1)
    carried = pltpu.roll(turned, 1, 0)
    lane = lax.broadcasted_iota(jnp.int32, tile.shape, 1)
    return jnp.where(lane == 0, carried, turned)


def wall_depth(depth):
    subs, lane = (lax.broadcasted_iota(jnp.int32, depth.shape, axis) for axis in (0, 1))
    last = (subs == depth.shape[0] - 1) & (lane == LANES - 1)
    return jnp.where(last, jnp.zeros_like(depth), jnp.minimum(depth, next_row(depth)))


def face_pair(level, face_depth, flow_sum):
    slope = SLOPE * flow_sum
    open_face = level < face_depth
    return (
        jnp.where(open_face, slope + SPREAD, 0.0),
        jnp.where(open_face, slope - SPREAD, 0.0),
    )


def outflow(pair, near, far):
    return pair[0] * near + pair[1] * far


def side_pairs(level, depths, flow):
    return (
        face_pair(level, depths[0], flow + next_row(flow)),
        face_pair(level, depths[1], -(flow + prior_row(flow))),
    )


def divergence_y(pairs, tile):
    return outflow(pairs[0], tile, next_row(tile)) + outflow(pairs[1], tile, prior_row(tile))


def side_depths(depth):
    north = wall_depth(depth)
    return north, prior_row(north)


def orientation():
    outer = lax.rem(lax.axis_index("lon"), 2)
    return outer, 1 - outer, (2 * outer - 1).astype(jnp.float32)


def steps(count, most):
    return max(u for u in range(1, most + 1) if count % u == 0)


def share(levels):
    assert lax.axis_size("grp") == 2 and levels % 2 == 0
    part = levels // 2
    return lax.axis_index("grp") * (levels - part), part


def pack_rim(sub, surface, bottom, target, base):
    for c in range(2):
        for v in range(VECTORS):
            target[base + v * 2 + c] = surface[v, pl.ds(c, sub, stride=2), :]
        target[base + DEPTHS + c] = bottom[pl.ds(c, sub, stride=2), :].astype(jnp.float32)


def move(source, target, sem):
    copy = pltpu.make_async_copy(source, target, sem)
    copy.start()
    return copy


def flow_kernel(levels, sub, zonal_hbm, flow, zonal, sem):
    outer, _, _ = orientation()
    start, part = share(levels)
    move(zonal_hbm.at[pl.ds(start, part)], zonal, sem).wait()

    def body(k, carry):
        flow[k] = zonal[k, pl.ds(outer, sub, stride=2), :]
        return carry

    lax.fori_loop(0, part, body, 0, unroll=part)


def edge_kernel(
    levels, sub, flow, tracer_hbm, surface_hbm, bottom_hbm, edge_hbm,
    tracer, surface, bottom, edge, sems_in, sems_out,
):
    del flow
    outer, _, _ = orientation()
    small = [move(surface_hbm, surface, sems_in.at[0]), move(bottom_hbm, bottom, sems_in.at[1])]
    arrivals = [move(tracer_hbm.at[v], tracer.at[v], sems_in.at[2 + v]) for v in range(VECTORS)]
    for copy in small:
        copy.wait()
    pack_rim(sub, surface, bottom, edge, VECTORS * levels)
    departures = []
    for v, arrival in enumerate(arrivals):
        arrival.wait()

        def body(k, carry, v=v):
            edge[v * levels + k] = tracer[v, k, pl.ds(outer, sub, stride=2), :]
            return carry

        lax.fori_loop(0, levels, body, 0, unroll=steps(levels, 10))
        rows = pl.ds(v * levels, levels + (RIM if v == VECTORS - 1 else 0))
        departures.append(move(edge.at[rows], edge_hbm.at[rows], sems_out.at[v]))
    for departure in departures:
        departure.wait()


def first_kernel(
    levels, sub, edge, tracer, zonal, merid, surface, bottom,
    cross, mate, raw, mate_raw, flow_in, mate_flow,
):
    del edge
    outer, inner, sign = orientation()

    def column(ref, where, *lead):
        return ref[(*lead, pl.ds(where, sub, stride=2), slice(None))]

    depth = [column(bottom, where).astype(jnp.float32) for where in (outer, inner)]
    between = jnp.minimum(*depth)
    along = [side_depths(d) for d in depth]
    pack_rim(sub, surface, bottom, mate_flow, levels)

    def body(k, carry):
        level = k.astype(jnp.float32)
        flow = [column(zonal, where, k) for where in (outer, inner)]
        turn = [column(merid, where, k) for where in (outer, inner)]
        middle = face_pair(level, between, -sign * (flow[0] + flow[1]))
        sides = [side_pairs(level, along[c], turn[c]) for c in range(2)]
        for v in range(VECTORS):
            cells = [column(tracer, where, v, k) for where in (outer, inner)]
            flux = outflow(middle, *cells)
            kept = [
                jnp.where(level < depth[c], cells[c], 0.0) - divergence_y(sides[c], cells[c])
                for c in range(2)
            ]
            cross[v * levels + k] = kept[0] - flux
            raw[v * levels + k] = cells[0]
            mate[v * levels + k] = kept[1] + flux
            mate_raw[v * levels + k] = cells[1]
        flow_in[k] = flow[0]
        mate_flow[k] = flow[1]
        return carry

    lax.fori_loop(0, levels, body, 0, unroll=steps(levels, 10))


def wrap(pole, width):
    for v in range(VECTORS):
        pole[v, 0] = pole[v, width]
        pole[v, width + 1] = pole[v, 1]


def spread(pole, face_x, face_y, face_z, v, x):
    west, centre, east = (pole[v, x + j] for j in range(3))
    return (face_x[x + 1] * (east - centre) - face_x[x] * (centre - west)) + (
        face_y[x] * (next_row(centre) - centre) - face_z[x] * (centre - prior_row(centre))
    )


def halo_kernel(
    levels, sub, raw, cross, mate, mate_raw, flow_in, mate_flow,
    raw_far, mate_far, mate_raw_far, mate_flow_far, flow_half, flow_other, merid,
    done, base, weight, sums, powers, flow_far,
):
    outer, inner, sign = orientation()
    start, part = share(levels)

    def unpack(i, carry):
        flow_far[start + i] = flow_half[i]
        flow_far[levels - part - start + i] = flow_other[i]
        return carry

    lax.fori_loop(0, part, unpack, 0, unroll=steps(part, 10))
    powers_of_heights(levels, mate_flow, mate_flow_far, raw_far, powers)
    near, far = (raw, mate_raw), (raw_far, mate_raw_far)
    rim = levels + DEPTHS
    depth = [mate_flow[rim + where] for where in (outer, inner)]
    beside = [
        jnp.minimum(depth[0], raw_far[VECTORS * levels + DEPTHS + inner]),
        jnp.minimum(depth[1], mate_flow_far[rim + outer]),
    ]
    between = jnp.minimum(*depth)
    along = [side_depths(d) for d in depth]
    zero = jnp.zeros_like(between)

    def body(k, carry):
        level = k.astype(jnp.float32)
        flow = [flow_in[k], mate_flow[k]]
        beyond = [flow_far[k], mate_flow_far[k]]
        turn = [merid[k, pl.ds(where, sub, stride=2), :] for where in (outer, inner)]
        middle = face_pair(level, between, -sign * (flow[0] + flow[1]))
        edges = [
            face_pair(level, beside[c], (sign, -sign)[c] * (flow[c] + beyond[c])) for c in range(2)
        ]
        sides = [side_pairs(level, along[c], turn[c]) for c in range(2)]
        weight[k] = edges[0][1]
        totals, grams = list(carry[:VECTORS]), list(carry[VECTORS:])
        fresh = []
        for v in range(VECTORS):
            row = v * levels + k
            flux = [outflow(edges[c], near[c][row], far[c][row]) for c in range(2)]
            outside, inside = cross[row] - flux[0], mate[row] - flux[1]
            other = mate_far[row] + flux[1]
            crossing = outflow(middle, outside, inside)
            base[v, k] = (
                outside
                - outflow(edges[0], outside, flux[0])
                - crossing
                - divergence_y(sides[0], outside)
            )
            value = (
                inside - outflow(edges[1], inside, other) + crossing - divergence_y(sides[1], inside)
            )
            done[v, k] = value
            totals[v] = totals[v] + value
            fresh.append(value)
        return (*totals, *add_products(grams, *fresh))

    found = lax.fori_loop(0, levels, body, (zero,) * (VECTORS + 3), unroll=steps(levels, 10))
    for row, tile in enumerate(found):
        sums[row] = tile


def interleave_kernel(levels, sub, column, done, tracer):
    outer, inner, _ = orientation()

    def body(k, carry):
        for v in range(VECTORS):
            tracer[v, k, pl.ds(outer, sub, stride=2), :] = column[v, k]
            tracer[v, k, pl.ds(inner, sub, stride=2), :] = done[v, k]
        return carry

    lax.fori_loop(0, levels, body, 0, unroll=steps(levels, 10))


def add_products(grams, a, b):
    return [grams[0] + a * a, grams[1] + a * b, grams[2] + b * b]


def second_kernel(levels, cross_far, base, weight, inside, powers, mate_flow, column, message):
    outer, inner, _ = orientation()
    zero = jnp.zeros(powers.shape[-2:], jnp.float32)

    def body(k, carry):
        totals, fresh = [], []
        for v in range(VECTORS):
            value = base[v, k] - weight[k] * cross_far[v * levels + k]
            column[v, k] = value
            totals.append(carry[v] + value)
            fresh.append(value)
        return (*totals, *add_products(carry[VECTORS:], *fresh))

    carry = lax.fori_loop(0, levels, body, (zero,) * (VECTORS + 3), unroll=steps(levels, 10))
    gain = STERIC_GAIN / levels
    rows = [a + inside[VECTORS + n] for n, a in enumerate(carry[VECTORS:])]
    residual = []
    for v in range(VECTORS):
        residual.append(
            [gain * total_of + powers[POWERS, v, c] for c, total_of in enumerate((carry[v], inside[v]))]
        )
        for c, where in enumerate((outer, inner)):
            message[v * 2 + where] = residual[v][c]

    def product(one, two):
        return one[0] * two[0] + one[1] * two[1]

    heights = [[powers[0, v, c] for c in range(2)] for v in range(VECTORS)]
    for n, (i, j) in enumerate(((0, 0), (0, 1), (1, 1))):
        rows[n] = rows[n] + product(heights[i], heights[j])
    for i in range(VECTORS):
        for j in range(VECTORS):
            for m in range(POWERS):
                rows.append(product([powers[m, i, c] for c in range(2)], residual[j]))
    message[GRAMS] = pack_rows(rows)
    for c in range(2):
        message[DEPTHS + c] = mate_flow[levels + DEPTHS + c]


def pack_rows(tiles):
    shape = tiles[0].shape
    sub, lane = (lax.broadcasted_iota(jnp.int32, shape, axis) for axis in (0, 1))
    half = shape[1] // 2
    packed = jnp.zeros(shape, jnp.float32)
    for n, tile in enumerate(tiles):
        row = jnp.sum(tile, axis=0, keepdims=True)
        row = row + pltpu.roll(row, half, 1)
        place = (sub == n % shape[0]) & ((lane < half) == (n < shape[0]))
        packed = jnp.where(place, row, packed)
    return packed


def unpack_rows(packed, count):
    lane = lax.broadcasted_iota(jnp.int32, packed.shape, 1)
    low = lane < packed.shape[1] // 2
    sums = [
        jnp.sum(jnp.where(side, packed, 0.0), axis=1, keepdims=True)
        for side in (low, jnp.logical_not(low))
    ]
    size = packed.shape[0]
    return [sums[n // size][n % size : n % size + 1] for n in range(count)]


def powers_of_heights(levels, mate_flow, mate_flow_far, raw_far, powers):
    outer, inner, _ = orientation()
    line = [
        (mate_flow_far, levels, inner),
        (mate_flow_far, levels, outer),
        (mate_flow, levels, inner),
        (mate_flow, levels, outer),
        (raw_far, VECTORS * levels, inner),
        (raw_far, VECTORS * levels, outer),
    ]
    depth = [ref[base + DEPTHS + where] for ref, base, where in line]
    faces = [SURFACE_COUPLING * jnp.minimum(a, b) for a, b in zip(depth, depth[1:])]
    sides = [side_depths(SURFACE_COUPLING * d) for d in depth[1:5]]
    for v in range(VECTORS):
        field = [
            jnp.where(d > 0, ref[base + v * 2 + where], 0.0)
            for d, (ref, base, where) in zip(depth, line)
        ]

        def bend(field, first, last):
            found = []
            for j in range(first, last):
                west, centre, east = field[j - 1 : j + 2]
                north, south = sides[j - 1]
                found.append(
                    (faces[j] * (east - centre) - faces[j - 1] * (centre - west))
                    + (north * (next_row(centre) - centre) - south * (centre - prior_row(centre)))
                )
            return found

        lap = bend(field, 1, 5)
        image = [None] + [h - p for h, p in zip(field[1:5], lap)]
        again = [p - q for p, q in zip(image[2:4], bend(image, 2, 4))]
        for c, where in enumerate((3, 2)):
            powers[0, v, c] = field[where]
            powers[1, v, c] = image[where]
            powers[2, v, c] = again[where - 2]
            powers[POWERS, v, c] = lap[where - 1]


def total(tile):
    return jnp.sum(jnp.sum(tile, axis=0, keepdims=True), axis=1, keepdims=True)


def combine(one, factor, two):
    longest = max(len(one), len(two))
    one, two = (list(c) + [0.0] * (longest - len(c)) for c in (one, two))
    return [a + factor * b for a, b in zip(one, two)]


def third_kernel(
    levels, sub, count, pair, fetched, fetched_mate, surface, tracer,
    scaled, surface_out, growth, pole, residual, answer, image, depth, face_x, face_y, face_z, packed,
):
    width = 2 * count
    me = lax.axis_index("lon")
    core = lax.rem(me, 2)
    zero = jnp.zeros((sub, LANES), jnp.float32)
    none = (zero,) * VECTORS

    def place(owner, block):
        packed[owner] = block(GRAMS)
        for c in range(2):
            x = 2 * owner + c
            depth[x] = block(DEPTHS + c)
            for v in range(VECTORS):
                value = block(v * 2 + c)
                residual[v, x] = value
                pole[v, x + 1] = value

    for slot in range(2):
        place(me ^ slot, lambda row, slot=slot: pair[slot, row])
    for ref, flip in ((fetched, 0), (fetched_mate, 1)):
        for j, masks in enumerate(chip_masks(count)):
            mask = jnp.where((core ^ flip) == 0, *masks)
            for slot in range(2):
                owner = me ^ flip ^ slot ^ (2 * mask)

                def put(owner=owner, ref=ref, j=j, slot=slot):
                    place(owner, lambda row: ref[j, slot, row])

                if all(masks):
                    put()
                else:
                    pl.when(mask > 0)(put)

    def over(body, init):
        return lax.fori_loop(0, count, body, init, unroll=steps(count, 16))

    def each(d):
        return [(v, c, 2 * d + c) for v in range(VECTORS) for c in range(2)]

    def prepare(d, carry):
        for x in (2 * d, 2 * d + 1):
            here, after = depth[x], depth[lax.rem(x + 1, width)]
            face_x[x + 1] = SURFACE_COUPLING * jnp.minimum(here, after)
            north, south = side_depths(here)
            face_y[x] = SURFACE_COUPLING * north
            face_z[x] = SURFACE_COUPLING * south
        return carry

    over(prepare, 0)
    face_x[0] = face_x[width]
    wrap(pole, width)

    def start(d, carry):
        sums = list(carry)
        for v, _, x in each(d):
            sums[v] = sums[v] + residual[v, x] * residual[v, x]
        return tuple(sums)

    norm = [total(t) for t in over(start, none)]
    taken, left, aim = ([[v for _ in range(VECTORS)] for v in ([], [1.0], [1.0])])

    def apply(d, carry):
        sums = list(carry)
        for v, _, x in each(d):
            centre = pole[v, x + 1]
            value = centre - spread(pole, face_x, face_y, face_z, v, x)
            image[v, x] = value
            sums[v] = sums[v] + centre * value
        return tuple(sums)

    for iteration in range(ITERS):
        energy = [total(t) for t in over(apply, none)]
        size = [n / e for n, e in zip(norm, energy)]
        taken = [combine(s, z, a) for s, z, a in zip(taken, size, aim)]
        if iteration + 1 < ITERS:

            def advance(d, carry, size=size, first=iteration == 0):
                sums = list(carry)
                for v, _, x in each(d):
                    gone = size[v] * pole[v, x + 1]
                    answer[v, x] = gone if first else answer[v, x] + gone
                    value = residual[v, x] - size[v] * image[v, x]
                    residual[v, x] = value
                    sums[v] = sums[v] + value * value
                return tuple(sums)

            fresh = [total(t) for t in over(advance, none)]
            ratio = [f / n for f, n in zip(fresh, norm)]
            left = [combine(l, -z, [0.0] + a) for l, z, a in zip(left, size, aim)]
            aim = [combine(l, q, a) for l, q, a in zip(left, ratio, aim)]

            def turn(d, carry, ratio=ratio):
                for v, _, x in each(d):
                    pole[v, x + 1] = residual[v, x] + ratio[v] * pole[v, x + 1]
                return carry

            over(turn, 0)
            wrap(pole, width)
            norm = fresh

    def finish(d, carry):
        grams = list(carry)
        for x in (2 * d, 2 * d + 1):
            a, b = (answer[v, x] + size[v] * pole[v, x + 1] for v in range(VECTORS))
            answer[0, x], answer[1, x] = a, b
            grams = [grams[0] + a * a, grams[1] + a * b, grams[2] + b * b]
        return (*grams, carry[3] + packed[d])

    *grams, packed_sums = over(finish, (zero,) * 4)
    sums = unpack_rows(packed_sums, 3 + VECTORS * VECTORS * POWERS)

    def heights_with(i, j):
        first = 3 + (i * VECTORS + j) * POWERS
        return sum(c * t for c, t in zip(taken[j], sums[first : first + POWERS]))

    cells = (levels + 1) * width * sub * LANES
    one, mix, two = (
        (sums[n] + total(grams[n]) + (heights_with(i, j) + heights_with(j, i))) / cells
        for n, (i, j) in enumerate(((0, 0), (0, 1), (1, 1)))
    )
    scale_one = jnp.sqrt(one + EPSILON)
    cross = mix / scale_one
    rest = two - 2.0 * cross * cross + cross * cross * one / (one + EPSILON)
    scale_two = jnp.sqrt(rest + EPSILON)
    over_one, over_two = 1.0 / scale_one, 1.0 / scale_two

    def scale(k, carry):
        unit = tracer[0, k] * over_one
        scaled[0, k] = unit
        scaled[1, k] = (tracer[1, k] - cross * unit) * over_two
        return carry

    lax.fori_loop(0, levels, scale, 0, unroll=steps(levels, 10))
    for c in range(2):
        x = 2 * me + c
        first, second = (
            jnp.where(depth[x] > 0, surface[v, pl.ds(c, sub, stride=2), :], 0.0) + answer[v, x]
            for v in range(VECTORS)
        )
        unit = first * over_one
        surface_out[0, pl.ds(c, sub, stride=2), :] = unit
        surface_out[1, pl.ds(c, sub, stride=2), :] = (second - cross * unit) * over_two
    for i, value in enumerate((scale_one, cross, scale_two)):
        growth[i] = value[0, 0]


def tiled(array):
    *lead, columns, rows = array.shape
    split = array.reshape(*lead, columns, rows // LANES, LANES)
    return jnp.swapaxes(split, -3, -2).reshape(*lead, rows // LANES * columns, LANES)


def untiled(array, columns):
    *lead, high, lanes = array.shape
    split = array.reshape(*lead, high // columns, columns, lanes)
    return jnp.swapaxes(split, -3, -2).reshape(*lead, columns, high // columns * lanes)


def swap(array, mask):
    count = lax.axis_size("lon")
    return lax.ppermute(array, "lon", [(i, i ^ mask) for i in range(count)])


def chip_masks(count):
    lists, loads = ([], []), [0, 0]
    for mask in range(count // 2 - 1, 0, -1):
        core = int(loads[1] < loads[0])
        lists[core].append(mask)
        loads[core] += mask % 2 + mask // 2
    longest = max(map(len, lists))
    return list(zip(*(one + [0] * (longest - len(one)) for one in lists)))


def gather(block):
    count = lax.axis_size("lon")
    pair = jnp.stack([block, swap(block, 1)])
    fetched = []
    for masks in chip_masks(count):
        moves = [(i, i ^ (2 * masks[i % 2])) for i in range(count) if masks[i % 2]]
        fetched.append(lax.ppermute(pair, "lon", moves))
    fetched = jnp.stack(fetched)
    return pair, fetched, swap(fetched, 1)


def on_device(tracer_pert, surface_pert, zonal_flow, merid_flow, bottom_level):
    vectors, levels, columns, rows = tracer_pert.shape
    count = lax.axis_size("lon")
    sub = rows // LANES
    assert vectors == VECTORS and columns == 2 and rows % LANES == 0
    assert count >= 8 and count & (count - 1) == 0
    width = 2 * count
    f32 = jnp.float32
    vmem = pl.BlockSpec(memory_space=pltpu.VMEM)
    hbm = pl.BlockSpec(memory_space=pltpu.HBM)
    params = pltpu.CompilerParams(vmem_limit_bytes=24 * 2**20)

    def shaped(*shape):
        return jax.ShapeDtypeStruct((*shape, sub, LANES), f32)

    def held(*shape):
        return pltpu.VMEM((*shape, sub, LANES), f32)

    both = pltpu.VMEM((vectors, levels, sub * 2, LANES), f32)
    tracer_pert, zonal_flow, merid_flow = map(tiled, (tracer_pert, zonal_flow, merid_flow))
    outward = [(i, (i + 1) % count if i % 2 else (i - 1) % count) for i in range(count)]
    part = levels // 2
    surface, bottom = tiled(surface_pert), tiled(bottom_level)

    first_params = pltpu.CompilerParams(vmem_limit_bytes=60 * 2**20)
    flow_edge = pl.pallas_call(
        functools.partial(flow_kernel, levels, sub),
        out_shape=shaped(part),
        in_specs=[hbm],
        out_specs=vmem,
        scratch_shapes=[pltpu.VMEM((part, sub * 2, LANES), f32), pltpu.SemaphoreType.DMA],
        compiler_params=first_params,
        name="flow_column",
    )(zonal_flow)
    flow_half = lax.ppermute(flow_edge, "lon", outward)
    flow_other = lax.ppermute(flow_half, "grp", [(0, 1), (1, 0)])
    edge = pl.pallas_call(
        functools.partial(edge_kernel, levels, sub),
        out_shape=shaped(VECTORS * levels + RIM),
        in_specs=[pl.BlockSpec(memory_space=pl.ANY)] + [hbm] * 3,
        out_specs=hbm,
        scratch_shapes=[
            both,
            pltpu.VMEM((vectors, sub * 2, LANES), f32),
            pltpu.VMEM((sub * 2, LANES), jnp.int32),
            held(VECTORS * levels + RIM),
            pltpu.SemaphoreType.DMA((VECTORS + 2,)),
            pltpu.SemaphoreType.DMA((VECTORS,)),
        ],
        compiler_params=first_params,
        name="edge_columns",
    )(flow_edge, tracer_pert, surface, bottom)
    edge_far = lax.ppermute(edge, "lon", outward)
    cross, mate, raw, mate_raw, flow_in, mate_flow = pl.pallas_call(
        functools.partial(first_kernel, levels, sub),
        out_shape=(
            shaped(VECTORS * levels),
            shaped(VECTORS * levels),
            shaped(VECTORS * levels),
            shaped(VECTORS * levels),
            shaped(levels),
            shaped(levels + RIM),
        ),
        in_specs=[pl.BlockSpec(memory_space=pl.ANY)] + [vmem] * 5,
        out_specs=(vmem,) * 6,
        compiler_params=params,
        name="partial_step",
    )(edge, tracer_pert, zonal_flow, merid_flow, surface, bottom)
    cross_far = lax.ppermute(cross, "lon", outward)
    mate_far, mate_raw_far, mate_flow_far = (swap(x, 1) for x in (mate, mate_raw, mate_flow))
    done, *rest = pl.pallas_call(
        functools.partial(halo_kernel, levels, sub),
        out_shape=(
            shaped(vectors, levels),
            shaped(vectors, levels),
            shaped(levels),
            shaped(VECTORS + 3),
            shaped(POWERS + 1, vectors, 2),
        ),
        in_specs=[vmem] * 13,
        out_specs=(vmem,) * 5,
        scratch_shapes=[held(levels)],
        compiler_params=params,
        name="both_steps",
    )(
        raw, cross, mate, mate_raw, flow_in, mate_flow,
        edge_far, mate_far, mate_raw_far, mate_flow_far, flow_half, flow_other, merid_flow,
    )
    column, message = pl.pallas_call(
        functools.partial(second_kernel, levels),
        out_shape=(shaped(vectors, levels), shaped(BLOCKS)),
        in_specs=[vmem] * 6,
        out_specs=(vmem, vmem),
        compiler_params=params,
        name="outer_column",
    )(cross_far, *rest, mate_flow)
    tracer = pl.pallas_call(
        functools.partial(interleave_kernel, levels, sub),
        out_shape=jax.ShapeDtypeStruct((vectors, levels, sub * 2, LANES), f32),
        in_specs=[vmem] * 2,
        out_specs=vmem,
        compiler_params=params,
        name="interleave",
    )(column, done)
    tracer_vec, surface_vec, growth = pl.pallas_call(
        functools.partial(third_kernel, levels, sub, count),
        out_shape=(
            jax.ShapeDtypeStruct((vectors, levels, sub * 2, LANES), f32),
            jax.ShapeDtypeStruct((vectors, sub * 2, LANES), f32),
            jax.ShapeDtypeStruct((3,), f32),
        ),
        in_specs=[vmem] * 5,
        out_specs=(vmem, vmem, pl.BlockSpec(memory_space=pltpu.SMEM)),
        scratch_shapes=[
            held(vectors, width + 2),
            *[held(vectors, width)] * 3,
            held(width),
            held(width + 1),
            held(width),
            held(width),
            held(count),
        ],
        compiler_params=pltpu.CompilerParams(vmem_limit_bytes=32 * 2**20),
        name="surface_and_scale",
    )(*gather(message), surface, tracer)
    return (untiled(tracer_vec, 2), untiled(surface_vec, 2), growth)


def solution(mesh):
    placed = (
        P("grp", None, "lon", None),
        P("grp", "lon", None),
        P(None, "lon", None),
        P(None, "lon", None),
        P("lon", None),
    )
    return jax.shard_map(
        on_device,
        mesh=mesh,
        in_specs=placed,
        out_specs=(P("grp", None, "lon", None), P("grp", "lon", None), P("grp")),
        check_vma=False,
    )
```

```python
import functools

import jax
import jax.numpy as jnp
from jax import lax
from jax.experimental import pallas as pl
from jax.experimental.pallas import tpu as pltpu
from jax.sharding import PartitionSpec as P

ITERS = 3


DIFFUSIVITY = 0.5
TIME_STEP = 0.2
SURFACE_COUPLING = 0.5
STERIC_GAIN = 2.0
EPSILON = 1e-06

LANES = 128
VECTORS = 2
SLOPE = 0.25 * TIME_STEP
SPREAD = TIME_STEP * DIFFUSIVITY
DEPTHS = VECTORS * 2
RIM = DEPTHS + 2
GRAMS = RIM
BLOCKS = GRAMS + 1
POWERS = ITERS


def next_row(tile):
    turned = pltpu.roll(tile, LANES - 1, 1)
    carried = pltpu.roll(turned, tile.shape[0] - 1, 0)
    lane = lax.broadcasted_iota(jnp.int32, tile.shape, 1)
    return jnp.where(lane == LANES - 1, carried, turned)


def prior_row(tile):
    turned = pltpu.roll(tile, 1, 1)
    carried = pltpu.roll(turned, 1, 0)
    lane = lax.broadcasted_iota(jnp.int32, tile.shape, 1)
    return jnp.where(lane == 0, carried, turned)


def wall_depth(depth):
    subs, lane = (lax.broadcasted_iota(jnp.int32, depth.shape, axis) for axis in (0, 1))
    last = (subs == depth.shape[0] - 1) & (lane == LANES - 1)
    return jnp.where(last, jnp.zeros_like(depth), jnp.minimum(depth, next_row(depth)))


def face_pair(level, face_depth, flow_sum):
    slope = SLOPE * flow_sum
    open_face = level < face_depth
    return (
        jnp.where(open_face, slope + SPREAD, 0.0),
        jnp.where(open_face, slope - SPREAD, 0.0),
    )


def outflow(pair, near, far):
    return pair[0] * near + pair[1] * far


def side_pairs(level, depths, flow):
    return (
        face_pair(level, depths[0], flow + next_row(flow)),
        face_pair(level, depths[1], -(flow + prior_row(flow))),
    )


def divergence_y(pairs, tile):
    return outflow(pairs[0], tile, next_row(tile)) + outflow(pairs[1], tile, prior_row(tile))


def side_depths(depth):
    north = wall_depth(depth)
    return north, prior_row(north)


def orientation():
    outer = lax.rem(lax.axis_index("lon"), 2)
    return outer, 1 - outer, (2 * outer - 1).astype(jnp.float32)


def steps(count, most):
    return max(u for u in range(1, most + 1) if count % u == 0)


def share(levels):
    assert lax.axis_size("grp") == 2 and levels % 2 == 0
    part = levels // 2
    return lax.axis_index("grp") * (levels - part), part


def pack_rim(sub, surface, bottom, target, base):
    for c in range(2):
        for v in range(VECTORS):
            target[base + v * 2 + c] = surface[v, pl.ds(c, sub, stride=2), :]
        target[base + DEPTHS + c] = bottom[pl.ds(c, sub, stride=2), :].astype(jnp.float32)


def edge_kernel(
    levels, sub, tracer_hbm, zonal_hbm, surface_hbm, bottom_hbm, edge_hbm, flow_hbm,
    tracer, zonal, surface, bottom, edge, flow, sems_in, sems_out,
):
    outer, _, _ = orientation()
    start, part = share(levels)

    def move(source, target, sem):
        copy = pltpu.make_async_copy(source, target, sem)
        copy.start()
        return copy

    first = [
        move(zonal_hbm.at[pl.ds(start, part)], zonal, sems_in.at[0]),
        move(surface_hbm, surface, sems_in.at[1]),
        move(bottom_hbm, bottom, sems_in.at[2]),
    ]
    arrivals = [move(tracer_hbm.at[v], tracer.at[v], sems_in.at[3 + v]) for v in range(VECTORS)]
    for copy in first:
        copy.wait()

    def take(k, carry):
        flow[k] = zonal[k, pl.ds(outer, sub, stride=2), :]
        return carry

    lax.fori_loop(0, part, take, 0, unroll=steps(part, 10))
    departures = [move(flow, flow_hbm, sems_out.at[VECTORS])]
    pack_rim(sub, surface, bottom, edge, VECTORS * levels)
    for v, arrival in enumerate(arrivals):
        arrival.wait()

        def body(k, carry, v=v):
            edge[v * levels + k] = tracer[v, k, pl.ds(outer, sub, stride=2), :]
            return carry

        lax.fori_loop(0, levels, body, 0, unroll=steps(levels, 10))
        rows = pl.ds(v * levels, levels + (RIM if v == VECTORS - 1 else 0))
        departures.append(move(edge.at[rows], edge_hbm.at[rows], sems_out.at[v]))
    for departure in departures:
        departure.wait()


def first_kernel(
    levels, sub, edge, tracer, zonal, merid, surface, bottom,
    cross, mate, raw, mate_raw, flow_in, mate_flow,
):
    del edge
    outer, inner, sign = orientation()

    def column(ref, where, *lead):
        return ref[(*lead, pl.ds(where, sub, stride=2), slice(None))]

    depth = [column(bottom, where).astype(jnp.float32) for where in (outer, inner)]
    between = jnp.minimum(*depth)
    along = [side_depths(d) for d in depth]
    pack_rim(sub, surface, bottom, mate_flow, levels)

    def body(k, carry):
        level = k.astype(jnp.float32)
        flow = [column(zonal, where, k) for where in (outer, inner)]
        turn = [column(merid, where, k) for where in (outer, inner)]
        middle = face_pair(level, between, -sign * (flow[0] + flow[1]))
        sides = [side_pairs(level, along[c], turn[c]) for c in range(2)]
        for v in range(VECTORS):
            cells = [column(tracer, where, v, k) for where in (outer, inner)]
            flux = outflow(middle, *cells)
            kept = [
                jnp.where(level < depth[c], cells[c], 0.0) - divergence_y(sides[c], cells[c])
                for c in range(2)
            ]
            cross[v * levels + k] = kept[0] - flux
            raw[v * levels + k] = cells[0]
            mate[v * levels + k] = kept[1] + flux
            mate_raw[v * levels + k] = cells[1]
        flow_in[k] = flow[0]
        mate_flow[k] = flow[1]
        return carry

    lax.fori_loop(0, levels, body, 0, unroll=steps(levels, 10))


def wrap(pole, width):
    for v in range(VECTORS):
        pole[v, 0] = pole[v, width]
        pole[v, width + 1] = pole[v, 1]


def spread(pole, face_x, face_y, face_z, v, x):
    west, centre, east = (pole[v, x + j] for j in range(3))
    return (face_x[x + 1] * (east - centre) - face_x[x] * (centre - west)) + (
        face_y[x] * (next_row(centre) - centre) - face_z[x] * (centre - prior_row(centre))
    )


def halo_kernel(
    levels, sub, raw, cross, mate, mate_raw, flow_in, mate_flow,
    raw_far, mate_far, mate_raw_far, mate_flow_far, flow_half, flow_other, merid,
    done, base, weight, sums, powers, flow_far,
):
    outer, inner, sign = orientation()
    start, part = share(levels)

    def unpack(i, carry):
        flow_far[start + i] = flow_half[i]
        flow_far[levels - part - start + i] = flow_other[i]
        return carry

    lax.fori_loop(0, part, unpack, 0, unroll=steps(part, 10))
    powers_of_heights(levels, mate_flow, mate_flow_far, raw_far, powers)
    near, far = (raw, mate_raw), (raw_far, mate_raw_far)
    rim = levels + DEPTHS
    depth = [mate_flow[rim + where] for where in (outer, inner)]
    beside = [
        jnp.minimum(depth[0], raw_far[VECTORS * levels + DEPTHS + inner]),
        jnp.minimum(depth[1], mate_flow_far[rim + outer]),
    ]
    between = jnp.minimum(*depth)
    along = [side_depths(d) for d in depth]
    zero = jnp.zeros_like(between)

    def body(k, carry):
        level = k.astype(jnp.float32)
        flow = [flow_in[k], mate_flow[k]]
        beyond = [flow_far[k], mate_flow_far[k]]
        turn = [merid[k, pl.ds(where, sub, stride=2), :] for where in (outer, inner)]
        middle = face_pair(level, between, -sign * (flow[0] + flow[1]))
        edges = [
            face_pair(level, beside[c], (sign, -sign)[c] * (flow[c] + beyond[c])) for c in range(2)
        ]
        sides = [side_pairs(level, along[c], turn[c]) for c in range(2)]
        weight[k] = edges[0][1]
        totals, grams = list(carry[:VECTORS]), list(carry[VECTORS:])
        fresh = []
        for v in range(VECTORS):
            row = v * levels + k
            flux = [outflow(edges[c], near[c][row], far[c][row]) for c in range(2)]
            outside, inside = cross[row] - flux[0], mate[row] - flux[1]
            other = mate_far[row] + flux[1]
            crossing = outflow(middle, outside, inside)
            base[v, k] = (
                outside
                - outflow(edges[0], outside, flux[0])
                - crossing
                - divergence_y(sides[0], outside)
            )
            value = (
                inside - outflow(edges[1], inside, other) + crossing - divergence_y(sides[1], inside)
            )
            done[v, k] = value
            totals[v] = totals[v] + value
            fresh.append(value)
        return (*totals, *add_products(grams, *fresh))

    found = lax.fori_loop(0, levels, body, (zero,) * (VECTORS + 3), unroll=steps(levels, 10))
    for row, tile in enumerate(found):
        sums[row] = tile


def interleave_kernel(levels, sub, column, done, tracer):
    outer, inner, _ = orientation()

    def body(k, carry):
        for v in range(VECTORS):
            tracer[v, k, pl.ds(outer, sub, stride=2), :] = column[v, k]
            tracer[v, k, pl.ds(inner, sub, stride=2), :] = done[v, k]
        return carry

    lax.fori_loop(0, levels, body, 0, unroll=steps(levels, 10))


def add_products(grams, a, b):
    return [grams[0] + a * a, grams[1] + a * b, grams[2] + b * b]


def second_kernel(levels, cross_far, base, weight, inside, powers, mate_flow, column, message):
    outer, inner, _ = orientation()
    zero = jnp.zeros(powers.shape[-2:], jnp.float32)

    def body(k, carry):
        totals, fresh = [], []
        for v in range(VECTORS):
            value = base[v, k] - weight[k] * cross_far[v * levels + k]
            column[v, k] = value
            totals.append(carry[v] + value)
            fresh.append(value)
        return (*totals, *add_products(carry[VECTORS:], *fresh))

    carry = lax.fori_loop(0, levels, body, (zero,) * (VECTORS + 3), unroll=steps(levels, 10))
    gain = STERIC_GAIN / levels
    rows = [a + inside[VECTORS + n] for n, a in enumerate(carry[VECTORS:])]
    residual = []
    for v in range(VECTORS):
        residual.append(
            [gain * total_of + powers[POWERS, v, c] for c, total_of in enumerate((carry[v], inside[v]))]
        )
        for c, where in enumerate((outer, inner)):
            message[v * 2 + where] = residual[v][c]

    def product(one, two):
        return one[0] * two[0] + one[1] * two[1]

    heights = [[powers[0, v, c] for c in range(2)] for v in range(VECTORS)]
    for n, (i, j) in enumerate(((0, 0), (0, 1), (1, 1))):
        rows[n] = rows[n] + product(heights[i], heights[j])
    for i in range(VECTORS):
        for j in range(VECTORS):
            for m in range(POWERS):
                rows.append(product([powers[m, i, c] for c in range(2)], residual[j]))
    message[GRAMS] = pack_rows(rows)
    for c in range(2):
        message[DEPTHS + c] = mate_flow[levels + DEPTHS + c]


def pack_rows(tiles):
    shape = tiles[0].shape
    sub, lane = (lax.broadcasted_iota(jnp.int32, shape, axis) for axis in (0, 1))
    half = shape[1] // 2
    packed = jnp.zeros(shape, jnp.float32)
    for n, tile in enumerate(tiles):
        row = jnp.sum(tile, axis=0, keepdims=True)
        row = row + pltpu.roll(row, half, 1)
        place = (sub == n % shape[0]) & ((lane < half) == (n < shape[0]))
        packed = jnp.where(place, row, packed)
    return packed


def unpack_rows(packed, count):
    lane = lax.broadcasted_iota(jnp.int32, packed.shape, 1)
    low = lane < packed.shape[1] // 2
    sums = [
        jnp.sum(jnp.where(side, packed, 0.0), axis=1, keepdims=True)
        for side in (low, jnp.logical_not(low))
    ]
    size = packed.shape[0]
    return [sums[n // size][n % size : n % size + 1] for n in range(count)]


def powers_of_heights(levels, mate_flow, mate_flow_far, raw_far, powers):
    outer, inner, _ = orientation()
    line = [
        (mate_flow_far, levels, inner),
        (mate_flow_far, levels, outer),
        (mate_flow, levels, inner),
        (mate_flow, levels, outer),
        (raw_far, VECTORS * levels, inner),
        (raw_far, VECTORS * levels, outer),
    ]
    depth = [ref[base + DEPTHS + where] for ref, base, where in line]
    faces = [SURFACE_COUPLING * jnp.minimum(a, b) for a, b in zip(depth, depth[1:])]
    sides = [side_depths(SURFACE_COUPLING * d) for d in depth[1:5]]
    for v in range(VECTORS):
        field = [
            jnp.where(d > 0, ref[base + v * 2 + where], 0.0)
            for d, (ref, base, where) in zip(depth, line)
        ]

        def bend(field, first, last):
            found = []
            for j in range(first, last):
                west, centre, east = field[j - 1 : j + 2]
                north, south = sides[j - 1]
                found.append(
                    (faces[j] * (east - centre) - faces[j - 1] * (centre - west))
                    + (north * (next_row(centre) - centre) - south * (centre - prior_row(centre)))
                )
            return found

        lap = bend(field, 1, 5)
        image = [None] + [h - p for h, p in zip(field[1:5], lap)]
        again = [p - q for p, q in zip(image[2:4], bend(image, 2, 4))]
        for c, where in enumerate((3, 2)):
            powers[0, v, c] = field[where]
            powers[1, v, c] = image[where]
            powers[2, v, c] = again[where - 2]
            powers[POWERS, v, c] = lap[where - 1]


def total(tile):
    return jnp.sum(jnp.sum(tile, axis=0, keepdims=True), axis=1, keepdims=True)


def combine(one, factor, two):
    longest = max(len(one), len(two))
    one, two = (list(c) + [0.0] * (longest - len(c)) for c in (one, two))
    return [a + factor * b for a, b in zip(one, two)]


def third_kernel(
    levels, sub, count, pair, fetched, fetched_mate, surface, tracer,
    scaled, surface_out, growth, pole, residual, answer, image, depth, face_x, face_y, face_z, packed,
):
    width = 2 * count
    me = lax.axis_index("lon")
    core = lax.rem(me, 2)
    zero = jnp.zeros((sub, LANES), jnp.float32)
    none = (zero,) * VECTORS

    def place(owner, block):
        packed[owner] = block(GRAMS)
        for c in range(2):
            x = 2 * owner + c
            depth[x] = block(DEPTHS + c)
            for v in range(VECTORS):
                value = block(v * 2 + c)
                residual[v, x] = value
                pole[v, x + 1] = value

    for slot in range(2):
        place(me ^ slot, lambda row, slot=slot: pair[slot, row])
    for ref, flip in ((fetched, 0), (fetched_mate, 1)):
        for j, masks in enumerate(chip_masks(count)):
            mask = jnp.where((core ^ flip) == 0, *masks)
            for slot in range(2):
                owner = me ^ flip ^ slot ^ (2 * mask)

                def put(owner=owner, ref=ref, j=j, slot=slot):
                    place(owner, lambda row: ref[j, slot, row])

                if all(masks):
                    put()
                else:
                    pl.when(mask > 0)(put)

    def over(body, init):
        return lax.fori_loop(0, count, body, init, unroll=steps(count, 16))

    def each(d):
        return [(v, c, 2 * d + c) for v in range(VECTORS) for c in range(2)]

    def prepare(d, carry):
        for x in (2 * d, 2 * d + 1):
            here, after = depth[x], depth[lax.rem(x + 1, width)]
            face_x[x + 1] = SURFACE_COUPLING * jnp.minimum(here, after)
            north, south = side_depths(here)
            face_y[x] = SURFACE_COUPLING * north
            face_z[x] = SURFACE_COUPLING * south
        return carry

    over(prepare, 0)
    face_x[0] = face_x[width]
    wrap(pole, width)

    def start(d, carry):
        sums = list(carry)
        for v, _, x in each(d):
            sums[v] = sums[v] + residual[v, x] * residual[v, x]
        return tuple(sums)

    norm = [total(t) for t in over(start, none)]
    taken, left, aim = ([[v for _ in range(VECTORS)] for v in ([], [1.0], [1.0])])

    def apply(d, carry):
        sums = list(carry)
        for v, _, x in each(d):
            centre = pole[v, x + 1]
            value = centre - spread(pole, face_x, face_y, face_z, v, x)
            image[v, x] = value
            sums[v] = sums[v] + centre * value
        return tuple(sums)

    for iteration in range(ITERS):
        energy = [total(t) for t in over(apply, none)]
        size = [n / e for n, e in zip(norm, energy)]
        taken = [combine(s, z, a) for s, z, a in zip(taken, size, aim)]
        if iteration + 1 < ITERS:

            def advance(d, carry, size=size, first=iteration == 0):
                sums = list(carry)
                for v, _, x in each(d):
                    gone = size[v] * pole[v, x + 1]
                    answer[v, x] = gone if first else answer[v, x] + gone
                    value = residual[v, x] - size[v] * image[v, x]
                    residual[v, x] = value
                    sums[v] = sums[v] + value * value
                return tuple(sums)

            fresh = [total(t) for t in over(advance, none)]
            ratio = [f / n for f, n in zip(fresh, norm)]
            left = [combine(l, -z, [0.0] + a) for l, z, a in zip(left, size, aim)]
            aim = [combine(l, q, a) for l, q, a in zip(left, ratio, aim)]

            def turn(d, carry, ratio=ratio):
                for v, _, x in each(d):
                    pole[v, x + 1] = residual[v, x] + ratio[v] * pole[v, x + 1]
                return carry

            over(turn, 0)
            wrap(pole, width)
            norm = fresh

    def finish(d, carry):
        grams = list(carry)
        for x in (2 * d, 2 * d + 1):
            a, b = (answer[v, x] + size[v] * pole[v, x + 1] for v in range(VECTORS))
            answer[0, x], answer[1, x] = a, b
            grams = [grams[0] + a * a, grams[1] + a * b, grams[2] + b * b]
        return (*grams, carry[3] + packed[d])

    *grams, packed_sums = over(finish, (zero,) * 4)
    sums = unpack_rows(packed_sums, 3 + VECTORS * VECTORS * POWERS)

    def heights_with(i, j):
        first = 3 + (i * VECTORS + j) * POWERS
        return sum(c * t for c, t in zip(taken[j], sums[first : first + POWERS]))

    cells = (levels + 1) * width * sub * LANES
    one, mix, two = (
        (sums[n] + total(grams[n]) + (heights_with(i, j) + heights_with(j, i))) / cells
        for n, (i, j) in enumerate(((0, 0), (0, 1), (1, 1)))
    )
    scale_one = jnp.sqrt(one + EPSILON)
    cross = mix / scale_one
    rest = two - 2.0 * cross * cross + cross * cross * one / (one + EPSILON)
    scale_two = jnp.sqrt(rest + EPSILON)
    over_one, over_two = 1.0 / scale_one, 1.0 / scale_two

    def scale(k, carry):
        unit = tracer[0, k] * over_one
        scaled[0, k] = unit
        scaled[1, k] = (tracer[1, k] - cross * unit) * over_two
        return carry

    lax.fori_loop(0, levels, scale, 0, unroll=steps(levels, 10))
    for c in range(2):
        x = 2 * me + c
        first, second = (
            jnp.where(depth[x] > 0, surface[v, pl.ds(c, sub, stride=2), :], 0.0) + answer[v, x]
            for v in range(VECTORS)
        )
        unit = first * over_one
        surface_out[0, pl.ds(c, sub, stride=2), :] = unit
        surface_out[1, pl.ds(c, sub, stride=2), :] = (second - cross * unit) * over_two
    for i, value in enumerate((scale_one, cross, scale_two)):
        growth[i] = value[0, 0]


def tiled(array):
    *lead, columns, rows = array.shape
    split = array.reshape(*lead, columns, rows // LANES, LANES)
    return jnp.swapaxes(split, -3, -2).reshape(*lead, rows // LANES * columns, LANES)


def untiled(array, columns):
    *lead, high, lanes = array.shape
    split = array.reshape(*lead, high // columns, columns, lanes)
    return jnp.swapaxes(split, -3, -2).reshape(*lead, columns, high // columns * lanes)


def swap(array, mask):
    count = lax.axis_size("lon")
    return lax.ppermute(array, "lon", [(i, i ^ mask) for i in range(count)])


def chip_masks(count):
    lists, loads = ([], []), [0, 0]
    for mask in range(count // 2 - 1, 0, -1):
        core = int(loads[1] < loads[0])
        lists[core].append(mask)
        loads[core] += mask % 2 + mask // 2
    longest = max(map(len, lists))
    return list(zip(*(one + [0] * (longest - len(one)) for one in lists)))


def gather(block):
    count = lax.axis_size("lon")
    pair = jnp.stack([block, swap(block, 1)])
    fetched = []
    for masks in chip_masks(count):
        moves = [(i, i ^ (2 * masks[i % 2])) for i in range(count) if masks[i % 2]]
        fetched.append(lax.ppermute(pair, "lon", moves))
    fetched = jnp.stack(fetched)
    return pair, fetched, swap(fetched, 1)


def on_device(tracer_pert, surface_pert, zonal_flow, merid_flow, bottom_level):
    vectors, levels, columns, rows = tracer_pert.shape
    count = lax.axis_size("lon")
    sub = rows // LANES
    assert vectors == VECTORS and columns == 2 and rows % LANES == 0
    assert count >= 8 and count & (count - 1) == 0
    width = 2 * count
    f32 = jnp.float32
    vmem = pl.BlockSpec(memory_space=pltpu.VMEM)
    hbm = pl.BlockSpec(memory_space=pltpu.HBM)
    params = pltpu.CompilerParams(vmem_limit_bytes=24 * 2**20)

    def shaped(*shape):
        return jax.ShapeDtypeStruct((*shape, sub, LANES), f32)

    def held(*shape):
        return pltpu.VMEM((*shape, sub, LANES), f32)

    both = pltpu.VMEM((vectors, levels, sub * 2, LANES), f32)
    tracer_pert, zonal_flow, merid_flow = map(tiled, (tracer_pert, zonal_flow, merid_flow))
    outward = [(i, (i + 1) % count if i % 2 else (i - 1) % count) for i in range(count)]
    part = levels // 2
    surface, bottom = tiled(surface_pert), tiled(bottom_level)

    packed = shaped(VECTORS * levels + RIM), shaped(part)
    edge, flow_edge = pl.pallas_call(
        functools.partial(edge_kernel, levels, sub),
        out_shape=packed,
        in_specs=[hbm] * 4,
        out_specs=(hbm, hbm),
        scratch_shapes=[
            both,
            pltpu.VMEM((part, sub * 2, LANES), f32),
            pltpu.VMEM((vectors, sub * 2, LANES), f32),
            pltpu.VMEM((sub * 2, LANES), jnp.int32),
            held(VECTORS * levels + RIM),
            held(part),
            pltpu.SemaphoreType.DMA((VECTORS + 3,)),
            pltpu.SemaphoreType.DMA((VECTORS + 1,)),
        ],
        compiler_params=pltpu.CompilerParams(vmem_limit_bytes=60 * 2**20),
        name="edge_columns",
    )(tracer_pert, zonal_flow, surface, bottom)
    flow_half = lax.ppermute(flow_edge, "lon", outward)
    edge_far = lax.ppermute(edge, "lon", outward)
    flow_other = lax.ppermute(flow_half, "grp", [(0, 1), (1, 0)])
    cross, mate, raw, mate_raw, flow_in, mate_flow = pl.pallas_call(
        functools.partial(first_kernel, levels, sub),
        out_shape=(
            shaped(VECTORS * levels),
            shaped(VECTORS * levels),
            shaped(VECTORS * levels),
            shaped(VECTORS * levels),
            shaped(levels),
            shaped(levels + RIM),
        ),
        in_specs=[pl.BlockSpec(memory_space=pl.ANY)] + [vmem] * 5,
        out_specs=(vmem,) * 6,
        compiler_params=params,
        name="partial_step",
    )(edge, tracer_pert, zonal_flow, merid_flow, surface, bottom)
    cross_far = lax.ppermute(cross, "lon", outward)
    mate_far, mate_raw_far, mate_flow_far = (swap(x, 1) for x in (mate, mate_raw, mate_flow))
    done, *rest = pl.pallas_call(
        functools.partial(halo_kernel, levels, sub),
        out_shape=(
            shaped(vectors, levels),
            shaped(vectors, levels),
            shaped(levels),
            shaped(VECTORS + 3),
            shaped(POWERS + 1, vectors, 2),
        ),
        in_specs=[vmem] * 13,
        out_specs=(vmem,) * 5,
        scratch_shapes=[held(levels)],
        compiler_params=params,
        name="both_steps",
    )(
        raw, cross, mate, mate_raw, flow_in, mate_flow,
        edge_far, mate_far, mate_raw_far, mate_flow_far, flow_half, flow_other, merid_flow,
    )
    column, message = pl.pallas_call(
        functools.partial(second_kernel, levels),
        out_shape=(shaped(vectors, levels), shaped(BLOCKS)),
        in_specs=[vmem] * 6,
        out_specs=(vmem, vmem),
        compiler_params=params,
        name="outer_column",
    )(cross_far, *rest, mate_flow)
    tracer = pl.pallas_call(
        functools.partial(interleave_kernel, levels, sub),
        out_shape=jax.ShapeDtypeStruct((vectors, levels, sub * 2, LANES), f32),
        in_specs=[vmem] * 2,
        out_specs=vmem,
        compiler_params=params,
        name="interleave",
    )(column, done)
    tracer_vec, surface_vec, growth = pl.pallas_call(
        functools.partial(third_kernel, levels, sub, count),
        out_shape=(
            jax.ShapeDtypeStruct((vectors, levels, sub * 2, LANES), f32),
            jax.ShapeDtypeStruct((vectors, sub * 2, LANES), f32),
            jax.ShapeDtypeStruct((3,), f32),
        ),
        in_specs=[vmem] * 5,
        out_specs=(vmem, vmem, pl.BlockSpec(memory_space=pltpu.SMEM)),
        scratch_shapes=[
            held(vectors, width + 2),
            *[held(vectors, width)] * 3,
            held(width),
            held(width + 1),
            held(width),
            held(width),
            held(count),
        ],
        compiler_params=pltpu.CompilerParams(vmem_limit_bytes=32 * 2**20),
        name="surface_and_scale",
    )(*gather(message), surface, tracer)
    return (untiled(tracer_vec, 2), untiled(surface_vec, 2), growth)


def solution(mesh):
    placed = (
        P("grp", None, "lon", None),
        P("grp", "lon", None),
        P(None, "lon", None),
        P(None, "lon", None),
        P("lon", None),
    )
    return jax.shard_map(
        on_device,
        mesh=mesh,
        in_specs=placed,
        out_specs=(P("grp", None, "lon", None), P("grp", "lon", None), P("grp")),
        check_vma=False,
    )
```

```python
import functools

import jax
import jax.numpy as jnp
from jax import lax
from jax.experimental import pallas as pl
from jax.experimental.pallas import tpu as pltpu
from jax.sharding import PartitionSpec as P

ITERS = 3


DIFFUSIVITY = 0.5
TIME_STEP = 0.2
SURFACE_COUPLING = 0.5
STERIC_GAIN = 2.0
EPSILON = 1e-06

LANES = 128
VECTORS = 2
SLOPE = 0.25 * TIME_STEP
SPREAD = TIME_STEP * DIFFUSIVITY
DEPTHS = VECTORS * 2
RIM = DEPTHS + 2
GRAMS = RIM
BLOCKS = GRAMS + 1
POWERS = ITERS


def next_row(tile):
    turned = pltpu.roll(tile, LANES - 1, 1)
    carried = pltpu.roll(turned, tile.shape[0] - 1, 0)
    lane = lax.broadcasted_iota(jnp.int32, tile.shape, 1)
    return jnp.where(lane == LANES - 1, carried, turned)


def prior_row(tile):
    turned = pltpu.roll(tile, 1, 1)
    carried = pltpu.roll(turned, 1, 0)
    lane = lax.broadcasted_iota(jnp.int32, tile.shape, 1)
    return jnp.where(lane == 0, carried, turned)


def wall_depth(depth):
    subs, lane = (lax.broadcasted_iota(jnp.int32, depth.shape, axis) for axis in (0, 1))
    last = (subs == depth.shape[0] - 1) & (lane == LANES - 1)
    return jnp.where(last, jnp.zeros_like(depth), jnp.minimum(depth, next_row(depth)))


def face_pair(level, face_depth, flow_sum):
    slope = SLOPE * flow_sum
    open_face = level < face_depth
    return (
        jnp.where(open_face, slope + SPREAD, 0.0),
        jnp.where(open_face, slope - SPREAD, 0.0),
    )


def outflow(pair, near, far):
    return pair[0] * near + pair[1] * far


def side_pairs(level, depths, flow):
    return (
        face_pair(level, depths[0], flow + next_row(flow)),
        face_pair(level, depths[1], -(flow + prior_row(flow))),
    )


def divergence_y(pairs, tile):
    return outflow(pairs[0], tile, next_row(tile)) + outflow(pairs[1], tile, prior_row(tile))


def side_depths(depth):
    north = wall_depth(depth)
    return north, prior_row(north)


def orientation():
    outer = lax.rem(lax.axis_index("lon"), 2)
    return outer, 1 - outer, (2 * outer - 1).astype(jnp.float32)


def steps(count, most):
    return max(u for u in range(1, most + 1) if count % u == 0)


def share(levels):
    assert lax.axis_size("grp") == 2 and levels % 2 == 0
    part = levels // 2
    return lax.axis_index("grp") * (levels - part), part


def pack_rim(sub, surface, bottom, target, base):
    for c in range(2):
        for v in range(VECTORS):
            target[base + v * 2 + c] = surface[v, pl.ds(c, sub, stride=2), :]
        target[base + DEPTHS + c] = bottom[pl.ds(c, sub, stride=2), :].astype(jnp.float32)


def edge_kernel(
    levels, sub, tracer_hbm, zonal_hbm, surface_hbm, bottom_hbm, edge_hbm, flow_hbm,
    tracer, zonal, surface, bottom, edge, flow, sems_in, sems_out,
):
    outer, _, _ = orientation()
    start, part = share(levels)

    def move(source, target, sem):
        copy = pltpu.make_async_copy(source, target, sem)
        copy.start()
        return copy

    first = [
        move(zonal_hbm.at[pl.ds(start, part)], zonal, sems_in.at[0]),
        move(surface_hbm, surface, sems_in.at[1]),
        move(bottom_hbm, bottom, sems_in.at[2]),
    ]
    arrivals = [move(tracer_hbm.at[v], tracer.at[v], sems_in.at[3 + v]) for v in range(VECTORS)]
    for copy in first:
        copy.wait()

    def take(k, carry):
        flow[k] = zonal[k, pl.ds(outer, sub, stride=2), :]
        return carry

    lax.fori_loop(0, part, take, 0, unroll=steps(part, 10))
    departures = [move(flow, flow_hbm, sems_out.at[VECTORS])]
    pack_rim(sub, surface, bottom, edge, VECTORS * levels)
    for v, arrival in enumerate(arrivals):
        arrival.wait()

        def body(k, carry, v=v):
            edge[v * levels + k] = tracer[v, k, pl.ds(outer, sub, stride=2), :]
            return carry

        lax.fori_loop(0, levels, body, 0, unroll=steps(levels, 10))
        rows = pl.ds(v * levels, levels + (RIM if v == VECTORS - 1 else 0))
        departures.append(move(edge.at[rows], edge_hbm.at[rows], sems_out.at[v]))
    for departure in departures:
        departure.wait()


def first_kernel(
    levels, sub, edge, tracer, zonal, merid, surface, bottom,
    cross, mate, raw, mate_raw, flow_in, mate_flow,
):
    del edge
    outer, inner, sign = orientation()

    def column(ref, where, *lead):
        return ref[(*lead, pl.ds(where, sub, stride=2), slice(None))]

    depth = [column(bottom, where).astype(jnp.float32) for where in (outer, inner)]
    between = jnp.minimum(*depth)
    along = [side_depths(d) for d in depth]
    pack_rim(sub, surface, bottom, mate_flow, levels)

    def body(k, carry):
        level = k.astype(jnp.float32)
        flow = [column(zonal, where, k) for where in (outer, inner)]
        turn = [column(merid, where, k) for where in (outer, inner)]
        middle = face_pair(level, between, -sign * (flow[0] + flow[1]))
        sides = [side_pairs(level, along[c], turn[c]) for c in range(2)]
        for v in range(VECTORS):
            cells = [column(tracer, where, v, k) for where in (outer, inner)]
            flux = outflow(middle, *cells)
            kept = [
                jnp.where(level < depth[c], cells[c], 0.0) - divergence_y(sides[c], cells[c])
                for c in range(2)
            ]
            cross[v * levels + k] = kept[0] - flux
            raw[v * levels + k] = cells[0]
            mate[v * levels + k] = kept[1] + flux
            mate_raw[v * levels + k] = cells[1]
        flow_in[k] = flow[0]
        mate_flow[k] = flow[1]
        return carry

    lax.fori_loop(0, levels, body, 0, unroll=steps(levels, 10))


def wrap(pole, width):
    for v in range(VECTORS):
        pole[v, 0] = pole[v, width]
        pole[v, width + 1] = pole[v, 1]


def spread(pole, face_x, face_y, face_z, v, x):
    west, centre, east = (pole[v, x + j] for j in range(3))
    return (face_x[x + 1] * (east - centre) - face_x[x] * (centre - west)) + (
        face_y[x] * (next_row(centre) - centre) - face_z[x] * (centre - prior_row(centre))
    )


def halo_kernel(
    levels, sub, raw, cross, mate, mate_raw, flow_in, mate_flow,
    raw_far, mate_far, mate_raw_far, mate_flow_far, flow_half, flow_other, merid,
    done, base, weight, sums, powers, flow_far,
):
    outer, inner, sign = orientation()
    start, part = share(levels)

    def unpack(i, carry):
        flow_far[start + i] = flow_half[i]
        flow_far[levels - part - start + i] = flow_other[i]
        return carry

    lax.fori_loop(0, part, unpack, 0, unroll=steps(part, 10))
    powers_of_heights(levels, mate_flow, mate_flow_far, raw_far, powers)
    near, far = (raw, mate_raw), (raw_far, mate_raw_far)
    rim = levels + DEPTHS
    depth = [mate_flow[rim + where] for where in (outer, inner)]
    beside = [
        jnp.minimum(depth[0], raw_far[VECTORS * levels + DEPTHS + inner]),
        jnp.minimum(depth[1], mate_flow_far[rim + outer]),
    ]
    between = jnp.minimum(*depth)
    along = [side_depths(d) for d in depth]
    zero = jnp.zeros_like(between)

    def body(k, carry):
        level = k.astype(jnp.float32)
        flow = [flow_in[k], mate_flow[k]]
        beyond = [flow_far[k], mate_flow_far[k]]
        turn = [merid[k, pl.ds(where, sub, stride=2), :] for where in (outer, inner)]
        middle = face_pair(level, between, -sign * (flow[0] + flow[1]))
        edges = [
            face_pair(level, beside[c], (sign, -sign)[c] * (flow[c] + beyond[c])) for c in range(2)
        ]
        sides = [side_pairs(level, along[c], turn[c]) for c in range(2)]
        weight[k] = edges[0][1]
        totals, grams = list(carry[:VECTORS]), list(carry[VECTORS:])
        fresh = []
        for v in range(VECTORS):
            row = v * levels + k
            flux = [outflow(edges[c], near[c][row], far[c][row]) for c in range(2)]
            outside, inside = cross[row] - flux[0], mate[row] - flux[1]
            other = mate_far[row] + flux[1]
            crossing = outflow(middle, outside, inside)
            base[v, k] = (
                outside
                - outflow(edges[0], outside, flux[0])
                - crossing
                - divergence_y(sides[0], outside)
            )
            value = (
                inside - outflow(edges[1], inside, other) + crossing - divergence_y(sides[1], inside)
            )
            done[v, k] = value
            totals[v] = totals[v] + value
            fresh.append(value)
        return (*totals, *add_products(grams, *fresh))

    found = lax.fori_loop(0, levels, body, (zero,) * (VECTORS + 3), unroll=steps(levels, 10))
    for row, tile in enumerate(found):
        sums[row] = tile


def interleave_kernel(levels, sub, column, done, tracer):
    outer, inner, _ = orientation()

    def body(k, carry):
        for v in range(VECTORS):
            tracer[v, k, pl.ds(outer, sub, stride=2), :] = column[v, k]
            tracer[v, k, pl.ds(inner, sub, stride=2), :] = done[v, k]
        return carry

    lax.fori_loop(0, levels, body, 0, unroll=steps(levels, 10))


def add_products(grams, a, b):
    return [grams[0] + a * a, grams[1] + a * b, grams[2] + b * b]


def second_kernel(levels, cross_far, base, weight, inside, powers, mate_flow, column, message):
    outer, inner, _ = orientation()
    zero = jnp.zeros(powers.shape[-2:], jnp.float32)

    def body(k, carry):
        totals, fresh = [], []
        for v in range(VECTORS):
            value = base[v, k] - weight[k] * cross_far[v * levels + k]
            column[v, k] = value
            totals.append(carry[v] + value)
            fresh.append(value)
        return (*totals, *add_products(carry[VECTORS:], *fresh))

    carry = lax.fori_loop(0, levels, body, (zero,) * (VECTORS + 3), unroll=steps(levels, 50))
    gain = STERIC_GAIN / levels
    rows = [a + inside[VECTORS + n] for n, a in enumerate(carry[VECTORS:])]
    residual = []
    for v in range(VECTORS):
        residual.append(
            [gain * total_of + powers[POWERS, v, c] for c, total_of in enumerate((carry[v], inside[v]))]
        )
        for c, where in enumerate((outer, inner)):
            message[v * 2 + where] = residual[v][c]

    def product(one, two):
        return one[0] * two[0] + one[1] * two[1]

    heights = [[powers[0, v, c] for c in range(2)] for v in range(VECTORS)]
    for n, (i, j) in enumerate(((0, 0), (0, 1), (1, 1))):
        rows[n] = rows[n] + product(heights[i], heights[j])
    for i in range(VECTORS):
        for j in range(VECTORS):
            for m in range(POWERS):
                rows.append(product([powers[m, i, c] for c in range(2)], residual[j]))
    message[GRAMS] = pack_rows(rows)
    for c in range(2):
        message[DEPTHS + c] = mate_flow[levels + DEPTHS + c]


def pack_rows(tiles):
    shape = tiles[0].shape
    sub, lane = (lax.broadcasted_iota(jnp.int32, shape, axis) for axis in (0, 1))
    half = shape[1] // 2
    packed = jnp.zeros(shape, jnp.float32)
    for n, tile in enumerate(tiles):
        row = jnp.sum(tile, axis=0, keepdims=True)
        row = row + pltpu.roll(row, half, 1)
        place = (sub == n % shape[0]) & ((lane < half) == (n < shape[0]))
        packed = jnp.where(place, row, packed)
    return packed


def unpack_rows(packed, count):
    lane = lax.broadcasted_iota(jnp.int32, packed.shape, 1)
    low = lane < packed.shape[1] // 2
    sums = [
        jnp.sum(jnp.where(side, packed, 0.0), axis=1, keepdims=True)
        for side in (low, jnp.logical_not(low))
    ]
    size = packed.shape[0]
    return [sums[n // size][n % size : n % size + 1] for n in range(count)]


def powers_of_heights(levels, mate_flow, mate_flow_far, raw_far, powers):
    outer, inner, _ = orientation()
    line = [
        (mate_flow_far, levels, inner),
        (mate_flow_far, levels, outer),
        (mate_flow, levels, inner),
        (mate_flow, levels, outer),
        (raw_far, VECTORS * levels, inner),
        (raw_far, VECTORS * levels, outer),
    ]
    depth = [ref[base + DEPTHS + where] for ref, base, where in line]
    faces = [SURFACE_COUPLING * jnp.minimum(a, b) for a, b in zip(depth, depth[1:])]
    sides = [side_depths(SURFACE_COUPLING * d) for d in depth[1:5]]
    for v in range(VECTORS):
        field = [
            jnp.where(d > 0, ref[base + v * 2 + where], 0.0)
            for d, (ref, base, where) in zip(depth, line)
        ]

        def bend(field, first, last):
            found = []
            for j in range(first, last):
                west, centre, east = field[j - 1 : j + 2]
                north, south = sides[j - 1]
                found.append(
                    (faces[j] * (east - centre) - faces[j - 1] * (centre - west))
                    + (north * (next_row(centre) - centre) - south * (centre - prior_row(centre)))
                )
            return found

        lap = bend(field, 1, 5)
        image = [None] + [h - p for h, p in zip(field[1:5], lap)]
        again = [p - q for p, q in zip(image[2:4], bend(image, 2, 4))]
        for c, where in enumerate((3, 2)):
            powers[0, v, c] = field[where]
            powers[1, v, c] = image[where]
            powers[2, v, c] = again[where - 2]
            powers[POWERS, v, c] = lap[where - 1]


def total(tile):
    return jnp.sum(jnp.sum(tile, axis=0, keepdims=True), axis=1, keepdims=True)


def combine(one, factor, two):
    longest = max(len(one), len(two))
    one, two = (list(c) + [0.0] * (longest - len(c)) for c in (one, two))
    return [a + factor * b for a, b in zip(one, two)]


def third_kernel(levels, sub, count, *refs):
    masks_of = chip_masks(count)
    blocks = 1 + 2 * len(masks_of)
    (surface, tracer, scaled, surface_out, growth) = refs[blocks : blocks + 5]
    (pole, residual, answer, image, depth, face_x, face_y, face_z, packed) = refs[blocks + 5 :]
    width = 2 * count
    me = lax.axis_index("lon")
    core = lax.rem(me, 2)
    zero = jnp.zeros((sub, LANES), jnp.float32)
    none = (zero,) * VECTORS

    def place(first, block):
        packed[first // 2] = block[2 * RIM]
        for slot in range(2):
            for c in range(2):
                x = 2 * (first ^ slot) + c
                depth[x] = block[RIM * slot + DEPTHS + c]
                for v in range(VECTORS):
                    value = block[RIM * slot + v * 2 + c]
                    residual[v, x] = value
                    pole[v, x + 1] = value

    place(me, refs[0])
    for n, block in enumerate(refs[1:blocks]):
        flip, masks = n // len(masks_of), masks_of[n % len(masks_of)]
        mask = jnp.where((core ^ flip) == 0, *masks)

        def put(first=me ^ flip ^ (2 * mask), block=block):
            place(first, block)

        if all(masks):
            put()
        else:
            pl.when(mask > 0)(put)

    def over(body, init):
        return lax.fori_loop(0, count, body, init, unroll=steps(count, 16))

    def each(d):
        return [(v, c, 2 * d + c) for v in range(VECTORS) for c in range(2)]

    def prepare(d, carry):
        for x in (2 * d, 2 * d + 1):
            here, after = depth[x], depth[lax.rem(x + 1, width)]
            face_x[x + 1] = SURFACE_COUPLING * jnp.minimum(here, after)
            north, south = side_depths(here)
            face_y[x] = SURFACE_COUPLING * north
            face_z[x] = SURFACE_COUPLING * south
        return carry

    over(prepare, 0)
    face_x[0] = face_x[width]
    wrap(pole, width)

    def start(d, carry):
        sums = list(carry)
        for v, _, x in each(d):
            sums[v] = sums[v] + residual[v, x] * residual[v, x]
        return tuple(sums)

    norm = [total(t) for t in over(start, none)]
    taken, left, aim = ([[v for _ in range(VECTORS)] for v in ([], [1.0], [1.0])])

    def apply(d, carry):
        sums = list(carry)
        for v, _, x in each(d):
            centre = pole[v, x + 1]
            value = centre - spread(pole, face_x, face_y, face_z, v, x)
            image[v, x] = value
            sums[v] = sums[v] + centre * value
        return tuple(sums)

    for iteration in range(ITERS):
        energy = [total(t) for t in over(apply, none)]
        size = [n / e for n, e in zip(norm, energy)]
        taken = [combine(s, z, a) for s, z, a in zip(taken, size, aim)]
        if iteration + 1 < ITERS:

            def advance(d, carry, size=size, first=iteration == 0):
                sums = list(carry)
                for v, _, x in each(d):
                    gone = size[v] * pole[v, x + 1]
                    answer[v, x] = gone if first else answer[v, x] + gone
                    value = residual[v, x] - size[v] * image[v, x]
                    residual[v, x] = value
                    sums[v] = sums[v] + value * value
                return tuple(sums)

            fresh = [total(t) for t in over(advance, none)]
            ratio = [f / n for f, n in zip(fresh, norm)]
            left = [combine(l, -z, [0.0] + a) for l, z, a in zip(left, size, aim)]
            aim = [combine(l, q, a) for l, q, a in zip(left, ratio, aim)]

            def turn(d, carry, ratio=ratio):
                for v, _, x in each(d):
                    pole[v, x + 1] = residual[v, x] + ratio[v] * pole[v, x + 1]
                return carry

            over(turn, 0)
            wrap(pole, width)
            norm = fresh

    def finish(d, carry):
        grams = list(carry)
        for x in (2 * d, 2 * d + 1):
            a, b = (answer[v, x] + size[v] * pole[v, x + 1] for v in range(VECTORS))
            answer[0, x], answer[1, x] = a, b
            grams = [grams[0] + a * a, grams[1] + a * b, grams[2] + b * b]
        return (*grams, carry[3])

    *grams, _ = over(finish, (zero,) * 4)
    packed_sums = sum((packed[n] for n in range(1, count // 2)), packed[0])
    sums = unpack_rows(packed_sums, 3 + VECTORS * VECTORS * POWERS)

    def heights_with(i, j):
        first = 3 + (i * VECTORS + j) * POWERS
        return sum(c * t for c, t in zip(taken[j], sums[first : first + POWERS]))

    cells = (levels + 1) * width * sub * LANES
    one, mix, two = (
        (sums[n] + total(grams[n]) + (heights_with(i, j) + heights_with(j, i))) / cells
        for n, (i, j) in enumerate(((0, 0), (0, 1), (1, 1)))
    )
    scale_one = jnp.sqrt(one + EPSILON)
    cross = mix / scale_one
    rest = two - 2.0 * cross * cross + cross * cross * one / (one + EPSILON)
    scale_two = jnp.sqrt(rest + EPSILON)
    over_one, over_two = 1.0 / scale_one, 1.0 / scale_two

    def scale(k, carry):
        unit = tracer[0, k] * over_one
        scaled[0, k] = unit
        scaled[1, k] = (tracer[1, k] - cross * unit) * over_two
        return carry

    lax.fori_loop(0, levels, scale, 0, unroll=steps(levels, 50))
    for c in range(2):
        x = 2 * me + c
        first, second = (
            jnp.where(depth[x] > 0, surface[v, pl.ds(c, sub, stride=2), :], 0.0) + answer[v, x]
            for v in range(VECTORS)
        )
        unit = first * over_one
        surface_out[0, pl.ds(c, sub, stride=2), :] = unit
        surface_out[1, pl.ds(c, sub, stride=2), :] = (second - cross * unit) * over_two
    for i, value in enumerate((scale_one, cross, scale_two)):
        growth[i] = value[0, 0]


def tiled(array):
    *lead, columns, rows = array.shape
    split = array.reshape(*lead, columns, rows // LANES, LANES)
    return jnp.swapaxes(split, -3, -2).reshape(*lead, rows // LANES * columns, LANES)


def untiled(array, columns):
    *lead, high, lanes = array.shape
    split = array.reshape(*lead, high // columns, columns, lanes)
    return jnp.swapaxes(split, -3, -2).reshape(*lead, columns, high // columns * lanes)


def swap(array, mask):
    count = lax.axis_size("lon")
    return lax.ppermute(array, "lon", [(i, i ^ mask) for i in range(count)])


def chip_masks(count):
    lists, loads = ([], []), [0, 0]
    for mask in range(count // 2 - 1, 0, -1):
        core = int(loads[1] < loads[0])
        lists[core].append(mask)
        loads[core] += mask % 2 + mask // 2
    longest = max(map(len, lists))
    return list(zip(*(one + [0] * (longest - len(one)) for one in lists)))


def gather(block):
    count = lax.axis_size("lon")
    beside = swap(block, 1)
    pair = jnp.concatenate([block[:RIM], beside[:RIM], block[RIM:] + beside[RIM:]])
    fetched = []
    for masks in chip_masks(count):
        moves = [(i, i ^ (2 * masks[i % 2])) for i in range(count) if masks[i % 2]]
        fetched.append(lax.ppermute(pair, "lon", moves))
    return pair, *fetched, *(swap(one, 1) for one in fetched)


def on_device(tracer_pert, surface_pert, zonal_flow, merid_flow, bottom_level):
    vectors, levels, columns, rows = tracer_pert.shape
    count = lax.axis_size("lon")
    sub = rows // LANES
    assert vectors == VECTORS and columns == 2 and rows % LANES == 0
    assert count >= 8 and count & (count - 1) == 0
    width = 2 * count
    f32 = jnp.float32
    vmem = pl.BlockSpec(memory_space=pltpu.VMEM)
    hbm = pl.BlockSpec(memory_space=pltpu.HBM)
    params = pltpu.CompilerParams(vmem_limit_bytes=24 * 2**20)

    def shaped(*shape):
        return jax.ShapeDtypeStruct((*shape, sub, LANES), f32)

    def held(*shape):
        return pltpu.VMEM((*shape, sub, LANES), f32)

    both = pltpu.VMEM((vectors, levels, sub * 2, LANES), f32)
    tracer_pert, zonal_flow, merid_flow = map(tiled, (tracer_pert, zonal_flow, merid_flow))
    outward = [(i, (i + 1) % count if i % 2 else (i - 1) % count) for i in range(count)]
    part = levels // 2
    surface, bottom = tiled(surface_pert), tiled(bottom_level)

    packed = shaped(VECTORS * levels + RIM), shaped(part)
    edge, flow_edge = pl.pallas_call(
        functools.partial(edge_kernel, levels, sub),
        out_shape=packed,
        in_specs=[hbm] * 4,
        out_specs=(hbm, hbm),
        scratch_shapes=[
            both,
            pltpu.VMEM((part, sub * 2, LANES), f32),
            pltpu.VMEM((vectors, sub * 2, LANES), f32),
            pltpu.VMEM((sub * 2, LANES), jnp.int32),
            held(VECTORS * levels + RIM),
            held(part),
            pltpu.SemaphoreType.DMA((VECTORS + 3,)),
            pltpu.SemaphoreType.DMA((VECTORS + 1,)),
        ],
        compiler_params=pltpu.CompilerParams(vmem_limit_bytes=60 * 2**20),
        name="edge_columns",
    )(tracer_pert, zonal_flow, surface, bottom)
    flow_half = lax.ppermute(flow_edge, "lon", outward)
    edge_far = lax.ppermute(edge, "lon", outward)
    flow_other = lax.ppermute(flow_half, "grp", [(0, 1), (1, 0)])
    cross, mate, raw, mate_raw, flow_in, mate_flow = pl.pallas_call(
        functools.partial(first_kernel, levels, sub),
        out_shape=(
            shaped(VECTORS * levels),
            shaped(VECTORS * levels),
            shaped(VECTORS * levels),
            shaped(VECTORS * levels),
            shaped(levels),
            shaped(levels + RIM),
        ),
        in_specs=[pl.BlockSpec(memory_space=pl.ANY)] + [vmem] * 5,
        out_specs=(vmem,) * 6,
        compiler_params=params,
        name="partial_step",
    )(edge, tracer_pert, zonal_flow, merid_flow, surface, bottom)
    cross_far = lax.ppermute(cross, "lon", outward)
    mate_far, mate_raw_far, mate_flow_far = (swap(x, 1) for x in (mate, mate_raw, mate_flow))
    done, *rest = pl.pallas_call(
        functools.partial(halo_kernel, levels, sub),
        out_shape=(
            shaped(vectors, levels),
            shaped(vectors, levels),
            shaped(levels),
            shaped(VECTORS + 3),
            shaped(POWERS + 1, vectors, 2),
        ),
        in_specs=[vmem] * 13,
        out_specs=(vmem,) * 5,
        scratch_shapes=[held(levels)],
        compiler_params=params,
        name="both_steps",
    )(
        raw, cross, mate, mate_raw, flow_in, mate_flow,
        edge_far, mate_far, mate_raw_far, mate_flow_far, flow_half, flow_other, merid_flow,
    )
    column, message = pl.pallas_call(
        functools.partial(second_kernel, levels),
        out_shape=(shaped(vectors, levels), shaped(BLOCKS)),
        in_specs=[vmem] * 6,
        out_specs=(vmem, vmem),
        compiler_params=params,
        name="outer_column",
    )(cross_far, *rest, mate_flow)
    tracer = pl.pallas_call(
        functools.partial(interleave_kernel, levels, sub),
        out_shape=jax.ShapeDtypeStruct((vectors, levels, sub * 2, LANES), f32),
        in_specs=[vmem] * 2,
        out_specs=vmem,
        compiler_params=params,
        name="interleave",
    )(column, done)
    blocks = gather(message)
    tracer_vec, surface_vec, growth = pl.pallas_call(
        functools.partial(third_kernel, levels, sub, count),
        out_shape=(
            jax.ShapeDtypeStruct((vectors, levels, sub * 2, LANES), f32),
            jax.ShapeDtypeStruct((vectors, sub * 2, LANES), f32),
            jax.ShapeDtypeStruct((3,), f32),
        ),
        in_specs=[vmem] * (len(blocks) + 2),
        out_specs=(vmem, vmem, pl.BlockSpec(memory_space=pltpu.SMEM)),
        scratch_shapes=[
            held(vectors, width + 2),
            *[held(vectors, width)] * 3,
            held(width),
            held(width + 1),
            held(width),
            held(width),
            held(count // 2),
        ],
        compiler_params=pltpu.CompilerParams(vmem_limit_bytes=32 * 2**20),
        name="surface_and_scale",
    )(*blocks, surface, tracer)
    return (untiled(tracer_vec, 2), untiled(surface_vec, 2), growth)


def solution(mesh):
    placed = (
        P("grp", None, "lon", None),
        P("grp", "lon", None),
        P(None, "lon", None),
        P(None, "lon", None),
        P("lon", None),
    )
    return jax.shard_map(
        on_device,
        mesh=mesh,
        in_specs=placed,
        out_specs=(P("grp", None, "lon", None), P("grp", "lon", None), P("grp")),
        check_vma=False,
    )
```

```python
import functools

import jax
import jax.numpy as jnp
from jax import lax
from jax.experimental import pallas as pl
from jax.experimental.pallas import tpu as pltpu
from jax.sharding import PartitionSpec as P

ITERS = 3


DIFFUSIVITY = 0.5
TIME_STEP = 0.2
SURFACE_COUPLING = 0.5
STERIC_GAIN = 2.0
EPSILON = 1e-06

LANES = 128
VECTORS = 2
SLOPE = 0.25 * TIME_STEP
SPREAD = TIME_STEP * DIFFUSIVITY
DEPTHS = VECTORS * 2
RIM = DEPTHS + 2
GRAMS = RIM
BLOCKS = GRAMS + 1
POWERS = ITERS


def next_row(tile):
    turned = pltpu.roll(tile, LANES - 1, 1)
    carried = pltpu.roll(turned, tile.shape[0] - 1, 0)
    lane = lax.broadcasted_iota(jnp.int32, tile.shape, 1)
    return jnp.where(lane == LANES - 1, carried, turned)


def prior_row(tile):
    turned = pltpu.roll(tile, 1, 1)
    carried = pltpu.roll(turned, 1, 0)
    lane = lax.broadcasted_iota(jnp.int32, tile.shape, 1)
    return jnp.where(lane == 0, carried, turned)


def wall_depth(depth):
    subs, lane = (lax.broadcasted_iota(jnp.int32, depth.shape, axis) for axis in (0, 1))
    last = (subs == depth.shape[0] - 1) & (lane == LANES - 1)
    return jnp.where(last, jnp.zeros_like(depth), jnp.minimum(depth, next_row(depth)))


def face_pair(level, face_depth, flow_sum):
    slope = SLOPE * flow_sum
    open_face = level < face_depth
    return (
        jnp.where(open_face, slope + SPREAD, 0.0),
        jnp.where(open_face, slope - SPREAD, 0.0),
    )


def outflow(pair, near, far):
    return pair[0] * near + pair[1] * far


def side_pairs(level, depths, flow):
    return (
        face_pair(level, depths[0], flow + next_row(flow)),
        face_pair(level, depths[1], -(flow + prior_row(flow))),
    )


def divergence_y(pairs, tile):
    return outflow(pairs[0], tile, next_row(tile)) + outflow(pairs[1], tile, prior_row(tile))


def side_depths(depth):
    north = wall_depth(depth)
    return north, prior_row(north)


def orientation():
    outer = lax.rem(lax.axis_index("lon"), 2)
    return outer, 1 - outer, (2 * outer - 1).astype(jnp.float32)


def steps(count, most):
    return max(u for u in range(1, most + 1) if count % u == 0)


def share(levels):
    assert lax.axis_size("grp") == 2 and levels % 2 == 0
    part = levels // 2
    return lax.axis_index("grp") * (levels - part), part


def pack_rim(sub, surface, bottom, target, base):
    for c in range(2):
        for v in range(VECTORS):
            target[base + v * 2 + c] = surface[v, pl.ds(c, sub, stride=2), :]
        target[base + DEPTHS + c] = bottom[pl.ds(c, sub, stride=2), :].astype(jnp.float32)


def edge_kernel(
    levels, sub, tracer_hbm, zonal_hbm, surface_hbm, bottom_hbm, edge, flow,
    tracer, zonal, surface, bottom, sems,
):
    outer, _, _ = orientation()
    start, part = share(levels)
    pairs = [
        (zonal_hbm.at[pl.ds(start, part)], zonal),
        (surface_hbm, surface),
        (bottom_hbm, bottom),
        *((tracer_hbm.at[v], tracer.at[v]) for v in range(VECTORS)),
    ]
    copies = [
        pltpu.make_async_copy(source, target, sems.at[i]) for i, (source, target) in enumerate(pairs)
    ]
    for copy in copies:
        copy.start()
    for copy in copies[:3]:
        copy.wait()

    def take(k, carry):
        flow[k] = zonal[k, pl.ds(outer, sub, stride=2), :]
        return carry

    lax.fori_loop(0, part, take, 0, unroll=steps(part, 25))
    pack_rim(sub, surface, bottom, edge, VECTORS * levels)
    for v in range(VECTORS):
        copies[3 + v].wait()

        def body(k, carry, v=v):
            edge[v * levels + k] = tracer[v, k, pl.ds(outer, sub, stride=2), :]
            return carry

        lax.fori_loop(0, levels, body, 0, unroll=steps(levels, 25))


def first_kernel(
    levels, sub, edge, tracer, zonal, merid, surface, bottom,
    cross, mate, raw, mate_raw, flow_in, mate_flow,
):
    del edge
    outer, inner, sign = orientation()

    def column(ref, where, *lead):
        return ref[(*lead, pl.ds(where, sub, stride=2), slice(None))]

    depth = [column(bottom, where).astype(jnp.float32) for where in (outer, inner)]
    between = jnp.minimum(*depth)
    along = [side_depths(d) for d in depth]
    pack_rim(sub, surface, bottom, mate_flow, levels)

    def body(k, carry):
        level = k.astype(jnp.float32)
        flow = [column(zonal, where, k) for where in (outer, inner)]
        turn = [column(merid, where, k) for where in (outer, inner)]
        middle = face_pair(level, between, -sign * (flow[0] + flow[1]))
        sides = [side_pairs(level, along[c], turn[c]) for c in range(2)]
        for v in range(VECTORS):
            cells = [column(tracer, where, v, k) for where in (outer, inner)]
            flux = outflow(middle, *cells)
            kept = [
                jnp.where(level < depth[c], cells[c], 0.0) - divergence_y(sides[c], cells[c])
                for c in range(2)
            ]
            cross[v * levels + k] = kept[0] - flux
            raw[v * levels + k] = cells[0]
            mate[v * levels + k] = kept[1] + flux
            mate_raw[v * levels + k] = cells[1]
        flow_in[k] = flow[0]
        mate_flow[k] = flow[1]
        return carry

    lax.fori_loop(0, levels, body, 0, unroll=steps(levels, 10))


def wrap(pole, width):
    for v in range(VECTORS):
        pole[v, 0] = pole[v, width]
        pole[v, width + 1] = pole[v, 1]


def spread(pole, face_x, face_y, face_z, v, x):
    west, centre, east = (pole[v, x + j] for j in range(3))
    return (face_x[x + 1] * (east - centre) - face_x[x] * (centre - west)) + (
        face_y[x] * (next_row(centre) - centre) - face_z[x] * (centre - prior_row(centre))
    )


def halo_kernel(
    levels, sub, raw, cross, mate, mate_raw, flow_in, mate_flow,
    raw_far, mate_far, mate_raw_far, mate_flow_far, flow_half, flow_other, merid,
    done, base, weight, sums, powers, flow_far,
):
    outer, inner, sign = orientation()
    start, part = share(levels)

    def unpack(i, carry):
        flow_far[start + i] = flow_half[i]
        flow_far[levels - part - start + i] = flow_other[i]
        return carry

    lax.fori_loop(0, part, unpack, 0, unroll=steps(part, 10))
    powers_of_heights(levels, mate_flow, mate_flow_far, raw_far, powers)
    near, far = (raw, mate_raw), (raw_far, mate_raw_far)
    rim = levels + DEPTHS
    depth = [mate_flow[rim + where] for where in (outer, inner)]
    beside = [
        jnp.minimum(depth[0], raw_far[VECTORS * levels + DEPTHS + inner]),
        jnp.minimum(depth[1], mate_flow_far[rim + outer]),
    ]
    between = jnp.minimum(*depth)
    along = [side_depths(d) for d in depth]
    zero = jnp.zeros_like(between)

    def body(k, carry):
        level = k.astype(jnp.float32)
        flow = [flow_in[k], mate_flow[k]]
        beyond = [flow_far[k], mate_flow_far[k]]
        turn = [merid[k, pl.ds(where, sub, stride=2), :] for where in (outer, inner)]
        middle = face_pair(level, between, -sign * (flow[0] + flow[1]))
        edges = [
            face_pair(level, beside[c], (sign, -sign)[c] * (flow[c] + beyond[c])) for c in range(2)
        ]
        sides = [side_pairs(level, along[c], turn[c]) for c in range(2)]
        weight[k] = edges[0][1]
        totals, grams = list(carry[:VECTORS]), list(carry[VECTORS:])
        fresh = []
        for v in range(VECTORS):
            row = v * levels + k
            flux = [outflow(edges[c], near[c][row], far[c][row]) for c in range(2)]
            outside, inside = cross[row] - flux[0], mate[row] - flux[1]
            other = mate_far[row] + flux[1]
            crossing = outflow(middle, outside, inside)
            base[v, k] = (
                outside
                - outflow(edges[0], outside, flux[0])
                - crossing
                - divergence_y(sides[0], outside)
            )
            value = (
                inside - outflow(edges[1], inside, other) + crossing - divergence_y(sides[1], inside)
            )
            done[v, k] = value
            totals[v] = totals[v] + value
            fresh.append(value)
        return (*totals, *add_products(grams, *fresh))

    found = lax.fori_loop(0, levels, body, (zero,) * (VECTORS + 3), unroll=steps(levels, 10))
    for row, tile in enumerate(found):
        sums[row] = tile


def interleave_kernel(levels, sub, column, done, tracer):
    outer, inner, _ = orientation()

    def body(k, carry):
        for v in range(VECTORS):
            tracer[v, k, pl.ds(outer, sub, stride=2), :] = column[v, k]
            tracer[v, k, pl.ds(inner, sub, stride=2), :] = done[v, k]
        return carry

    lax.fori_loop(0, levels, body, 0, unroll=steps(levels, 10))


def add_products(grams, a, b):
    return [grams[0] + a * a, grams[1] + a * b, grams[2] + b * b]


def second_kernel(levels, cross_far, base, weight, inside, powers, mate_flow, column, message):
    outer, inner, _ = orientation()
    zero = jnp.zeros(powers.shape[-2:], jnp.float32)

    def body(k, carry):
        totals, fresh = [], []
        for v in range(VECTORS):
            value = base[v, k] - weight[k] * cross_far[v * levels + k]
            column[v, k] = value
            totals.append(carry[v] + value)
            fresh.append(value)
        return (*totals, *add_products(carry[VECTORS:], *fresh))

    carry = lax.fori_loop(0, levels, body, (zero,) * (VECTORS + 3), unroll=steps(levels, 50))
    gain = STERIC_GAIN / levels
    rows = [a + inside[VECTORS + n] for n, a in enumerate(carry[VECTORS:])]
    residual = []
    for v in range(VECTORS):
        residual.append(
            [gain * total_of + powers[POWERS, v, c] for c, total_of in enumerate((carry[v], inside[v]))]
        )
        for c, where in enumerate((outer, inner)):
            message[v * 2 + where] = residual[v][c]

    def product(one, two):
        return one[0] * two[0] + one[1] * two[1]

    heights = [[powers[0, v, c] for c in range(2)] for v in range(VECTORS)]
    for n, (i, j) in enumerate(((0, 0), (0, 1), (1, 1))):
        rows[n] = rows[n] + product(heights[i], heights[j])
    for i in range(VECTORS):
        for j in range(VECTORS):
            for m in range(POWERS):
                rows.append(product([powers[m, i, c] for c in range(2)], residual[j]))
    message[GRAMS] = pack_rows(rows)
    for c in range(2):
        message[DEPTHS + c] = mate_flow[levels + DEPTHS + c]


def pack_rows(tiles):
    shape = tiles[0].shape
    sub, lane = (lax.broadcasted_iota(jnp.int32, shape, axis) for axis in (0, 1))
    half = shape[1] // 2
    packed = jnp.zeros(shape, jnp.float32)
    for n, tile in enumerate(tiles):
        row = jnp.sum(tile, axis=0, keepdims=True)
        row = row + pltpu.roll(row, half, 1)
        place = (sub == n % shape[0]) & ((lane < half) == (n < shape[0]))
        packed = jnp.where(place, row, packed)
    return packed


def unpack_rows(packed, count):
    lane = lax.broadcasted_iota(jnp.int32, packed.shape, 1)
    low = lane < packed.shape[1] // 2
    sums = [
        jnp.sum(jnp.where(side, packed, 0.0), axis=1, keepdims=True)
        for side in (low, jnp.logical_not(low))
    ]
    size = packed.shape[0]
    return [sums[n // size][n % size : n % size + 1] for n in range(count)]


def powers_of_heights(levels, mate_flow, mate_flow_far, raw_far, powers):
    outer, inner, _ = orientation()
    line = [
        (mate_flow_far, levels, inner),
        (mate_flow_far, levels, outer),
        (mate_flow, levels, inner),
        (mate_flow, levels, outer),
        (raw_far, VECTORS * levels, inner),
        (raw_far, VECTORS * levels, outer),
    ]
    depth = [ref[base + DEPTHS + where] for ref, base, where in line]
    faces = [SURFACE_COUPLING * jnp.minimum(a, b) for a, b in zip(depth, depth[1:])]
    sides = [side_depths(SURFACE_COUPLING * d) for d in depth[1:5]]
    for v in range(VECTORS):
        field = [
            jnp.where(d > 0, ref[base + v * 2 + where], 0.0)
            for d, (ref, base, where) in zip(depth, line)
        ]

        def bend(field, first, last):
            found = []
            for j in range(first, last):
                west, centre, east = field[j - 1 : j + 2]
                north, south = sides[j - 1]
                found.append(
                    (faces[j] * (east - centre) - faces[j - 1] * (centre - west))
                    + (north * (next_row(centre) - centre) - south * (centre - prior_row(centre)))
                )
            return found

        lap = bend(field, 1, 5)
        image = [None] + [h - p for h, p in zip(field[1:5], lap)]
        again = [p - q for p, q in zip(image[2:4], bend(image, 2, 4))]
        for c, where in enumerate((3, 2)):
            powers[0, v, c] = field[where]
            powers[1, v, c] = image[where]
            powers[2, v, c] = again[where - 2]
            powers[POWERS, v, c] = lap[where - 1]


def total(tile):
    return jnp.sum(jnp.sum(tile, axis=0, keepdims=True), axis=1, keepdims=True)


def combine(one, factor, two):
    longest = max(len(one), len(two))
    one, two = (list(c) + [0.0] * (longest - len(c)) for c in (one, two))
    return [a + factor * b for a, b in zip(one, two)]


def third_kernel(levels, sub, count, *refs):
    masks_of = chip_masks(count)
    blocks = 1 + 2 * len(masks_of)
    (surface, tracer, scaled, surface_out, growth) = refs[blocks : blocks + 5]
    (pole, residual, answer, image, depth, face_x, face_y, face_z, packed) = refs[blocks + 5 :]
    width = 2 * count
    me = lax.axis_index("lon")
    core = lax.rem(me, 2)
    zero = jnp.zeros((sub, LANES), jnp.float32)
    none = (zero,) * VECTORS

    def place(first, block):
        packed[first // 2] = block[2 * RIM]
        for slot in range(2):
            for c in range(2):
                x = 2 * (first ^ slot) + c
                depth[x] = block[RIM * slot + DEPTHS + c]
                for v in range(VECTORS):
                    value = block[RIM * slot + v * 2 + c]
                    residual[v, x] = value
                    pole[v, x + 1] = value

    place(me, refs[0])
    for n, block in enumerate(refs[1:blocks]):
        flip, masks = n // len(masks_of), masks_of[n % len(masks_of)]
        mask = jnp.where((core ^ flip) == 0, *masks)

        def put(first=me ^ flip ^ (2 * mask), block=block):
            place(first, block)

        if all(masks):
            put()
        else:
            pl.when(mask > 0)(put)

    def over(body, init):
        return lax.fori_loop(0, count, body, init, unroll=steps(count, 16))

    def each(d):
        return [(v, c, 2 * d + c) for v in range(VECTORS) for c in range(2)]

    def prepare(d, carry):
        for x in (2 * d, 2 * d + 1):
            here, after = depth[x], depth[lax.rem(x + 1, width)]
            face_x[x + 1] = SURFACE_COUPLING * jnp.minimum(here, after)
            north, south = side_depths(here)
            face_y[x] = SURFACE_COUPLING * north
            face_z[x] = SURFACE_COUPLING * south
        return carry

    over(prepare, 0)
    face_x[0] = face_x[width]
    wrap(pole, width)

    def start(d, carry):
        sums = list(carry)
        for v, _, x in each(d):
            sums[v] = sums[v] + residual[v, x] * residual[v, x]
        return tuple(sums)

    norm = [total(t) for t in over(start, none)]
    taken, left, aim = ([[v for _ in range(VECTORS)] for v in ([], [1.0], [1.0])])

    def apply(d, carry):
        sums = list(carry)
        for v, _, x in each(d):
            centre = pole[v, x + 1]
            value = centre - spread(pole, face_x, face_y, face_z, v, x)
            image[v, x] = value
            sums[v] = sums[v] + centre * value
        return tuple(sums)

    for iteration in range(ITERS):
        energy = [total(t) for t in over(apply, none)]
        size = [n / e for n, e in zip(norm, energy)]
        taken = [combine(s, z, a) for s, z, a in zip(taken, size, aim)]
        if iteration + 1 < ITERS:

            def advance(d, carry, size=size, first=iteration == 0):
                sums = list(carry)
                for v, _, x in each(d):
                    gone = size[v] * pole[v, x + 1]
                    answer[v, x] = gone if first else answer[v, x] + gone
                    value = residual[v, x] - size[v] * image[v, x]
                    residual[v, x] = value
                    sums[v] = sums[v] + value * value
                return tuple(sums)

            fresh = [total(t) for t in over(advance, none)]
            ratio = [f / n for f, n in zip(fresh, norm)]
            left = [combine(l, -z, [0.0] + a) for l, z, a in zip(left, size, aim)]
            aim = [combine(l, q, a) for l, q, a in zip(left, ratio, aim)]

            def turn(d, carry, ratio=ratio):
                for v, _, x in each(d):
                    pole[v, x + 1] = residual[v, x] + ratio[v] * pole[v, x + 1]
                return carry

            over(turn, 0)
            wrap(pole, width)
            norm = fresh

    def finish(d, carry):
        grams = list(carry)
        for x in (2 * d, 2 * d + 1):
            a, b = (answer[v, x] + size[v] * pole[v, x + 1] for v in range(VECTORS))
            answer[0, x], answer[1, x] = a, b
            grams = [grams[0] + a * a, grams[1] + a * b, grams[2] + b * b]
        return (*grams, carry[3])

    *grams, _ = over(finish, (zero,) * 4)
    packed_sums = sum((packed[n] for n in range(1, count // 2)), packed[0])
    sums = unpack_rows(packed_sums, 3 + VECTORS * VECTORS * POWERS)

    def heights_with(i, j):
        first = 3 + (i * VECTORS + j) * POWERS
        return sum(c * t for c, t in zip(taken[j], sums[first : first + POWERS]))

    cells = (levels + 1) * width * sub * LANES
    one, mix, two = (
        (sums[n] + total(grams[n]) + (heights_with(i, j) + heights_with(j, i))) / cells
        for n, (i, j) in enumerate(((0, 0), (0, 1), (1, 1)))
    )
    scale_one = jnp.sqrt(one + EPSILON)
    cross = mix / scale_one
    rest = two - 2.0 * cross * cross + cross * cross * one / (one + EPSILON)
    scale_two = jnp.sqrt(rest + EPSILON)
    over_one, over_two = 1.0 / scale_one, 1.0 / scale_two

    def scale(k, carry):
        unit = tracer[0, k] * over_one
        scaled[0, k] = unit
        scaled[1, k] = (tracer[1, k] - cross * unit) * over_two
        return carry

    lax.fori_loop(0, levels, scale, 0, unroll=steps(levels, 50))
    for c in range(2):
        x = 2 * me + c
        first, second = (
            jnp.where(depth[x] > 0, surface[v, pl.ds(c, sub, stride=2), :], 0.0) + answer[v, x]
            for v in range(VECTORS)
        )
        unit = first * over_one
        surface_out[0, pl.ds(c, sub, stride=2), :] = unit
        surface_out[1, pl.ds(c, sub, stride=2), :] = (second - cross * unit) * over_two
    for i, value in enumerate((scale_one, cross, scale_two)):
        growth[i] = value[0, 0]


def tiled(array):
    *lead, columns, rows = array.shape
    split = array.reshape(*lead, columns, rows // LANES, LANES)
    return jnp.swapaxes(split, -3, -2).reshape(*lead, rows // LANES * columns, LANES)


def untiled(array, columns):
    *lead, high, lanes = array.shape
    split = array.reshape(*lead, high // columns, columns, lanes)
    return jnp.swapaxes(split, -3, -2).reshape(*lead, columns, high // columns * lanes)


def swap(array, mask):
    count = lax.axis_size("lon")
    return lax.ppermute(array, "lon", [(i, i ^ mask) for i in range(count)])


def chip_masks(count):
    lists, loads = ([], []), [0, 0]
    for mask in range(count // 2 - 1, 0, -1):
        core = int(loads[1] < loads[0])
        lists[core].append(mask)
        loads[core] += mask % 2 + mask // 2
    longest = max(map(len, lists))
    return list(zip(*(one + [0] * (longest - len(one)) for one in lists)))


def gather(block):
    count = lax.axis_size("lon")
    beside = swap(block, 1)
    pair = jnp.concatenate([block[:RIM], beside[:RIM], block[RIM:] + beside[RIM:]])
    fetched = []
    for masks in chip_masks(count):
        moves = [(i, i ^ (2 * masks[i % 2])) for i in range(count) if masks[i % 2]]
        fetched.append(lax.ppermute(pair, "lon", moves))
    return pair, *fetched, *(swap(one, 1) for one in fetched)


def on_device(tracer_pert, surface_pert, zonal_flow, merid_flow, bottom_level):
    vectors, levels, columns, rows = tracer_pert.shape
    count = lax.axis_size("lon")
    sub = rows // LANES
    assert vectors == VECTORS and columns == 2 and rows % LANES == 0
    assert count >= 8 and count & (count - 1) == 0
    width = 2 * count
    f32 = jnp.float32
    vmem = pl.BlockSpec(memory_space=pltpu.VMEM)
    hbm = pl.BlockSpec(memory_space=pltpu.HBM)
    params = pltpu.CompilerParams(vmem_limit_bytes=24 * 2**20)

    def shaped(*shape):
        return jax.ShapeDtypeStruct((*shape, sub, LANES), f32)

    def held(*shape):
        return pltpu.VMEM((*shape, sub, LANES), f32)

    both = pltpu.VMEM((vectors, levels, sub * 2, LANES), f32)
    tracer_pert, zonal_flow, merid_flow = map(tiled, (tracer_pert, zonal_flow, merid_flow))
    outward = [(i, (i + 1) % count if i % 2 else (i - 1) % count) for i in range(count)]
    part = levels // 2
    surface, bottom = tiled(surface_pert), tiled(bottom_level)

    pinned = [
        pltpu.with_memory_space_constraint(array, pltpu.HBM)
        for array in (tracer_pert, zonal_flow, surface, bottom)
    ]
    edge, flow_edge = pl.pallas_call(
        functools.partial(edge_kernel, levels, sub),
        out_shape=(shaped(VECTORS * levels + RIM), shaped(part)),
        in_specs=[hbm] * 4,
        out_specs=(vmem, vmem),
        scratch_shapes=[
            both,
            pltpu.VMEM((part, sub * 2, LANES), f32),
            pltpu.VMEM((vectors, sub * 2, LANES), f32),
            pltpu.VMEM((sub * 2, LANES), jnp.int32),
            pltpu.SemaphoreType.DMA((VECTORS + 3,)),
        ],
        compiler_params=pltpu.CompilerParams(vmem_limit_bytes=16 * 2**20),
        name="edge_columns",
    )(*pinned)
    flow_half = lax.ppermute(flow_edge, "lon", outward)
    edge_far = lax.ppermute(edge, "lon", outward)
    flow_other = lax.ppermute(flow_half, "grp", [(0, 1), (1, 0)])
    cross, mate, raw, mate_raw, flow_in, mate_flow = pl.pallas_call(
        functools.partial(first_kernel, levels, sub),
        out_shape=(
            shaped(VECTORS * levels),
            shaped(VECTORS * levels),
            shaped(VECTORS * levels),
            shaped(VECTORS * levels),
            shaped(levels),
            shaped(levels + RIM),
        ),
        in_specs=[pl.BlockSpec(memory_space=pl.ANY)] + [vmem] * 5,
        out_specs=(vmem,) * 6,
        compiler_params=params,
        name="partial_step",
    )(edge, tracer_pert, zonal_flow, merid_flow, surface, bottom)
    cross_far = lax.ppermute(cross, "lon", outward)
    mate_far, mate_raw_far, mate_flow_far = (swap(x, 1) for x in (mate, mate_raw, mate_flow))
    done, *rest = pl.pallas_call(
        functools.partial(halo_kernel, levels, sub),
        out_shape=(
            shaped(vectors, levels),
            shaped(vectors, levels),
            shaped(levels),
            shaped(VECTORS + 3),
            shaped(POWERS + 1, vectors, 2),
        ),
        in_specs=[vmem] * 13,
        out_specs=(vmem,) * 5,
        scratch_shapes=[held(levels)],
        compiler_params=params,
        name="both_steps",
    )(
        raw, cross, mate, mate_raw, flow_in, mate_flow,
        edge_far, mate_far, mate_raw_far, mate_flow_far, flow_half, flow_other, merid_flow,
    )
    column, message = pl.pallas_call(
        functools.partial(second_kernel, levels),
        out_shape=(shaped(vectors, levels), shaped(BLOCKS)),
        in_specs=[vmem] * 6,
        out_specs=(vmem, vmem),
        compiler_params=params,
        name="outer_column",
    )(cross_far, *rest, mate_flow)
    tracer = pl.pallas_call(
        functools.partial(interleave_kernel, levels, sub),
        out_shape=jax.ShapeDtypeStruct((vectors, levels, sub * 2, LANES), f32),
        in_specs=[vmem] * 2,
        out_specs=vmem,
        compiler_params=params,
        name="interleave",
    )(column, done)
    blocks = gather(message)
    tracer_vec, surface_vec, growth = pl.pallas_call(
        functools.partial(third_kernel, levels, sub, count),
        out_shape=(
            jax.ShapeDtypeStruct((vectors, levels, sub * 2, LANES), f32),
            jax.ShapeDtypeStruct((vectors, sub * 2, LANES), f32),
            jax.ShapeDtypeStruct((3,), f32),
        ),
        in_specs=[vmem] * (len(blocks) + 2),
        out_specs=(vmem, vmem, pl.BlockSpec(memory_space=pltpu.SMEM)),
        scratch_shapes=[
            held(vectors, width + 2),
            *[held(vectors, width)] * 3,
            held(width),
            held(width + 1),
            held(width),
            held(width),
            held(count // 2),
        ],
        compiler_params=pltpu.CompilerParams(vmem_limit_bytes=32 * 2**20),
        name="surface_and_scale",
    )(*blocks, surface, tracer)
    return (untiled(tracer_vec, 2), untiled(surface_vec, 2), growth)


def solution(mesh):
    placed = (
        P("grp", None, "lon", None),
        P("grp", "lon", None),
        P(None, "lon", None),
        P(None, "lon", None),
        P("lon", None),
    )
    return jax.shard_map(
        on_device,
        mesh=mesh,
        in_specs=placed,
        out_specs=(P("grp", None, "lon", None), P("grp", "lon", None), P("grp")),
        check_vma=False,
    )
```

```python
import functools

import jax
import jax.numpy as jnp
from jax import lax
from jax.experimental import pallas as pl
from jax.experimental.pallas import tpu as pltpu
from jax.sharding import PartitionSpec as P

ITERS = 3


DIFFUSIVITY = 0.5
TIME_STEP = 0.2
SURFACE_COUPLING = 0.5
STERIC_GAIN = 2.0
EPSILON = 1e-06

LANES = 128
VECTORS = 2
SLOPE = 0.25 * TIME_STEP
SPREAD = TIME_STEP * DIFFUSIVITY
DEPTHS = VECTORS * 2
RIM = DEPTHS + 2
GRAMS = RIM
BLOCKS = GRAMS + 1
POWERS = ITERS


def next_row(tile):
    turned = pltpu.roll(tile, LANES - 1, 1)
    carried = pltpu.roll(turned, tile.shape[0] - 1, 0)
    lane = lax.broadcasted_iota(jnp.int32, tile.shape, 1)
    return jnp.where(lane == LANES - 1, carried, turned)


def prior_row(tile):
    turned = pltpu.roll(tile, 1, 1)
    carried = pltpu.roll(turned, 1, 0)
    lane = lax.broadcasted_iota(jnp.int32, tile.shape, 1)
    return jnp.where(lane == 0, carried, turned)


def wall_depth(depth):
    subs, lane = (lax.broadcasted_iota(jnp.int32, depth.shape, axis) for axis in (0, 1))
    last = (subs == depth.shape[0] - 1) & (lane == LANES - 1)
    return jnp.where(last, jnp.zeros_like(depth), jnp.minimum(depth, next_row(depth)))


def face_pair(level, face_depth, flow_sum):
    slope = SLOPE * flow_sum
    open_face = level < face_depth
    return (
        jnp.where(open_face, slope + SPREAD, 0.0),
        jnp.where(open_face, slope - SPREAD, 0.0),
    )


def outflow(pair, near, far):
    return pair[0] * near + pair[1] * far


def side_pairs(level, depths, flow):
    return (
        face_pair(level, depths[0], flow + next_row(flow)),
        face_pair(level, depths[1], -(flow + prior_row(flow))),
    )


def divergence_y(pairs, tile):
    return outflow(pairs[0], tile, next_row(tile)) + outflow(pairs[1], tile, prior_row(tile))


def side_depths(depth):
    north = wall_depth(depth)
    return north, prior_row(north)


def orientation():
    outer = lax.rem(lax.axis_index("lon"), 2)
    return outer, 1 - outer, (2 * outer - 1).astype(jnp.float32)


def steps(count, most):
    return max(u for u in range(1, most + 1) if count % u == 0)


def share(levels):
    assert lax.axis_size("grp") == 2 and levels % 2 == 0
    part = levels // 2
    return lax.axis_index("grp") * (levels - part), part


def pack_rim(sub, surface, bottom, target, base):
    for c in range(2):
        for v in range(VECTORS):
            target[base + v * 2 + c] = surface[v, pl.ds(c, sub, stride=2), :]
        target[base + DEPTHS + c] = bottom[pl.ds(c, sub, stride=2), :].astype(jnp.float32)


def edge_kernel(
    levels, sub, tracer_hbm, zonal_hbm, surface_hbm, bottom_hbm, edge, flow,
    tracer, zonal, surface, bottom, sems,
):
    outer, _, _ = orientation()
    start, part = share(levels)
    pairs = [
        (zonal_hbm.at[pl.ds(start, part)], zonal),
        (surface_hbm, surface),
        (bottom_hbm, bottom),
        *((tracer_hbm.at[v], tracer.at[v]) for v in range(VECTORS)),
    ]
    copies = [
        pltpu.make_async_copy(source, target, sems.at[i]) for i, (source, target) in enumerate(pairs)
    ]
    for copy in copies:
        copy.start()
    for copy in copies[:3]:
        copy.wait()

    def take(k, carry):
        flow[k] = zonal[k, pl.ds(outer, sub, stride=2), :]
        return carry

    lax.fori_loop(0, part, take, 0, unroll=steps(part, 25))
    pack_rim(sub, surface, bottom, edge, VECTORS * levels)
    for v in range(VECTORS):
        copies[3 + v].wait()

        def body(k, carry, v=v):
            edge[v * levels + k] = tracer[v, k, pl.ds(outer, sub, stride=2), :]
            return carry

        lax.fori_loop(0, levels, body, 0, unroll=steps(levels, 25))


def first_kernel(
    levels, sub, edge, tracer_hbm, zonal_hbm, merid_hbm, surface_hbm, bottom_hbm,
    cross, mate, raw, mate_raw, flow_in, mate_flow,
    tracer, zonal, merid, surface, bottom, sems,
):
    del edge
    pairs = (
        (surface_hbm, surface),
        (bottom_hbm, bottom),
        (zonal_hbm, zonal),
        (merid_hbm, merid),
        (tracer_hbm, tracer),
    )
    copies = [
        pltpu.make_async_copy(source, target, sems.at[i]) for i, (source, target) in enumerate(pairs)
    ]
    for copy in copies:
        copy.start()
    for copy in copies:
        copy.wait()
    outer, inner, sign = orientation()

    def column(ref, where, *lead):
        return ref[(*lead, pl.ds(where, sub, stride=2), slice(None))]

    depth = [column(bottom, where).astype(jnp.float32) for where in (outer, inner)]
    between = jnp.minimum(*depth)
    along = [side_depths(d) for d in depth]
    pack_rim(sub, surface, bottom, mate_flow, levels)

    def body(k, carry):
        level = k.astype(jnp.float32)
        flow = [column(zonal, where, k) for where in (outer, inner)]
        turn = [column(merid, where, k) for where in (outer, inner)]
        middle = face_pair(level, between, -sign * (flow[0] + flow[1]))
        sides = [side_pairs(level, along[c], turn[c]) for c in range(2)]
        for v in range(VECTORS):
            cells = [column(tracer, where, v, k) for where in (outer, inner)]
            flux = outflow(middle, *cells)
            kept = [
                jnp.where(level < depth[c], cells[c], 0.0) - divergence_y(sides[c], cells[c])
                for c in range(2)
            ]
            cross[v * levels + k] = kept[0] - flux
            raw[v * levels + k] = cells[0]
            mate[v * levels + k] = kept[1] + flux
            mate_raw[v * levels + k] = cells[1]
        flow_in[k] = flow[0]
        mate_flow[k] = flow[1]
        return carry

    lax.fori_loop(0, levels, body, 0, unroll=steps(levels, 10))


def wrap(pole, width):
    for v in range(VECTORS):
        pole[v, 0] = pole[v, width]
        pole[v, width + 1] = pole[v, 1]


def spread(pole, face_x, face_y, face_z, v, x):
    west, centre, east = (pole[v, x + j] for j in range(3))
    return (face_x[x + 1] * (east - centre) - face_x[x] * (centre - west)) + (
        face_y[x] * (next_row(centre) - centre) - face_z[x] * (centre - prior_row(centre))
    )


def halo_kernel(
    levels, sub, raw, cross, mate, mate_raw, flow_in, mate_flow,
    raw_far, mate_far, mate_raw_far, mate_flow_far, flow_half, flow_other, merid,
    done, base, weight, sums, powers, flow_far,
):
    outer, inner, sign = orientation()
    start, part = share(levels)

    def unpack(i, carry):
        flow_far[start + i] = flow_half[i]
        flow_far[levels - part - start + i] = flow_other[i]
        return carry

    lax.fori_loop(0, part, unpack, 0, unroll=steps(part, 10))
    powers_of_heights(levels, mate_flow, mate_flow_far, raw_far, powers)
    near, far = (raw, mate_raw), (raw_far, mate_raw_far)
    rim = levels + DEPTHS
    depth = [mate_flow[rim + where] for where in (outer, inner)]
    beside = [
        jnp.minimum(depth[0], raw_far[VECTORS * levels + DEPTHS + inner]),
        jnp.minimum(depth[1], mate_flow_far[rim + outer]),
    ]
    between = jnp.minimum(*depth)
    along = [side_depths(d) for d in depth]
    zero = jnp.zeros_like(between)

    def body(k, carry):
        level = k.astype(jnp.float32)
        flow = [flow_in[k], mate_flow[k]]
        beyond = [flow_far[k], mate_flow_far[k]]
        turn = [merid[k, pl.ds(where, sub, stride=2), :] for where in (outer, inner)]
        middle = face_pair(level, between, -sign * (flow[0] + flow[1]))
        edges = [
            face_pair(level, beside[c], (sign, -sign)[c] * (flow[c] + beyond[c])) for c in range(2)
        ]
        sides = [side_pairs(level, along[c], turn[c]) for c in range(2)]
        weight[k] = edges[0][1]
        totals, grams = list(carry[:VECTORS]), list(carry[VECTORS:])
        fresh = []
        for v in range(VECTORS):
            row = v * levels + k
            flux = [outflow(edges[c], near[c][row], far[c][row]) for c in range(2)]
            outside, inside = cross[row] - flux[0], mate[row] - flux[1]
            other = mate_far[row] + flux[1]
            crossing = outflow(middle, outside, inside)
            base[v, k] = (
                outside
                - outflow(edges[0], outside, flux[0])
                - crossing
                - divergence_y(sides[0], outside)
            )
            value = (
                inside - outflow(edges[1], inside, other) + crossing - divergence_y(sides[1], inside)
            )
            done[v, k] = value
            totals[v] = totals[v] + value
            fresh.append(value)
        return (*totals, *add_products(grams, *fresh))

    found = lax.fori_loop(0, levels, body, (zero,) * (VECTORS + 3), unroll=steps(levels, 10))
    for row, tile in enumerate(found):
        sums[row] = tile


def interleave_kernel(levels, sub, column, done, tracer):
    outer, inner, _ = orientation()

    def body(k, carry):
        for v in range(VECTORS):
            tracer[v, k, pl.ds(outer, sub, stride=2), :] = column[v, k]
            tracer[v, k, pl.ds(inner, sub, stride=2), :] = done[v, k]
        return carry

    lax.fori_loop(0, levels, body, 0, unroll=steps(levels, 10))


def add_products(grams, a, b):
    return [grams[0] + a * a, grams[1] + a * b, grams[2] + b * b]


def second_kernel(levels, cross_far, base, weight, inside, powers, mate_flow, column, message):
    outer, inner, _ = orientation()
    zero = jnp.zeros(powers.shape[-2:], jnp.float32)

    def body(k, carry):
        totals, fresh = [], []
        for v in range(VECTORS):
            value = base[v, k] - weight[k] * cross_far[v * levels + k]
            column[v, k] = value
            totals.append(carry[v] + value)
            fresh.append(value)
        return (*totals, *add_products(carry[VECTORS:], *fresh))

    carry = lax.fori_loop(0, levels, body, (zero,) * (VECTORS + 3), unroll=steps(levels, 50))
    gain = STERIC_GAIN / levels
    rows = [a + inside[VECTORS + n] for n, a in enumerate(carry[VECTORS:])]
    residual = []
    for v in range(VECTORS):
        residual.append(
            [gain * total_of + powers[POWERS, v, c] for c, total_of in enumerate((carry[v], inside[v]))]
        )
        for c, where in enumerate((outer, inner)):
            message[v * 2 + where] = residual[v][c]

    def product(one, two):
        return one[0] * two[0] + one[1] * two[1]

    heights = [[powers[0, v, c] for c in range(2)] for v in range(VECTORS)]
    for n, (i, j) in enumerate(((0, 0), (0, 1), (1, 1))):
        rows[n] = rows[n] + product(heights[i], heights[j])
    for i in range(VECTORS):
        for j in range(VECTORS):
            for m in range(POWERS):
                rows.append(product([powers[m, i, c] for c in range(2)], residual[j]))
    message[GRAMS] = pack_rows(rows)
    for c in range(2):
        message[DEPTHS + c] = mate_flow[levels + DEPTHS + c]


def pack_rows(tiles):
    shape = tiles[0].shape
    sub, lane = (lax.broadcasted_iota(jnp.int32, shape, axis) for axis in (0, 1))
    half = shape[1] // 2
    packed = jnp.zeros(shape, jnp.float32)
    for n, tile in enumerate(tiles):
        row = jnp.sum(tile, axis=0, keepdims=True)
        row = row + pltpu.roll(row, half, 1)
        place = (sub == n % shape[0]) & ((lane < half) == (n < shape[0]))
        packed = jnp.where(place, row, packed)
    return packed


def unpack_rows(packed, count):
    lane = lax.broadcasted_iota(jnp.int32, packed.shape, 1)
    low = lane < packed.shape[1] // 2
    sums = [
        jnp.sum(jnp.where(side, packed, 0.0), axis=1, keepdims=True)
        for side in (low, jnp.logical_not(low))
    ]
    size = packed.shape[0]
    return [sums[n // size][n % size : n % size + 1] for n in range(count)]


def powers_of_heights(levels, mate_flow, mate_flow_far, raw_far, powers):
    outer, inner, _ = orientation()
    line = [
        (mate_flow_far, levels, inner),
        (mate_flow_far, levels, outer),
        (mate_flow, levels, inner),
        (mate_flow, levels, outer),
        (raw_far, VECTORS * levels, inner),
        (raw_far, VECTORS * levels, outer),
    ]
    depth = [ref[base + DEPTHS + where] for ref, base, where in line]
    faces = [SURFACE_COUPLING * jnp.minimum(a, b) for a, b in zip(depth, depth[1:])]
    sides = [side_depths(SURFACE_COUPLING * d) for d in depth[1:5]]
    for v in range(VECTORS):
        field = [
            jnp.where(d > 0, ref[base + v * 2 + where], 0.0)
            for d, (ref, base, where) in zip(depth, line)
        ]

        def bend(field, first, last):
            found = []
            for j in range(first, last):
                west, centre, east = field[j - 1 : j + 2]
                north, south = sides[j - 1]
                found.append(
                    (faces[j] * (east - centre) - faces[j - 1] * (centre - west))
                    + (north * (next_row(centre) - centre) - south * (centre - prior_row(centre)))
                )
            return found

        lap = bend(field, 1, 5)
        image = [None] + [h - p for h, p in zip(field[1:5], lap)]
        again = [p - q for p, q in zip(image[2:4], bend(image, 2, 4))]
        for c, where in enumerate((3, 2)):
            powers[0, v, c] = field[where]
            powers[1, v, c] = image[where]
            powers[2, v, c] = again[where - 2]
            powers[POWERS, v, c] = lap[where - 1]


def total(tile):
    return jnp.sum(jnp.sum(tile, axis=0, keepdims=True), axis=1, keepdims=True)


def combine(one, factor, two):
    longest = max(len(one), len(two))
    one, two = (list(c) + [0.0] * (longest - len(c)) for c in (one, two))
    return [a + factor * b for a, b in zip(one, two)]


def third_kernel(levels, sub, count, *refs):
    masks_of = chip_masks(count)
    blocks = 1 + 2 * len(masks_of)
    (surface, tracer, scaled, surface_out, growth) = refs[blocks : blocks + 5]
    (pole, residual, answer, image, depth, face_x, face_y, face_z, packed) = refs[blocks + 5 :]
    width = 2 * count
    me = lax.axis_index("lon")
    core = lax.rem(me, 2)
    zero = jnp.zeros((sub, LANES), jnp.float32)
    none = (zero,) * VECTORS

    def place(first, block):
        packed[first // 2] = block[2 * RIM]
        for slot in range(2):
            for c in range(2):
                x = 2 * (first ^ slot) + c
                depth[x] = block[RIM * slot + DEPTHS + c]
                for v in range(VECTORS):
                    value = block[RIM * slot + v * 2 + c]
                    residual[v, x] = value
                    pole[v, x + 1] = value

    place(me, refs[0])
    for n, block in enumerate(refs[1:blocks]):
        flip, masks = n // len(masks_of), masks_of[n % len(masks_of)]
        mask = jnp.where((core ^ flip) == 0, *masks)

        def put(first=me ^ flip ^ (2 * mask), block=block):
            place(first, block)

        if all(masks):
            put()
        else:
            pl.when(mask > 0)(put)

    def over(body, init):
        return lax.fori_loop(0, count, body, init, unroll=steps(count, 16))

    def each(d):
        return [(v, c, 2 * d + c) for v in range(VECTORS) for c in range(2)]

    def prepare(d, carry):
        for x in (2 * d, 2 * d + 1):
            here, after = depth[x], depth[lax.rem(x + 1, width)]
            face_x[x + 1] = SURFACE_COUPLING * jnp.minimum(here, after)
            north, south = side_depths(here)
            face_y[x] = SURFACE_COUPLING * north
            face_z[x] = SURFACE_COUPLING * south
        return carry

    over(prepare, 0)
    face_x[0] = face_x[width]
    wrap(pole, width)

    def start(d, carry):
        sums = list(carry)
        for v, _, x in each(d):
            sums[v] = sums[v] + residual[v, x] * residual[v, x]
        return tuple(sums)

    norm = [total(t) for t in over(start, none)]
    taken, left, aim = ([[v for _ in range(VECTORS)] for v in ([], [1.0], [1.0])])

    def apply(d, carry):
        sums = list(carry)
        for v, _, x in each(d):
            centre = pole[v, x + 1]
            value = centre - spread(pole, face_x, face_y, face_z, v, x)
            image[v, x] = value
            sums[v] = sums[v] + centre * value
        return tuple(sums)

    for iteration in range(ITERS):
        energy = [total(t) for t in over(apply, none)]
        size = [n / e for n, e in zip(norm, energy)]
        taken = [combine(s, z, a) for s, z, a in zip(taken, size, aim)]
        if iteration + 1 < ITERS:

            def advance(d, carry, size=size, first=iteration == 0):
                sums = list(carry)
                for v, _, x in each(d):
                    gone = size[v] * pole[v, x + 1]
                    answer[v, x] = gone if first else answer[v, x] + gone
                    value = residual[v, x] - size[v] * image[v, x]
                    residual[v, x] = value
                    sums[v] = sums[v] + value * value
                return tuple(sums)

            fresh = [total(t) for t in over(advance, none)]
            ratio = [f / n for f, n in zip(fresh, norm)]
            left = [combine(l, -z, [0.0] + a) for l, z, a in zip(left, size, aim)]
            aim = [combine(l, q, a) for l, q, a in zip(left, ratio, aim)]

            def turn(d, carry, ratio=ratio):
                for v, _, x in each(d):
                    pole[v, x + 1] = residual[v, x] + ratio[v] * pole[v, x + 1]
                return carry

            over(turn, 0)
            wrap(pole, width)
            norm = fresh

    def finish(d, carry):
        grams = list(carry)
        for x in (2 * d, 2 * d + 1):
            a, b = (answer[v, x] + size[v] * pole[v, x + 1] for v in range(VECTORS))
            answer[0, x], answer[1, x] = a, b
            grams = [grams[0] + a * a, grams[1] + a * b, grams[2] + b * b]
        return (*grams, carry[3])

    *grams, _ = over(finish, (zero,) * 4)
    packed_sums = sum((packed[n] for n in range(1, count // 2)), packed[0])
    sums = unpack_rows(packed_sums, 3 + VECTORS * VECTORS * POWERS)

    def heights_with(i, j):
        first = 3 + (i * VECTORS + j) * POWERS
        return sum(c * t for c, t in zip(taken[j], sums[first : first + POWERS]))

    cells = (levels + 1) * width * sub * LANES
    one, mix, two = (
        (sums[n] + total(grams[n]) + (heights_with(i, j) + heights_with(j, i))) / cells
        for n, (i, j) in enumerate(((0, 0), (0, 1), (1, 1)))
    )
    scale_one = jnp.sqrt(one + EPSILON)
    cross = mix / scale_one
    rest = two - 2.0 * cross * cross + cross * cross * one / (one + EPSILON)
    scale_two = jnp.sqrt(rest + EPSILON)
    over_one, over_two = 1.0 / scale_one, 1.0 / scale_two

    def scale(k, carry):
        unit = tracer[0, k] * over_one
        scaled[0, k] = unit
        scaled[1, k] = (tracer[1, k] - cross * unit) * over_two
        return carry

    lax.fori_loop(0, levels, scale, 0, unroll=steps(levels, 50))
    for c in range(2):
        x = 2 * me + c
        first, second = (
            jnp.where(depth[x] > 0, surface[v, pl.ds(c, sub, stride=2), :], 0.0) + answer[v, x]
            for v in range(VECTORS)
        )
        unit = first * over_one
        surface_out[0, pl.ds(c, sub, stride=2), :] = unit
        surface_out[1, pl.ds(c, sub, stride=2), :] = (second - cross * unit) * over_two
    for i, value in enumerate((scale_one, cross, scale_two)):
        growth[i] = value[0, 0]


def tiled(array):
    *lead, columns, rows = array.shape
    split = array.reshape(*lead, columns, rows // LANES, LANES)
    return jnp.swapaxes(split, -3, -2).reshape(*lead, rows // LANES * columns, LANES)


def untiled(array, columns):
    *lead, high, lanes = array.shape
    split = array.reshape(*lead, high // columns, columns, lanes)
    return jnp.swapaxes(split, -3, -2).reshape(*lead, columns, high // columns * lanes)


def swap(array, mask):
    count = lax.axis_size("lon")
    return lax.ppermute(array, "lon", [(i, i ^ mask) for i in range(count)])


def chip_masks(count):
    lists, loads = ([], []), [0, 0]
    for mask in range(count // 2 - 1, 0, -1):
        core = int(loads[1] < loads[0])
        lists[core].append(mask)
        loads[core] += mask % 2 + mask // 2
    longest = max(map(len, lists))
    return list(zip(*(one + [0] * (longest - len(one)) for one in lists)))


def gather(block):
    count = lax.axis_size("lon")
    beside = swap(block, 1)
    pair = jnp.concatenate([block[:RIM], beside[:RIM], block[RIM:] + beside[RIM:]])
    fetched = []
    for masks in chip_masks(count):
        moves = [(i, i ^ (2 * masks[i % 2])) for i in range(count) if masks[i % 2]]
        fetched.append(lax.ppermute(pair, "lon", moves))
    return pair, *fetched, *(swap(one, 1) for one in fetched)


def on_device(tracer_pert, surface_pert, zonal_flow, merid_flow, bottom_level):
    vectors, levels, columns, rows = tracer_pert.shape
    count = lax.axis_size("lon")
    sub = rows // LANES
    assert vectors == VECTORS and columns == 2 and rows % LANES == 0
    assert count >= 8 and count & (count - 1) == 0
    width = 2 * count
    f32 = jnp.float32
    vmem = pl.BlockSpec(memory_space=pltpu.VMEM)
    hbm = pl.BlockSpec(memory_space=pltpu.HBM)
    params = pltpu.CompilerParams(vmem_limit_bytes=24 * 2**20)

    def shaped(*shape):
        return jax.ShapeDtypeStruct((*shape, sub, LANES), f32)

    def held(*shape):
        return pltpu.VMEM((*shape, sub, LANES), f32)

    both = pltpu.VMEM((vectors, levels, sub * 2, LANES), f32)
    tracer_pert, zonal_flow, merid_flow = map(tiled, (tracer_pert, zonal_flow, merid_flow))
    outward = [(i, (i + 1) % count if i % 2 else (i - 1) % count) for i in range(count)]
    part = levels // 2
    surface, bottom = tiled(surface_pert), tiled(bottom_level)

    pinned = [
        pltpu.with_memory_space_constraint(array, pltpu.HBM)
        for array in (tracer_pert, zonal_flow, surface, bottom)
    ]
    edge, flow_edge = pl.pallas_call(
        functools.partial(edge_kernel, levels, sub),
        out_shape=(shaped(VECTORS * levels + RIM), shaped(part)),
        in_specs=[hbm] * 4,
        out_specs=(vmem, vmem),
        scratch_shapes=[
            both,
            pltpu.VMEM((part, sub * 2, LANES), f32),
            pltpu.VMEM((vectors, sub * 2, LANES), f32),
            pltpu.VMEM((sub * 2, LANES), jnp.int32),
            pltpu.SemaphoreType.DMA((VECTORS + 3,)),
        ],
        compiler_params=pltpu.CompilerParams(vmem_limit_bytes=16 * 2**20),
        name="edge_columns",
    )(*pinned)
    flow_half = lax.ppermute(flow_edge, "lon", outward)
    edge_far = lax.ppermute(edge, "lon", outward)
    flow_other = lax.ppermute(flow_half, "grp", [(0, 1), (1, 0)])
    cross, mate, raw, mate_raw, flow_in, mate_flow = pl.pallas_call(
        functools.partial(first_kernel, levels, sub),
        out_shape=(
            shaped(VECTORS * levels),
            shaped(VECTORS * levels),
            shaped(VECTORS * levels),
            shaped(VECTORS * levels),
            shaped(levels),
            shaped(levels + RIM),
        ),
        in_specs=[pl.BlockSpec(memory_space=pl.ANY)] + [hbm] * 5,
        out_specs=(vmem,) * 6,
        scratch_shapes=[
            both,
            pltpu.VMEM((levels, sub * 2, LANES), f32),
            pltpu.VMEM((levels, sub * 2, LANES), f32),
            pltpu.VMEM((vectors, sub * 2, LANES), f32),
            pltpu.VMEM((sub * 2, LANES), jnp.int32),
            pltpu.SemaphoreType.DMA((5,)),
        ],
        compiler_params=params,
        name="partial_step",
    )(
        edge, pinned[0], pinned[1], pltpu.with_memory_space_constraint(merid_flow, pltpu.HBM),
        pinned[2], pinned[3],
    )
    cross_far = lax.ppermute(cross, "lon", outward)
    mate_far, mate_raw_far, mate_flow_far = (swap(x, 1) for x in (mate, mate_raw, mate_flow))
    done, *rest = pl.pallas_call(
        functools.partial(halo_kernel, levels, sub),
        out_shape=(
            shaped(vectors, levels),
            shaped(vectors, levels),
            shaped(levels),
            shaped(VECTORS + 3),
            shaped(POWERS + 1, vectors, 2),
        ),
        in_specs=[vmem] * 13,
        out_specs=(vmem,) * 5,
        scratch_shapes=[held(levels)],
        compiler_params=params,
        name="both_steps",
    )(
        raw, cross, mate, mate_raw, flow_in, mate_flow,
        edge_far, mate_far, mate_raw_far, mate_flow_far, flow_half, flow_other, merid_flow,
    )
    column, message = pl.pallas_call(
        functools.partial(second_kernel, levels),
        out_shape=(shaped(vectors, levels), shaped(BLOCKS)),
        in_specs=[vmem] * 6,
        out_specs=(vmem, vmem),
        compiler_params=params,
        name="outer_column",
    )(cross_far, *rest, mate_flow)
    tracer = pl.pallas_call(
        functools.partial(interleave_kernel, levels, sub),
        out_shape=jax.ShapeDtypeStruct((vectors, levels, sub * 2, LANES), f32),
        in_specs=[vmem] * 2,
        out_specs=vmem,
        compiler_params=params,
        name="interleave",
    )(column, done)
    blocks = gather(message)
    tracer_vec, surface_vec, growth = pl.pallas_call(
        functools.partial(third_kernel, levels, sub, count),
        out_shape=(
            jax.ShapeDtypeStruct((vectors, levels, sub * 2, LANES), f32),
            jax.ShapeDtypeStruct((vectors, sub * 2, LANES), f32),
            jax.ShapeDtypeStruct((3,), f32),
        ),
        in_specs=[vmem] * (len(blocks) + 2),
        out_specs=(vmem, vmem, pl.BlockSpec(memory_space=pltpu.SMEM)),
        scratch_shapes=[
            held(vectors, width + 2),
            *[held(vectors, width)] * 3,
            held(width),
            held(width + 1),
            held(width),
            held(width),
            held(count // 2),
        ],
        compiler_params=pltpu.CompilerParams(vmem_limit_bytes=32 * 2**20),
        name="surface_and_scale",
    )(*blocks, surface, tracer)
    return (untiled(tracer_vec, 2), untiled(surface_vec, 2), growth)


def solution(mesh):
    placed = (
        P("grp", None, "lon", None),
        P("grp", "lon", None),
        P(None, "lon", None),
        P(None, "lon", None),
        P("lon", None),
    )
    return jax.shard_map(
        on_device,
        mesh=mesh,
        in_specs=placed,
        out_specs=(P("grp", None, "lon", None), P("grp", "lon", None), P("grp")),
        check_vma=False,
    )
```

```python
import functools

import jax
import jax.numpy as jnp
from jax import lax
from jax.experimental import pallas as pl
from jax.experimental.pallas import tpu as pltpu
from jax.sharding import PartitionSpec as P

ITERS = 3


DIFFUSIVITY = 0.5
TIME_STEP = 0.2
SURFACE_COUPLING = 0.5
STERIC_GAIN = 2.0
EPSILON = 1e-06

LANES = 128
VECTORS = 2
SLOPE = 0.25 * TIME_STEP
SPREAD = TIME_STEP * DIFFUSIVITY
DEPTHS = VECTORS * 2
RIM = DEPTHS + 2
GRAMS = RIM
BLOCKS = GRAMS + 1
POWERS = ITERS


def next_row(tile):
    turned = pltpu.roll(tile, LANES - 1, 1)
    carried = pltpu.roll(turned, tile.shape[0] - 1, 0)
    lane = lax.broadcasted_iota(jnp.int32, tile.shape, 1)
    return jnp.where(lane == LANES - 1, carried, turned)


def prior_row(tile):
    turned = pltpu.roll(tile, 1, 1)
    carried = pltpu.roll(turned, 1, 0)
    lane = lax.broadcasted_iota(jnp.int32, tile.shape, 1)
    return jnp.where(lane == 0, carried, turned)


def wall_depth(depth):
    subs, lane = (lax.broadcasted_iota(jnp.int32, depth.shape, axis) for axis in (0, 1))
    last = (subs == depth.shape[0] - 1) & (lane == LANES - 1)
    return jnp.where(last, jnp.zeros_like(depth), jnp.minimum(depth, next_row(depth)))


def face_pair(level, face_depth, flow_sum):
    slope = SLOPE * flow_sum
    open_face = level < face_depth
    return (
        jnp.where(open_face, slope + SPREAD, 0.0),
        jnp.where(open_face, slope - SPREAD, 0.0),
    )


def outflow(pair, near, far):
    return pair[0] * near + pair[1] * far


def side_pairs(level, depths, flow):
    return (
        face_pair(level, depths[0], flow + next_row(flow)),
        face_pair(level, depths[1], -(flow + prior_row(flow))),
    )


def divergence_y(pairs, tile):
    return outflow(pairs[0], tile, next_row(tile)) + outflow(pairs[1], tile, prior_row(tile))


def side_depths(depth):
    north = wall_depth(depth)
    return north, prior_row(north)


def orientation():
    outer = lax.rem(lax.axis_index("lon"), 2)
    return outer, 1 - outer, (2 * outer - 1).astype(jnp.float32)


def steps(count, most):
    return max(u for u in range(1, most + 1) if count % u == 0)


def share(levels):
    assert lax.axis_size("grp") == 2 and levels % 2 == 0
    part = levels // 2
    return lax.axis_index("grp") * (levels - part), part


def pack_rim(sub, surface, bottom, target, base):
    for c in range(2):
        for v in range(VECTORS):
            target[base + v * 2 + c] = surface[v, pl.ds(c, sub, stride=2), :]
        target[base + DEPTHS + c] = bottom[pl.ds(c, sub, stride=2), :].astype(jnp.float32)


def edge_kernel(
    levels, sub, tracer_hbm, zonal_hbm, surface_hbm, bottom_hbm, edge, flow,
    tracer, zonal, surface, bottom, sems,
):
    outer, _, _ = orientation()
    start, part = share(levels)
    pairs = [
        (zonal_hbm.at[pl.ds(start, part)], zonal),
        (surface_hbm, surface),
        (bottom_hbm, bottom),
        *((tracer_hbm.at[v], tracer.at[v]) for v in range(VECTORS)),
    ]
    copies = [
        pltpu.make_async_copy(source, target, sems.at[i]) for i, (source, target) in enumerate(pairs)
    ]
    for copy in copies:
        copy.start()
    for copy in copies[:3]:
        copy.wait()

    def take(k, carry):
        flow[k] = zonal[k, pl.ds(outer, sub, stride=2), :]
        return carry

    lax.fori_loop(0, part, take, 0, unroll=steps(part, 25))
    shared = jnp.where(lax.axis_index("grp") == 0, outer, 1 - outer)
    flow[part] = bottom[pl.ds(shared, sub, stride=2), :].astype(jnp.float32)
    for c in range(2):
        for v in range(VECTORS):
            edge[VECTORS * levels + v * 2 + c] = surface[v, pl.ds(c, sub, stride=2), :]
    for v in range(VECTORS):
        copies[3 + v].wait()

        def body(k, carry, v=v):
            edge[v * levels + k] = tracer[v, k, pl.ds(outer, sub, stride=2), :]
            return carry

        lax.fori_loop(0, levels, body, 0, unroll=steps(levels, 25))


def first_kernel(
    levels, sub, edge, tracer, zonal, merid, surface, bottom,
    cross, mate, raw, mate_raw, flow_in, mate_flow,
):
    del edge
    outer, inner, sign = orientation()

    def column(ref, where, *lead):
        return ref[(*lead, pl.ds(where, sub, stride=2), slice(None))]

    depth = [column(bottom, where).astype(jnp.float32) for where in (outer, inner)]
    between = jnp.minimum(*depth)
    along = [side_depths(d) for d in depth]
    pack_rim(sub, surface, bottom, mate_flow, levels)

    def body(k, carry):
        level = k.astype(jnp.float32)
        flow = [column(zonal, where, k) for where in (outer, inner)]
        turn = [column(merid, where, k) for where in (outer, inner)]
        middle = face_pair(level, between, -sign * (flow[0] + flow[1]))
        sides = [side_pairs(level, along[c], turn[c]) for c in range(2)]
        for v in range(VECTORS):
            cells = [column(tracer, where, v, k) for where in (outer, inner)]
            flux = outflow(middle, *cells)
            kept = [
                jnp.where(level < depth[c], cells[c], 0.0) - divergence_y(sides[c], cells[c])
                for c in range(2)
            ]
            cross[v * levels + k] = kept[0] - flux
            raw[v * levels + k] = cells[0]
            mate[v * levels + k] = kept[1] + flux
            mate_raw[v * levels + k] = cells[1]
        flow_in[k] = flow[0]
        mate_flow[k] = flow[1]
        return carry

    lax.fori_loop(0, levels, body, 0, unroll=steps(levels, 10))


def wrap(pole, width):
    for v in range(VECTORS):
        pole[v, 0] = pole[v, width]
        pole[v, width + 1] = pole[v, 1]


def spread(pole, face_x, face_y, face_z, v, x):
    west, centre, east = (pole[v, x + j] for j in range(3))
    return (face_x[x + 1] * (east - centre) - face_x[x] * (centre - west)) + (
        face_y[x] * (next_row(centre) - centre) - face_z[x] * (centre - prior_row(centre))
    )


def halo_kernel(
    levels, sub, raw, cross, mate, mate_raw, flow_in, mate_flow,
    raw_far, mate_far, mate_raw_far, mate_flow_far, flow_half, flow_other, merid,
    done, base, weight, sums, powers, flow_far,
):
    outer, inner, sign = orientation()
    start, part = share(levels)

    def unpack(i, carry):
        flow_far[start + i] = flow_half[i]
        flow_far[levels - part - start + i] = flow_other[i]
        return carry

    lax.fori_loop(0, part, unpack, 0, unroll=steps(part, 10))
    first = lax.axis_index("grp") == 0
    fetched, told = flow_half[part], flow_other[part]
    depth_far = [jnp.where(first, fetched, told), jnp.where(first, told, fetched)]
    powers_of_heights(levels, mate_flow, mate_flow_far, raw_far, depth_far, powers)
    near, far = (raw, mate_raw), (raw_far, mate_raw_far)
    rim = levels + DEPTHS
    depth = [mate_flow[rim + where] for where in (outer, inner)]
    beside = [
        jnp.minimum(depth[0], depth_far[0]),
        jnp.minimum(depth[1], mate_flow_far[rim + outer]),
    ]
    between = jnp.minimum(*depth)
    along = [side_depths(d) for d in depth]
    zero = jnp.zeros_like(between)

    def body(k, carry):
        level = k.astype(jnp.float32)
        flow = [flow_in[k], mate_flow[k]]
        beyond = [flow_far[k], mate_flow_far[k]]
        turn = [merid[k, pl.ds(where, sub, stride=2), :] for where in (outer, inner)]
        middle = face_pair(level, between, -sign * (flow[0] + flow[1]))
        edges = [
            face_pair(level, beside[c], (sign, -sign)[c] * (flow[c] + beyond[c])) for c in range(2)
        ]
        sides = [side_pairs(level, along[c], turn[c]) for c in range(2)]
        weight[k] = edges[0][1]
        totals, grams = list(carry[:VECTORS]), list(carry[VECTORS:])
        fresh = []
        for v in range(VECTORS):
            row = v * levels + k
            flux = [outflow(edges[c], near[c][row], far[c][row]) for c in range(2)]
            outside, inside = cross[row] - flux[0], mate[row] - flux[1]
            other = mate_far[row] + flux[1]
            crossing = outflow(middle, outside, inside)
            base[v, k] = (
                outside
                - outflow(edges[0], outside, flux[0])
                - crossing
                - divergence_y(sides[0], outside)
            )
            value = (
                inside - outflow(edges[1], inside, other) + crossing - divergence_y(sides[1], inside)
            )
            done[v, k] = value
            totals[v] = totals[v] + value
            fresh.append(value)
        return (*totals, *add_products(grams, *fresh))

    found = lax.fori_loop(0, levels, body, (zero,) * (VECTORS + 3), unroll=steps(levels, 10))
    for row, tile in enumerate(found):
        sums[row] = tile


def interleave_kernel(levels, sub, column, done, tracer):
    outer, inner, _ = orientation()

    def body(k, carry):
        for v in range(VECTORS):
            tracer[v, k, pl.ds(outer, sub, stride=2), :] = column[v, k]
            tracer[v, k, pl.ds(inner, sub, stride=2), :] = done[v, k]
        return carry

    lax.fori_loop(0, levels, body, 0, unroll=steps(levels, 10))


def add_products(grams, a, b):
    return [grams[0] + a * a, grams[1] + a * b, grams[2] + b * b]


def second_kernel(levels, cross_far, base, weight, inside, powers, mate_flow, column, message):
    outer, inner, _ = orientation()
    zero = jnp.zeros(powers.shape[-2:], jnp.float32)

    def body(k, carry):
        totals, fresh = [], []
        for v in range(VECTORS):
            value = base[v, k] - weight[k] * cross_far[v * levels + k]
            column[v, k] = value
            totals.append(carry[v] + value)
            fresh.append(value)
        return (*totals, *add_products(carry[VECTORS:], *fresh))

    carry = lax.fori_loop(0, levels, body, (zero,) * (VECTORS + 3), unroll=steps(levels, 50))
    gain = STERIC_GAIN / levels
    rows = [a + inside[VECTORS + n] for n, a in enumerate(carry[VECTORS:])]
    residual = []
    for v in range(VECTORS):
        residual.append(
            [gain * total_of + powers[POWERS, v, c] for c, total_of in enumerate((carry[v], inside[v]))]
        )
        for c, where in enumerate((outer, inner)):
            message[v * 2 + where] = residual[v][c]

    def product(one, two):
        return one[0] * two[0] + one[1] * two[1]

    heights = [[powers[0, v, c] for c in range(2)] for v in range(VECTORS)]
    for n, (i, j) in enumerate(((0, 0), (0, 1), (1, 1))):
        rows[n] = rows[n] + product(heights[i], heights[j])
    for i in range(VECTORS):
        for j in range(VECTORS):
            for m in range(POWERS):
                rows.append(product([powers[m, i, c] for c in range(2)], residual[j]))
    message[GRAMS] = pack_rows(rows)
    for c in range(2):
        message[DEPTHS + c] = mate_flow[levels + DEPTHS + c]


def pack_rows(tiles):
    shape = tiles[0].shape
    sub, lane = (lax.broadcasted_iota(jnp.int32, shape, axis) for axis in (0, 1))
    half = shape[1] // 2
    packed = jnp.zeros(shape, jnp.float32)
    for n, tile in enumerate(tiles):
        row = jnp.sum(tile, axis=0, keepdims=True)
        row = row + pltpu.roll(row, half, 1)
        place = (sub == n % shape[0]) & ((lane < half) == (n < shape[0]))
        packed = jnp.where(place, row, packed)
    return packed


def unpack_rows(packed, count):
    lane = lax.broadcasted_iota(jnp.int32, packed.shape, 1)
    low = lane < packed.shape[1] // 2
    sums = [
        jnp.sum(jnp.where(side, packed, 0.0), axis=1, keepdims=True)
        for side in (low, jnp.logical_not(low))
    ]
    size = packed.shape[0]
    return [sums[n // size][n % size : n % size + 1] for n in range(count)]


def powers_of_heights(levels, mate_flow, mate_flow_far, raw_far, beyond, powers):
    outer, inner, _ = orientation()
    line = [
        (mate_flow_far, levels, inner),
        (mate_flow_far, levels, outer),
        (mate_flow, levels, inner),
        (mate_flow, levels, outer),
        (raw_far, VECTORS * levels, inner),
        (raw_far, VECTORS * levels, outer),
    ]
    depth = [ref[base + DEPTHS + where] for ref, base, where in line[:4]] + beyond
    faces = [SURFACE_COUPLING * jnp.minimum(a, b) for a, b in zip(depth, depth[1:])]
    sides = [side_depths(SURFACE_COUPLING * d) for d in depth[1:5]]
    for v in range(VECTORS):
        field = [
            jnp.where(d > 0, ref[base + v * 2 + where], 0.0)
            for d, (ref, base, where) in zip(depth, line)
        ]

        def bend(field, first, last):
            found = []
            for j in range(first, last):
                west, centre, east = field[j - 1 : j + 2]
                north, south = sides[j - 1]
                found.append(
                    (faces[j] * (east - centre) - faces[j - 1] * (centre - west))
                    + (north * (next_row(centre) - centre) - south * (centre - prior_row(centre)))
                )
            return found

        lap = bend(field, 1, 5)
        image = [None] + [h - p for h, p in zip(field[1:5], lap)]
        again = [p - q for p, q in zip(image[2:4], bend(image, 2, 4))]
        for c, where in enumerate((3, 2)):
            powers[0, v, c] = field[where]
            powers[1, v, c] = image[where]
            powers[2, v, c] = again[where - 2]
            powers[POWERS, v, c] = lap[where - 1]


def total(tile):
    return jnp.sum(jnp.sum(tile, axis=0, keepdims=True), axis=1, keepdims=True)


def combine(one, factor, two):
    longest = max(len(one), len(two))
    one, two = (list(c) + [0.0] * (longest - len(c)) for c in (one, two))
    return [a + factor * b for a, b in zip(one, two)]


def third_kernel(levels, sub, count, *refs):
    masks_of = chip_masks(count)
    blocks = 1 + 2 * len(masks_of)
    (surface, tracer, scaled, surface_out, growth) = refs[blocks : blocks + 5]
    (pole, residual, answer, image, depth, face_x, face_y, face_z, packed) = refs[blocks + 5 :]
    width = 2 * count
    me = lax.axis_index("lon")
    core = lax.rem(me, 2)
    zero = jnp.zeros((sub, LANES), jnp.float32)
    none = (zero,) * VECTORS

    def place(first, block):
        packed[first // 2] = block[2 * RIM]
        for slot in range(2):
            for c in range(2):
                x = 2 * (first ^ slot) + c
                depth[x] = block[RIM * slot + DEPTHS + c]
                for v in range(VECTORS):
                    value = block[RIM * slot + v * 2 + c]
                    residual[v, x] = value
                    pole[v, x + 1] = value

    place(me, refs[0])
    for n, block in enumerate(refs[1:blocks]):
        flip, masks = n // len(masks_of), masks_of[n % len(masks_of)]
        mask = jnp.where((core ^ flip) == 0, *masks)

        def put(first=me ^ flip ^ (2 * mask), block=block):
            place(first, block)

        if all(masks):
            put()
        else:
            pl.when(mask > 0)(put)

    def over(body, init):
        return lax.fori_loop(0, count, body, init, unroll=steps(count, 16))

    def each(d):
        return [(v, c, 2 * d + c) for v in range(VECTORS) for c in range(2)]

    def prepare(d, carry):
        for x in (2 * d, 2 * d + 1):
            here, after = depth[x], depth[lax.rem(x + 1, width)]
            face_x[x + 1] = SURFACE_COUPLING * jnp.minimum(here, after)
            north, south = side_depths(here)
            face_y[x] = SURFACE_COUPLING * north
            face_z[x] = SURFACE_COUPLING * south
        return carry

    over(prepare, 0)
    face_x[0] = face_x[width]
    wrap(pole, width)

    def start(d, carry):
        sums = list(carry)
        for v, _, x in each(d):
            sums[v] = sums[v] + residual[v, x] * residual[v, x]
        return tuple(sums)

    norm = [total(t) for t in over(start, none)]
    taken, left, aim = ([[v for _ in range(VECTORS)] for v in ([], [1.0], [1.0])])

    def apply(d, carry):
        sums = list(carry)
        for v, _, x in each(d):
            centre = pole[v, x + 1]
            value = centre - spread(pole, face_x, face_y, face_z, v, x)
            image[v, x] = value
            sums[v] = sums[v] + centre * value
        return tuple(sums)

    for iteration in range(ITERS):
        energy = [total(t) for t in over(apply, none)]
        size = [n / e for n, e in zip(norm, energy)]
        taken = [combine(s, z, a) for s, z, a in zip(taken, size, aim)]
        if iteration + 1 < ITERS:

            def advance(d, carry, size=size, first=iteration == 0):
                sums = list(carry)
                for v, _, x in each(d):
                    gone = size[v] * pole[v, x + 1]
                    answer[v, x] = gone if first else answer[v, x] + gone
                    value = residual[v, x] - size[v] * image[v, x]
                    residual[v, x] = value
                    sums[v] = sums[v] + value * value
                return tuple(sums)

            fresh = [total(t) for t in over(advance, none)]
            ratio = [f / n for f, n in zip(fresh, norm)]
            left = [combine(l, -z, [0.0] + a) for l, z, a in zip(left, size, aim)]
            aim = [combine(l, q, a) for l, q, a in zip(left, ratio, aim)]

            def turn(d, carry, ratio=ratio):
                for v, _, x in each(d):
                    pole[v, x + 1] = residual[v, x] + ratio[v] * pole[v, x + 1]
                return carry

            over(turn, 0)
            wrap(pole, width)
            norm = fresh

    def finish(d, carry):
        grams = list(carry)
        for x in (2 * d, 2 * d + 1):
            a, b = (answer[v, x] + size[v] * pole[v, x + 1] for v in range(VECTORS))
            answer[0, x], answer[1, x] = a, b
            grams = [grams[0] + a * a, grams[1] + a * b, grams[2] + b * b]
        return (*grams, carry[3])

    *grams, _ = over(finish, (zero,) * 4)
    packed_sums = sum((packed[n] for n in range(1, count // 2)), packed[0])
    sums = unpack_rows(packed_sums, 3 + VECTORS * VECTORS * POWERS)

    def heights_with(i, j):
        first = 3 + (i * VECTORS + j) * POWERS
        return sum(c * t for c, t in zip(taken[j], sums[first : first + POWERS]))

    cells = (levels + 1) * width * sub * LANES
    one, mix, two = (
        (sums[n] + total(grams[n]) + (heights_with(i, j) + heights_with(j, i))) / cells
        for n, (i, j) in enumerate(((0, 0), (0, 1), (1, 1)))
    )
    scale_one = jnp.sqrt(one + EPSILON)
    cross = mix / scale_one
    rest = two - 2.0 * cross * cross + cross * cross * one / (one + EPSILON)
    scale_two = jnp.sqrt(rest + EPSILON)
    over_one, over_two = 1.0 / scale_one, 1.0 / scale_two

    def scale(k, carry):
        unit = tracer[0, k] * over_one
        scaled[0, k] = unit
        scaled[1, k] = (tracer[1, k] - cross * unit) * over_two
        return carry

    lax.fori_loop(0, levels, scale, 0, unroll=steps(levels, 50))
    for c in range(2):
        x = 2 * me + c
        first, second = (
            jnp.where(depth[x] > 0, surface[v, pl.ds(c, sub, stride=2), :], 0.0) + answer[v, x]
            for v in range(VECTORS)
        )
        unit = first * over_one
        surface_out[0, pl.ds(c, sub, stride=2), :] = unit
        surface_out[1, pl.ds(c, sub, stride=2), :] = (second - cross * unit) * over_two
    for i, value in enumerate((scale_one, cross, scale_two)):
        growth[i] = value[0, 0]


def tiled(array):
    *lead, columns, rows = array.shape
    split = array.reshape(*lead, columns, rows // LANES, LANES)
    return jnp.swapaxes(split, -3, -2).reshape(*lead, rows // LANES * columns, LANES)


def untiled(array, columns):
    *lead, high, lanes = array.shape
    split = array.reshape(*lead, high // columns, columns, lanes)
    return jnp.swapaxes(split, -3, -2).reshape(*lead, columns, high // columns * lanes)


def swap(array, mask):
    count = lax.axis_size("lon")
    return lax.ppermute(array, "lon", [(i, i ^ mask) for i in range(count)])


def chip_masks(count):
    lists, loads = ([], []), [0, 0]
    for mask in range(count // 2 - 1, 0, -1):
        core = int(loads[1] < loads[0])
        lists[core].append(mask)
        loads[core] += mask % 2 + mask // 2
    longest = max(map(len, lists))
    return list(zip(*(one + [0] * (longest - len(one)) for one in lists)))


def gather(block):
    count = lax.axis_size("lon")
    beside = swap(block, 1)
    pair = jnp.concatenate([block[:RIM], beside[:RIM], block[RIM:] + beside[RIM:]])
    fetched = []
    for masks in chip_masks(count):
        moves = [(i, i ^ (2 * masks[i % 2])) for i in range(count) if masks[i % 2]]
        fetched.append(lax.ppermute(pair, "lon", moves))
    return pair, *fetched, *(swap(one, 1) for one in fetched)


def on_device(tracer_pert, surface_pert, zonal_flow, merid_flow, bottom_level):
    vectors, levels, columns, rows = tracer_pert.shape
    count = lax.axis_size("lon")
    sub = rows // LANES
    assert vectors == VECTORS and columns == 2 and rows % LANES == 0
    assert count >= 8 and count & (count - 1) == 0
    width = 2 * count
    f32 = jnp.float32
    vmem = pl.BlockSpec(memory_space=pltpu.VMEM)
    hbm = pl.BlockSpec(memory_space=pltpu.HBM)
    params = pltpu.CompilerParams(vmem_limit_bytes=24 * 2**20)

    def shaped(*shape):
        return jax.ShapeDtypeStruct((*shape, sub, LANES), f32)

    def held(*shape):
        return pltpu.VMEM((*shape, sub, LANES), f32)

    both = pltpu.VMEM((vectors, levels, sub * 2, LANES), f32)
    tracer_pert, zonal_flow, merid_flow = map(tiled, (tracer_pert, zonal_flow, merid_flow))
    outward = [(i, (i + 1) % count if i % 2 else (i - 1) % count) for i in range(count)]
    part = levels // 2
    surface, bottom = tiled(surface_pert), tiled(bottom_level)

    pinned = [
        pltpu.with_memory_space_constraint(array, pltpu.HBM)
        for array in (tracer_pert, zonal_flow, surface, bottom)
    ]
    edge, flow_edge = pl.pallas_call(
        functools.partial(edge_kernel, levels, sub),
        out_shape=(shaped(VECTORS * levels + DEPTHS), shaped(part + 1)),
        in_specs=[hbm] * 4,
        out_specs=(vmem, vmem),
        scratch_shapes=[
            both,
            pltpu.VMEM((part, sub * 2, LANES), f32),
            pltpu.VMEM((vectors, sub * 2, LANES), f32),
            pltpu.VMEM((sub * 2, LANES), jnp.int32),
            pltpu.SemaphoreType.DMA((VECTORS + 3,)),
        ],
        compiler_params=pltpu.CompilerParams(vmem_limit_bytes=16 * 2**20),
        name="edge_columns",
    )(*pinned)
    flow_half = lax.ppermute(flow_edge, "lon", outward)
    edge_far = lax.ppermute(edge, "lon", outward)
    flow_other = lax.ppermute(flow_half, "grp", [(0, 1), (1, 0)])
    cross, mate, raw, mate_raw, flow_in, mate_flow = pl.pallas_call(
        functools.partial(first_kernel, levels, sub),
        out_shape=(
            shaped(VECTORS * levels),
            shaped(VECTORS * levels),
            shaped(VECTORS * levels),
            shaped(VECTORS * levels),
            shaped(levels),
            shaped(levels + RIM),
        ),
        in_specs=[pl.BlockSpec(memory_space=pl.ANY)] + [vmem] * 5,
        out_specs=(vmem,) * 6,
        compiler_params=params,
        name="partial_step",
    )(edge, tracer_pert, zonal_flow, merid_flow, surface, bottom)
    cross_far = lax.ppermute(cross, "lon", outward)
    mate_far, mate_raw_far, mate_flow_far = (swap(x, 1) for x in (mate, mate_raw, mate_flow))
    done, *rest = pl.pallas_call(
        functools.partial(halo_kernel, levels, sub),
        out_shape=(
            shaped(vectors, levels),
            shaped(vectors, levels),
            shaped(levels),
            shaped(VECTORS + 3),
            shaped(POWERS + 1, vectors, 2),
        ),
        in_specs=[vmem] * 13,
        out_specs=(vmem,) * 5,
        scratch_shapes=[held(levels)],
        compiler_params=params,
        name="both_steps",
    )(
        raw, cross, mate, mate_raw, flow_in, mate_flow,
        edge_far, mate_far, mate_raw_far, mate_flow_far, flow_half, flow_other, merid_flow,
    )
    column, message = pl.pallas_call(
        functools.partial(second_kernel, levels),
        out_shape=(shaped(vectors, levels), shaped(BLOCKS)),
        in_specs=[vmem] * 6,
        out_specs=(vmem, vmem),
        compiler_params=params,
        name="outer_column",
    )(cross_far, *rest, mate_flow)
    tracer = pl.pallas_call(
        functools.partial(interleave_kernel, levels, sub),
        out_shape=jax.ShapeDtypeStruct((vectors, levels, sub * 2, LANES), f32),
        in_specs=[vmem] * 2,
        out_specs=vmem,
        compiler_params=params,
        name="interleave",
    )(column, done)
    blocks = gather(message)
    tracer_vec, surface_vec, growth = pl.pallas_call(
        functools.partial(third_kernel, levels, sub, count),
        out_shape=(
            jax.ShapeDtypeStruct((vectors, levels, sub * 2, LANES), f32),
            jax.ShapeDtypeStruct((vectors, sub * 2, LANES), f32),
            jax.ShapeDtypeStruct((3,), f32),
        ),
        in_specs=[vmem] * (len(blocks) + 2),
        out_specs=(vmem, vmem, pl.BlockSpec(memory_space=pltpu.SMEM)),
        scratch_shapes=[
            held(vectors, width + 2),
            *[held(vectors, width)] * 3,
            held(width),
            held(width + 1),
            held(width),
            held(width),
            held(count // 2),
        ],
        compiler_params=pltpu.CompilerParams(vmem_limit_bytes=32 * 2**20),
        name="surface_and_scale",
    )(*blocks, surface, tracer)
    return (untiled(tracer_vec, 2), untiled(surface_vec, 2), growth)


def solution(mesh):
    placed = (
        P("grp", None, "lon", None),
        P("grp", "lon", None),
        P(None, "lon", None),
        P(None, "lon", None),
        P("lon", None),
    )
    return jax.shard_map(
        on_device,
        mesh=mesh,
        in_specs=placed,
        out_specs=(P("grp", None, "lon", None), P("grp", "lon", None), P("grp")),
        check_vma=False,
    )
```
